256 devices in a mesh: gx: 4 (over y), gy: 8 (over z), gz: 8 (over x, core).
Axes of the slice: x: 4, y: 4, z: 8, core: 2. Of those that a mesh axis runs over, the one named last changes fastest.
Arguments:
- source: float32 [32, 512, 1024], P('gx', 'gy', 'gz'), may hold values from -8 to 8
- coefficient: float32 [32, 512, 1024], P('gx', 'gy', 'gz'), may hold values from 0.05 to 4
Outputs:
- posterior_mean: float32 [32, 512, 1024], P('gx', 'gy', 'gz')
- residual: float32 [32, 512, 1024], P('gx', 'gy', 'gz')
The draws below stay inside these ranges and needn't reach their ends.
All inputs are finite; a program needn't handle non-finite values.
Results may differ from the reference program's by a relative error of at most 0.000024.
Values sent between devices are 32-bit elements; how exact they have to be, the bound alone decides.
No kernel may reach another device: no remote copies, remote signals or barrier semaphores. Data moves between devices by JAX's collectives and lax.ppermute only.
A program may use at most 128 MiB of HBM per device.

```python
import math
import jax
import jax.numpy as jnp

SWEEPS = 3
COARSE_SWEEPS = 6
NX = 32
NY = 512
NZ = 1024


def steps_of(rng, dims, pieces, smallest, top_value):
    def one(axis_at, blocks):
        draws = jax.random.uniform(jax.random.fold_in(jax.random.fold_in(rng, 6), axis_at), (blocks,), jnp.float32, smallest / len(pieces), top_value / len(pieces))
        return jnp.repeat(jnp.exp(draws), dims[axis_at] // blocks).reshape((-1,) + (1,) * (len(dims) - axis_at - 1))

    gain = one(*pieces[0])
    for cut in pieces[1:]:
        gain = gain * one(*cut)
    return gain


def normal_values(own_key, shape, scale, bound, pieces=(), held_as=jnp.bfloat16):
    loudness = steps_of(own_key, shape, pieces, -0.22, 0.18) if pieces else 1.0
    array = jax.random.normal(own_key, shape, jnp.float32) * scale * loudness
    return jnp.minimum(jnp.maximum(array, -bound), bound).astype(held_as)


def setup_inputs(seed: int = 0) -> dict:
    arg_keys = jax.random.split(jax.random.key(seed), 3)
    return {
        "source": normal_values(arg_keys[0], (NX, NY, NZ), 1.0, 8.0, ((0, 4), (1, 8), (2, 8)), jnp.float32),
        "coefficient": jnp.clip(jnp.exp(math.log(4.0) - 4.3820266 * jax.random.uniform(arg_keys[1], (NX, NY, NZ), jnp.float32) ** steps_of(arg_keys[1], (NX, NY, NZ), ((0, 4), (1, 8), (2, 8)), -0.2, 0.2)), 0.05, 4.0),
    }


THETA = 1.25
DELTA = 0.75


def operate(field, diag, scale):
    padded = jnp.pad(field, 1)
    beside = padded[2:, 1:-1, 1:-1] + padded[:-2, 1:-1, 1:-1]
    beside = beside + padded[1:-1, 2:, 1:-1] + padded[1:-1, :-2, 1:-1]
    beside = beside + padded[1:-1, 1:-1, 2:] + padded[1:-1, 1:-1, :-2]
    return (diag + 6.0 * scale) * field - scale * beside


def smooth(sol, res, diag, scale, sweeps):
    sigma = THETA / DELTA
    rho = 1.0 / sigma
    inverse = 1.0 / (diag + 6.0 * scale)
    step_dir = res * inverse / THETA
    for sweep in range(sweeps):
        sol = sol + step_dir
        res = res - operate(step_dir, diag, scale)
        rho_new = 1.0 / (2.0 * sigma - rho)
        step_dir = (rho_new * rho) * step_dir + (2.0 * rho_new / DELTA) * res * inverse
        rho = rho_new
    return sol, res


def coarsen(field):
    a, b, c = field.shape
    return field.reshape(a // 2, 2, b // 2, 2, c // 2, 2).mean(axis=(1, 3, 5))


def refine(field):
    return jnp.repeat(jnp.repeat(jnp.repeat(field, 2, 0), 2, 1), 2, 2)


def reference(source, coefficient):
    coef_mid = coarsen(coefficient)
    coef_low = coarsen(coef_mid)
    sol0, res0 = smooth(jnp.zeros_like(source), source, coefficient, 1.0, SWEEPS)
    res1 = coarsen(res0)
    sol1, res1 = smooth(jnp.zeros_like(res1), res1, coef_mid, 0.25, SWEEPS)
    res2 = coarsen(res1)
    sol2, unused = smooth(jnp.zeros_like(res2), res2, coef_low, 0.0625, COARSE_SWEEPS)
    lifted = refine(sol2)
    sol1 = sol1 + lifted
    res1 = res1 - operate(lifted, coef_mid, 0.25)
    sol1, res1 = smooth(sol1, res1, coef_mid, 0.25, SWEEPS)
    lifted = refine(sol1)
    sol0 = sol0 + lifted
    res0 = res0 - operate(lifted, coefficient, 1.0)
    sol0, res0 = smooth(sol0, res0, coefficient, 1.0, SWEEPS)
    return sol0, res0
```

```python
import jax
import jax.numpy as jnp
from jax import lax
from jax.experimental import pallas as pl
from jax.experimental.pallas import tpu as pltpu
from jax.sharding import PartitionSpec as P

SWEEPS = 3
COARSE_SWEEPS = 6
THETA = 1.25
DELTA = 0.75
F32 = jnp.float32
EXACT = lax.Precision.HIGHEST

XH = 3
NX0, NY0, NZ0 = 8, 64, 128
NXE = NX0 + 2 * XH
W = 9
R0 = 88
Q0 = 72
R1 = 40
Q1 = 48
R2 = 32
VM = 60 * 1024 * 1024


def coefficients(count):
    sigma = THETA / DELTA
    rho = 1.0 / sigma
    pairs = []
    for _ in range(count):
        rho_new = 1.0 / (2.0 * sigma - rho)
        pairs.append((rho_new * rho, 2.0 * rho_new / DELTA))
        rho = rho_new
    return pairs


def turn(value, shift, axis):
    return pltpu.roll(value, shift % value.shape[axis], axis)


def beside(value):
    return (turn(value, 1, 0) + turn(value, -1, 0)) + (turn(value, 1, 1) + turn(value, -1, 1))


def rows_of(shape):
    return lax.broadcasted_iota(jnp.int32, shape, 0)


def lanes_of(shape):
    return lax.broadcasted_iota(jnp.int32, shape, 1)


def inside_yz(shape, own_rows, split_row, own_lanes, split_lane):
    gy, gz = lax.axis_index("gy"), lax.axis_index("gz")
    last_y, last_z = lax.axis_size("gy") - 1, lax.axis_size("gz") - 1
    row, lane = rows_of(shape), lanes_of(shape)
    up_y, down_y = (gy < last_y).astype(jnp.int32), (gy > 0).astype(jnp.int32)
    up_z, down_z = (gz < last_z).astype(jnp.int32), (gz > 0).astype(jnp.int32)
    in_y = jnp.where(row < own_rows, 1, jnp.where(row < split_row, up_y, down_y))
    in_z = jnp.where(lane < own_lanes, 1, jnp.where(lane < split_lane, up_z, down_z))
    return (in_y * in_z) > 0


def dot(a, b):
    return jnp.dot(a, b, precision=EXACT, preferred_element_type=F32)


def call(body, outs, scratch, *args):
    vmem = pl.BlockSpec(memory_space=pltpu.VMEM)
    return pl.pallas_call(
        body,
        out_shape=[jax.ShapeDtypeStruct(s, F32) for s in outs],
        in_specs=[vmem] * len(args),
        out_specs=[vmem] * len(outs),
        scratch_shapes=[pltpu.VMEM(s, F32) for s in scratch],
        compiler_params=pltpu.CompilerParams(vmem_limit_bytes=VM),
    )(*args)


def ring(value, axis, shift):
    size = lax.axis_size(axis)
    return lax.ppermute(value, axis, [(i, (i + shift) % size) for i in range(size)])


def plane_of(own, low, high, which, x):
    if x < XH:
        return low.at[which * XH + x]
    if x < XH + NX0:
        return own[which].at[x - XH]
    return high.at[which * XH + x - XH - NX0]


def pack_y(s, c, low, high, up, down):
    for a in range(2):
        for x in range(NXE):
            src = plane_of((s, c), low, high, a, x)
            at = a * NXE + x
            up[at * 8 : at * 8 + 8, :] = src[56:64, :]
            down[at * 8 : at * 8 + 8, :] = src[0:8, :]
            up[224 + at : 225 + at, :] = src[55:56, :]
            down[224 + at : 225 + at, :] = src[8:9, :]
    up[252:256, :] = jnp.zeros((4, 128), F32)
    down[252:256, :] = jnp.zeros((4, 128), F32)


def pack_z(s, c, low, high, below, above, main, up, down):
    lane = lanes_of((R0, 128))
    for a in range(2):
        ups = jnp.zeros((R0, 128), F32)
        downs = jnp.zeros((R0, 128), F32)
        for x in range(NXE):
            src = plane_of((s, c), low, high, a, x)
            at = a * NXE + x
            main[a, x, 0:64, :] = src[...]
            main[a, x, 64:72, :] = above[at * 8 : at * 8 + 8, :]
            main[a, x, 72:80, :] = jnp.zeros((8, 128), F32)
            main[a, x, 72:73, :] = above[224 + at : 225 + at, :]
            main[a, x, 79:80, :] = below[224 + at : 225 + at, :]
            main[a, x, 80:88, :] = below[at * 8 : at * 8 + 8, :]
            plane = main[a, x]
            here = (lane >= W * x) & (lane < W * x + W)
            ups = jnp.where(here, turn(plane, W * x - (128 - W), 1), ups)
            downs = jnp.where(here, turn(plane, W * x, 1), downs)
        up[a] = ups
        down[a] = downs


def fine_sweep(src, dst, res, diag, inverse, first, stop, pair, also):
    def body(x, carry):
        d = src[x]
        near = beside(d) + (src[x - 1] + src[x + 1])
        r = res[x] - (diag[x] * d - near)
        res[x] = r
        also(x, d)
        if pair is not None:
            dst[x] = pair[0] * d + (pair[1] * inverse[x]) * r
        return carry

    lax.fori_loop(first, stop, body, 0)


def to_q0(ref, x):
    tail = jnp.where(rows_of((8, 256)) < 4, ref[x, 64:72, :], ref[x, 80:88, :])
    return ref[x, 0:64, :], tail


def fine_before(
    main, below, above, sol, res_q, diag_q, inv_q, msg2, msg_up, msg_down, res, diag, inv, da, db
):
    lane = lanes_of((R0, 128))
    for a in range(2):
        left, right = below[a], above[a]
        for x in range(NXE):
            side = jnp.where(lane < W, turn(right, -W * x, 1), 0.0)
            side = jnp.where(lane >= 128 - W, turn(left, 128 - W - W * x, 1), side)
            ref = (res, diag)[a]
            ref[x, :, 0:128] = main[a, x]
            ref[x, :, 128:256] = side
    row40, row88 = rows_of((R1, R0)), lanes_of((R1, R0))
    fold_y = jnp.where(row88 // 2 == jnp.where(row40 < 36, row40, row40 + 4), 0.125, 0.0).astype(F32)
    fold_z = jnp.where(rows_of((256, 128)) // 2 == lanes_of((256, 128)), 1.0, 0.0).astype(F32)

    def fold(ref, i):
        both = ref[XH + 2 * i] + ref[XH + 2 * i + 1]
        return dot(fold_y, dot(both, fold_z))

    coef1 = [fold(diag, i) for i in range(4)]

    gx = lax.axis_index("gx")
    in_yz = inside_yz((R0, 256), 64, 76, 128, 192)
    low_x, high_x = gx > 0, gx < lax.axis_size("gx") - 1

    def start(x, carry):
        g = diag[x] + 6.0
        diag[x] = g
        here = ((x >= XH) | low_x) & ((x < XH + NX0) | high_x)
        inverse = jnp.where(in_yz & here, 1.0 / g, 0.0)
        inv[x] = inverse
        da[x] = res[x] * inverse * (1.0 / THETA)
        top, tail = to_q0(diag, x)
        diag_q[x, 0:64, :] = top
        diag_q[x, 64:72, :] = tail
        top, tail = to_q0(inv, x)
        inv_q[x, 0:64, :] = top
        inv_q[x, 64:72, :] = tail
        return carry

    lax.fori_loop(0, NXE, start, 0)

    def add(first):
        def put(x, d):
            own = d[0:64, 0:128]
            at = jnp.clip(x - XH, 0, NX0 - 1)
            if first:
                sol[at] = own
            else:
                inside = ((x >= XH) & (x < XH + NX0)).astype(F32)
                sol[at] += inside * own

        return put

    pairs = coefficients(SWEEPS)
    buffers = (da, db)
    for k in range(SWEEPS):
        src, dst = buffers[k % 2], buffers[(k + 1) % 2]
        last = k == SWEEPS - 1

        def nothing(x, d):
            return None

        fine_sweep(src, dst, res, diag, inv, k + 1, NXE - 1 - k, None if last else pairs[k], nothing)

        def gather(x, carry):
            own = src[XH + x, 0:64, 0:128]
            sol[x] = own if k == 0 else sol[x] + own
            return carry

        lax.fori_loop(0, NX0, gather, 0)

    def keep(x, carry):
        top, tail = to_q0(res, XH + x)
        res_q[x, 0:64, :] = top
        res_q[x, 64:72, :] = tail
        return carry

    lax.fori_loop(0, NX0, keep, 0)

    lane40 = lanes_of((R1, 128))
    halo = jnp.zeros((R1, 128), F32)
    for i in range(4):
        r1, c1 = fold(res, i), coef1[i]
        both = jnp.where(lane40 < 64, r1, turn(c1, 64, 1))
        for msg in (msg2, msg_up, msg_down):
            msg[i * R1 : i * R1 + R1, :] = both
        for a, v in ((0, r1), (1, c1)):
            base = (a * 4 + i) * 8
            halo = jnp.where((lane40 >= base) & (lane40 < base + 4), turn(v, base - 64, 1), halo)
            halo = jnp.where((lane40 >= base + 4) & (lane40 < base + 8), turn(v, base + 4 - 124, 1), halo)
    msg2[160:200, :] = halo
    lane72 = lanes_of((Q0, 128))
    for msg, first in ((msg_up, NX0 - XH), (msg_down, 0)):
        side = jnp.zeros((Q0, 128), F32)
        for i in range(XH):
            msg[160 + i * Q0 : 160 + i * Q0 + Q0, :] = res_q[first + i, :, 0:128]
            v = res_q[first + i, :, 128:256]
            base = 64 + 6 * i
            side = jnp.where((lane72 >= base) & (lane72 < base + 3), turn(v, base, 1), side)
            side = jnp.where((lane72 >= base + 3) & (lane72 < base + 6), turn(v, base + 3 - 125, 1), side)
        at = 160 + XH * Q0
        msg[at : at + R1, :] = jnp.where(lane40 < 64, halo, side[0:R1])
        msg[at + R1 : at + Q0, :] = side[R1:Q0]


def line_sweep(src, dst, res, diag, inverse, planes, scale, pair):
    def body(x, carry):
        d = src[x + 1]
        near = beside(d) + (src[x] + src[x + 2])
        r = res[x] - (diag[x] * d - scale * near)
        res[x] = r
        if pair is not None:
            dst[x + 1] = pair[0] * d + (pair[1] * inverse[x]) * r
        return carry

    lax.fori_loop(0, planes, body, 0, unroll=2)


def middle_before(own, low, high, far, res, sol, coef, low_res, low_coef, up, down, diag, inv, da, db):
    gx = lax.axis_index("gx")
    size = lax.axis_size("gx")
    lane40 = lanes_of((R1, 128))
    for msg, shift, side_at in ((own, 0, 160), (low, 3, 160 + XH * Q0), (high, 1, 160 + XH * Q0), (far, 2, 160)):
        place = lax.rem(gx + shift, size) * 4
        side = msg[side_at : side_at + R1, :]
        for i in range(4):
            both = msg[i * R1 : i * R1 + R1, :]
            for a, ref in ((0, res), (1, coef)):
                base = (a * 4 + i) * 8
                v = both if a == 0 else turn(both, 64, 1)
                v = jnp.where(lane40 < 64, v, turn(side, 64 - base, 1))
                v = jnp.where(lane40 < 68, v, 0.0)
                v = jnp.where(lane40 < 124, v, turn(side, 124 - base - 4, 1))
                ref[place + i] = v
    in_yz = inside_yz((R1, 128), 32, 36, 64, 96)
    empty = jnp.zeros((R1, 128), F32)
    for buffer in (da, db):
        buffer[0] = empty
        buffer[17] = empty

    def start(x, carry):
        g = coef[x] + 1.5
        diag[x] = g
        inverse = jnp.where(in_yz, 1.0 / g, 0.0)
        inv[x] = inverse
        d = res[x] * inverse * (1.0 / THETA)
        da[x + 1] = d
        sol[x] = d
        return carry

    lax.fori_loop(0, 16, start, 0)
    pairs = coefficients(SWEEPS)
    buffers = (da, db)
    for k in range(SWEEPS):
        src, dst = buffers[k % 2], buffers[(k + 1) % 2]
        line_sweep(src, dst, res, diag, inv, 16, 0.25, pairs[k] if k < SWEEPS - 1 else None)
        if k < SWEEPS - 1:

            def gather(x, carry):
                sol[x] += dst[x + 1]
                return carry

            lax.fori_loop(0, 16, gather, 0, unroll=2)
    fold_y = jnp.where(lanes_of((16, R1)) // 2 == rows_of((16, R1)), 0.125, 0.0).astype(F32)
    fold_z = jnp.where(
        (rows_of((128, 128)) // 2 == lanes_of((128, 128))) & (lanes_of((128, 128)) < 32), 1.0, 0.0
    ).astype(F32)
    lane8 = lanes_of((8, 128))
    for i in range(8):
        r2 = dot(fold_y, dot(res[2 * i] + res[2 * i + 1], fold_z))
        c2 = dot(fold_y, dot(coef[2 * i] + coef[2 * i + 1], fold_z))
        low_res[i] = r2
        low_coef[i] = c2
        both = r2 + turn(c2, 32, 1)
        up[i * 8 : i * 8 + 8, :] = both[8:16]
        down[i * 8 : i * 8 + 8, :] = both[0:8]
    for x in range(16):
        at = 64 + x * 8
        up[at : at + 8, :] = jnp.where(lane8 < 64, res[x, 24:32, :], turn(sol[x, 24:32, :], 64, 1))
        down[at : at + 8, :] = jnp.where(lane8 < 64, res[x, 0:8, :], turn(sol[x, 0:8, :], 64, 1))


def pack_low_z(low_res, low_coef, res, sol, below, above, res2, coef2, res1, sol1, up, down):
    lane2 = lanes_of((R2, 128))
    lane1 = lanes_of((Q1, 128))
    lane8 = lanes_of((8, 128))
    ups = jnp.zeros((R2, 128), F32)
    downs = jnp.zeros((R2, 128), F32)
    for i in range(8):
        res2[i, 0:16, :] = low_res[i]
        coef2[i, 0:16, :] = low_coef[i]
        for msg, at in ((above, 16), (below, 24)):
            both = msg[i * 8 : i * 8 + 8, :]
            res2[i, at : at + 8, :] = jnp.where(lane8 < 32, both, 0.0)
            coef2[i, at : at + 8, :] = jnp.where(lane8 < 32, turn(both, -32, 1), 0.0)
        for a, ref in ((0, res2), (1, coef2)):
            v = ref[i]
            base = a * 64 + i * 8
            here = (lane2 >= base) & (lane2 < base + 8)
            ups = jnp.where(here, turn(v, base - 24, 1), ups)
            downs = jnp.where(here, turn(v, base, 1), downs)
    up[0:R2, :] = ups
    down[0:R2, :] = downs
    ups = jnp.zeros((Q1, 128), F32)
    downs = jnp.zeros((Q1, 128), F32)
    for x in range(16):
        res1[x, 0:32, :] = jnp.where(lanes_of((32, 128)) < 64, res[x, 0:32, :], 0.0)
        sol1[x, 0:32, :] = jnp.where(lanes_of((32, 128)) < 64, sol[x, 0:32, :], 0.0)
        for msg, at in ((above, 32), (below, 40)):
            both = msg[64 + x * 8 : 72 + x * 8, :]
            res1[x, at : at + 8, :] = jnp.where(lane8 < 64, both, 0.0)
            sol1[x, at : at + 8, :] = jnp.where(lane8 < 64, turn(both, 64, 1), 0.0)
        base = 4 * x
        here = (lane1 >= base) & (lane1 < base + 4)
        ups = jnp.where(here, turn(res1[x], base - 60, 1), ups)
        downs = jnp.where(here, turn(res1[x], base, 1), downs)
        base = 64 + 2 * x
        here = (lane1 >= base) & (lane1 < base + 2)
        ups = jnp.where(here, turn(sol1[x], base - 62, 1), ups)
        downs = jnp.where(here, turn(sol1[x], base, 1), downs)
    up[R2 : R2 + Q1, :] = ups
    down[R2 : R2 + Q1, :] = downs


def finish(
    res2_in, coef2_in, res1_in, sol1_in, coef1, left, right, sol0, res_q, diag_q, inv_q, low, high,
    out_sol, out_res,
    res2, diag2, inv2, sol2, da2, db2, res1, diag1, inv1, sol1, da1, db1, p0, res0, da0, db0,
):
    gx = lax.axis_index("gx")
    lane2 = lanes_of((R2, 128))
    in_yz = inside_yz((R2, 128), 16, 24, 32, 64)
    empty = jnp.zeros((R2, 128), F32)
    for buffer in (da2, db2):
        buffer[0] = empty
        buffer[9] = empty
    from_left, from_right = left[0:R2, :], right[0:R2, :]
    for i in range(8):
        parts = []
        for a, ref in ((0, res2_in), (1, coef2_in)):
            base = a * 64 + i * 8
            v = jnp.where(lane2 < 32, ref[i], turn(from_right, 32 - base, 1))
            v = jnp.where(lane2 < 40, v, 0.0)
            parts.append(jnp.where(lane2 < 120, v, turn(from_left, 120 - base, 1)))
        g = parts[1] + 0.375
        inverse = jnp.where(in_yz, 1.0 / g, 0.0)
        res2[i] = parts[0]
        diag2[i] = g
        inv2[i] = inverse
        d = parts[0] * inverse * (1.0 / THETA)
        da2[i + 1] = d
        sol2[i] = d
    pairs = coefficients(COARSE_SWEEPS)
    buffers = (da2, db2)
    for k in range(COARSE_SWEEPS - 1):
        src, dst = buffers[k % 2], buffers[(k + 1) % 2]
        line_sweep(src, dst, res2, diag2, inv2, 8, 0.0625, pairs[k])

        def gather(x, carry):
            sol2[x] += dst[x + 1]
            return carry

        lax.fori_loop(0, 8, gather, 0, unroll=2)

    lane1 = lanes_of((Q1, 128))
    in_yz1 = inside_yz((Q1, 128), 32, 40, 64, 96)
    empty = jnp.zeros((Q1, 128), F32)
    for buffer in (da1, db1):
        buffer[0] = empty
        buffer[17] = empty
    for x in (0, 1, 18, 19):
        sol1[x] = empty
    from_left, from_right = left[R2 : R2 + Q1, :], right[R2 : R2 + Q1, :]
    row, col = rows_of((Q1, R2)), lanes_of((Q1, R2))
    lift_y = jnp.where(col == row // 2 + jnp.where(row >= 40, 8, 0), 1.0, 0.0).astype(F32)
    row, col = rows_of((128, 128)), lanes_of((128, 128))
    lift_z = jnp.where(row == col // 2 + jnp.where(col >= 96, 64, 0), 1.0, 0.0).astype(F32)
    for i in range(8):
        lifted = dot(lift_y, dot(sol2[i], lift_z))
        for x in (2 * i, 2 * i + 1):
            db1[x + 1] = lifted
            base = 4 * x
            v = jnp.where(lane1 < 64, res1_in[x], turn(from_right, 64 - base, 1))
            v = jnp.where(lane1 < 68, v, 0.0)
            res1[x] = jnp.where(lane1 < 124, v, turn(from_left, 124 - base, 1))
            base = 64 + 2 * x
            v = jnp.where(lane1 < 64, sol1_in[x], turn(from_right, 64 - base, 1))
            v = jnp.where(lane1 < 66, v, 0.0)
            v = jnp.where(lane1 < 126, v, turn(from_left, 126 - base, 1))
            sol1[x + 2] = jnp.where(in_yz1, v, 0.0) + lifted

    def correct1(x, carry):
        g = jnp.concatenate([coef1[x], coef1[x, 32:40, :]], 0) + 1.5
        inverse = jnp.where(in_yz1, 1.0 / g, 0.0)
        diag1[x] = g
        inv1[x] = inverse
        p = db1[x + 1]
        near = beside(p) + (db1[x] + db1[x + 2])
        r = res1[x] - (g * p - 0.25 * near)
        res1[x] = r
        d = r * inverse * (1.0 / THETA)
        da1[x + 1] = d
        sol1[x + 2] += d
        return carry

    lax.fori_loop(0, 16, correct1, 0)
    pairs = coefficients(SWEEPS)
    buffers = (da1, db1)
    for k in range(SWEEPS - 1):
        src, dst = buffers[k % 2], buffers[(k + 1) % 2]
        line_sweep(src, dst, res1, diag1, inv1, 16, 0.25, pairs[k])

        def gather1(x, carry):
            sol1[x + 2] += dst[x + 1]
            return carry

        lax.fori_loop(0, 16, gather1, 0, unroll=2)

    row, col = rows_of((Q0, Q1)), lanes_of((Q0, Q1))
    lift_y = jnp.where(col == row // 2 + jnp.where(row >= 68, 12, 0), 1.0, 0.0).astype(F32)
    lift_z = jnp.where(rows_of((128, 256)) == lanes_of((128, 256)) // 2, 1.0, 0.0).astype(F32)
    for i in range(8):
        lifted = dot(lift_y, dot(sol1[gx * 4 + i], lift_z))
        p0[2 * i] = lifted
        p0[2 * i + 1] = lifted
    lane72 = lanes_of((Q0, 128))
    at = 160 + XH * Q0
    for msg, first in ((low, 0), (high, XH + NX0)):
        side = msg[at : at + Q0, :]
        for i in range(XH):
            base = 64 + 6 * i
            v = jnp.where(lane72 < 3, turn(side, -base, 1), 0.0)
            v = jnp.where(lane72 < 125, v, turn(side, 125 - base - 3, 1))
            res0[first + i, :, 0:128] = msg[160 + i * Q0 : 160 + i * Q0 + Q0, :]
            res0[first + i, :, 128:256] = v

    def fetch(x, carry):
        res0[x + XH] = res_q[x]
        return carry

    lax.fori_loop(0, NX0, fetch, 0)

    def correct0(x, carry):
        p = p0[x + 1]
        near = beside(p) + (p0[x] + p0[x + 2])
        r = res0[x] - (diag_q[x] * p - near)
        res0[x] = r
        da0[x] = r * inv_q[x] * (1.0 / THETA)
        return carry

    lax.fori_loop(0, NXE, correct0, 0)

    def begin(x, carry):
        out_sol[x] = sol0[x] + p0[x + XH + 1, 0:64, 0:128]
        return carry

    lax.fori_loop(0, NX0, begin, 0)
    buffers = (da0, db0)
    for k in range(SWEEPS):
        src, dst = buffers[k % 2], buffers[(k + 1) % 2]

        def gather0(x, carry):
            out_sol[x] += src[x + XH, 0:64, 0:128]
            return carry

        lax.fori_loop(0, NX0, gather0, 0)
        fine_sweep(
            src, dst, res0, diag_q, inv_q, k + 1, NXE - 1 - k, pairs[k] if k < SWEEPS - 1 else None,
            lambda x, d: None,
        )

    def put(x, carry):
        out_res[x] = res0[x + XH, 0:64, 0:128]
        return carry

    lax.fori_loop(0, NX0, put, 0)


def per_device(s, c):
    up = jnp.concatenate([s[NX0 - XH :], c[NX0 - XH :]], 0)
    down = jnp.concatenate([s[:XH], c[:XH]], 0)
    low, high = ring(up, "gx", 1), ring(down, "gx", -1)
    up, down = call(pack_y, [(256, 128)] * 2, [], s, c, low, high)
    below, above = ring(up, "gy", 1), ring(down, "gy", -1)
    main, up, down = call(
        pack_z, [(2, NXE, R0, 128), (2, R0, 128), (2, R0, 128)], [], s, c, low, high, below, above
    )
    below, above = ring(up, "gz", 1), ring(down, "gz", -1)
    big = (NXE, R0, 256)
    sol0, res_q, diag_q, inv_q, msg2, msg_up, msg_down = call(
        fine_before,
        [(NX0, 64, 128), (NX0, Q0, 256), (NXE, Q0, 256), (NXE, Q0, 256), (200, 128), (448, 128), (448, 128)],
        [big] * 5,
        main, below, above,
    )
    low, high, far = ring(msg_up, "gx", 1), ring(msg_down, "gx", -1), ring(msg2, "gx", 2)
    mid = (16, R1, 128)
    res1, sol1, coef1, res2, coef2, up, down = call(
        middle_before,
        [mid, mid, mid, (8, 16, 128), (8, 16, 128), (192, 128), (192, 128)],
        [mid, mid, (18, R1, 128), (18, R1, 128)],
        msg2, low, high, far,
    )
    below, above = ring(up, "gy", 1), ring(down, "gy", -1)
    bot, mid = (8, R2, 128), (16, Q1, 128)
    res2, coef2, res1, sol1, up, down = call(
        pack_low_z,
        [bot, bot, mid, mid, (R2 + Q1, 128), (R2 + Q1, 128)],
        [],
        res2, coef2, res1, sol1, below, above,
    )
    left, right = ring(up, "gz", 1), ring(down, "gz", -1)
    big = (NXE, Q0, 256)
    own = (NX0, NY0, NZ0)
    return tuple(
        call(
            finish,
            [own, own],
            [bot] * 4 + [(10, R2, 128)] * 2 + [mid] * 3 + [(20, Q1, 128)] + [(18, Q1, 128)] * 2
            + [(16, Q0, 256)] + [big] * 3,
            res2, coef2, res1, sol1, coef1, left, right, sol0, res_q, diag_q, inv_q, low, high,
        )
    )


def solution(mesh):
    return jax.shard_map(
        per_device,
        mesh=mesh,
        in_specs=(P("gx", "gy", "gz"), P("gx", "gy", "gz")),
        out_specs=(P("gx", "gy", "gz"), P("gx", "gy", "gz")),
        check_vma=False,
    )
```

```python
import jax
import jax.numpy as jnp
from jax import lax
from jax.experimental import pallas as pl
from jax.experimental.pallas import tpu as pltpu
from jax.sharding import PartitionSpec as P

SWEEPS = 3
COARSE_SWEEPS = 6
THETA = 1.25
DELTA = 0.75
F32 = jnp.float32
EXACT = lax.Precision.HIGHEST

XH = 3
NX0, NY0, NZ0 = 8, 64, 128
NXE = NX0 + 2 * XH
W = 9
R0 = 88
Q0 = 72
R1 = 40
Q1 = 48
R2 = 32
MIB = 1024 * 1024


def coefficients(count):
    sigma = THETA / DELTA
    rho = 1.0 / sigma
    pairs = []
    for _ in range(count):
        rho_new = 1.0 / (2.0 * sigma - rho)
        pairs.append((rho_new * rho, 2.0 * rho_new / DELTA))
        rho = rho_new
    return pairs


def turn(value, shift, axis):
    return pltpu.roll(value, shift % value.shape[axis], axis)


def beside(value):
    return (turn(value, 1, 0) + turn(value, -1, 0)) + (turn(value, 1, 1) + turn(value, -1, 1))


def rows_of(shape):
    return lax.broadcasted_iota(jnp.int32, shape, 0)


def lanes_of(shape):
    return lax.broadcasted_iota(jnp.int32, shape, 1)


def inside_yz(shape, own_rows, split_row, own_lanes, split_lane):
    gy, gz = lax.axis_index("gy"), lax.axis_index("gz")
    last_y, last_z = lax.axis_size("gy") - 1, lax.axis_size("gz") - 1
    row, lane = rows_of(shape), lanes_of(shape)
    up_y, down_y = (gy < last_y).astype(jnp.int32), (gy > 0).astype(jnp.int32)
    up_z, down_z = (gz < last_z).astype(jnp.int32), (gz > 0).astype(jnp.int32)
    in_y = jnp.where(row < own_rows, 1, jnp.where(row < split_row, up_y, down_y))
    in_z = jnp.where(lane < own_lanes, 1, jnp.where(lane < split_lane, up_z, down_z))
    return (in_y * in_z) > 0


def dot(a, b):
    return jnp.dot(a, b, precision=EXACT, preferred_element_type=F32)


def call(body, limit, outs, scratch, *args):
    vmem = pl.BlockSpec(memory_space=pltpu.VMEM)
    return pl.pallas_call(
        body,
        out_shape=[jax.ShapeDtypeStruct(s, F32) for s in outs],
        in_specs=[vmem] * len(args),
        out_specs=[vmem] * len(outs),
        scratch_shapes=[pltpu.VMEM(s, F32) for s in scratch],
        compiler_params=pltpu.CompilerParams(vmem_limit_bytes=limit * MIB),
    )(*args)


def ring(value, axis, shift):
    size = lax.axis_size(axis)
    return lax.ppermute(value, axis, [(i, (i + shift) % size) for i in range(size)])


def plane_of(own, low, high, which, x):
    if x < XH:
        return low.at[which * XH + x]
    if x < XH + NX0:
        return own[which].at[x - XH]
    return high.at[which * XH + x - XH - NX0]


def pack_y(s, c, low, high, up, down):
    for a in range(2):
        for x in range(NXE):
            src = plane_of((s, c), low, high, a, x)
            at = a * NXE + x
            up[at * 8 : at * 8 + 8, :] = src[56:64, :]
            down[at * 8 : at * 8 + 8, :] = src[0:8, :]
            up[224 + at : 225 + at, :] = src[55:56, :]
            down[224 + at : 225 + at, :] = src[8:9, :]
    up[252:256, :] = jnp.zeros((4, 128), F32)
    down[252:256, :] = jnp.zeros((4, 128), F32)


def pack_z(s, c, low, high, below, above, main, up, down):
    lane = lanes_of((R0, 128))
    for a in range(2):
        ups = jnp.zeros((R0, 128), F32)
        downs = jnp.zeros((R0, 128), F32)
        for x in range(NXE):
            src = plane_of((s, c), low, high, a, x)
            at = a * NXE + x
            main[a, x, 0:64, :] = src[...]
            main[a, x, 64:72, :] = above[at * 8 : at * 8 + 8, :]
            main[a, x, 72:80, :] = jnp.zeros((8, 128), F32)
            main[a, x, 72:73, :] = above[224 + at : 225 + at, :]
            main[a, x, 79:80, :] = below[224 + at : 225 + at, :]
            main[a, x, 80:88, :] = below[at * 8 : at * 8 + 8, :]
            plane = main[a, x]
            here = (lane >= W * x) & (lane < W * x + W)
            ups = jnp.where(here, turn(plane, W * x - (128 - W), 1), ups)
            downs = jnp.where(here, turn(plane, W * x, 1), downs)
        up[a] = ups
        down[a] = downs


def fine_sweep(src, dst, res, diag, inverse, first, stop, pair, also):
    def body(x, carry):
        d = src[x]
        near = beside(d) + (src[x - 1] + src[x + 1])
        r = res[x] - (diag[x] * d - near)
        res[x] = r
        also(x, d)
        if pair is not None:
            dst[x] = pair[0] * d + (pair[1] * inverse[x]) * r
        return carry

    lax.fori_loop(first, stop, body, 0)


def to_q0(ref, x):
    tail = jnp.where(rows_of((8, 256)) < 4, ref[x, 64:72, :], ref[x, 80:88, :])
    return ref[x, 0:64, :], tail


def fine_before(
    main, below, above, sol, res_q, diag_q, inv_q, msg2, msg_up, msg_down, res, diag, inv, da, db
):
    lane = lanes_of((R0, 128))
    for a in range(2):
        left, right = below[a], above[a]
        for x in range(NXE):
            side = jnp.where(lane < W, turn(right, -W * x, 1), 0.0)
            side = jnp.where(lane >= 128 - W, turn(left, 128 - W - W * x, 1), side)
            ref = (res, diag)[a]
            ref[x, :, 0:128] = main[a, x]
            ref[x, :, 128:256] = side
    row40, row88 = rows_of((R1, R0)), lanes_of((R1, R0))
    fold_y = jnp.where(row88 // 2 == jnp.where(row40 < 36, row40, row40 + 4), 0.125, 0.0).astype(F32)
    fold_z = jnp.where(rows_of((256, 128)) // 2 == lanes_of((256, 128)), 1.0, 0.0).astype(F32)

    def fold(ref, i):
        both = ref[XH + 2 * i] + ref[XH + 2 * i + 1]
        return dot(fold_y, dot(both, fold_z))

    coef1 = [fold(diag, i) for i in range(4)]

    gx = lax.axis_index("gx")
    in_yz = inside_yz((R0, 256), 64, 76, 128, 192)
    low_x, high_x = gx > 0, gx < lax.axis_size("gx") - 1

    def start(x, carry):
        g = diag[x] + 6.0
        diag[x] = g
        here = ((x >= XH) | low_x) & ((x < XH + NX0) | high_x)
        inverse = jnp.where(in_yz & here, 1.0 / g, 0.0)
        inv[x] = inverse
        da[x] = res[x] * inverse * (1.0 / THETA)
        top, tail = to_q0(diag, x)
        diag_q[x, 0:64, :] = top
        diag_q[x, 64:72, :] = tail
        top, tail = to_q0(inv, x)
        inv_q[x, 0:64, :] = top
        inv_q[x, 64:72, :] = tail
        return carry

    lax.fori_loop(0, NXE, start, 0)

    pairs = coefficients(SWEEPS)
    buffers = (da, db)
    for k in range(SWEEPS):
        src, dst = buffers[k % 2], buffers[(k + 1) % 2]
        last = k == SWEEPS - 1

        def nothing(x, d):
            return None

        fine_sweep(src, dst, res, diag, inv, k + 1, NXE - 1 - k, None if last else pairs[k], nothing)

        def gather(x, carry):
            own = src[XH + x, 0:64, 0:128]
            sol[x] = own if k == 0 else sol[x] + own
            return carry

        lax.fori_loop(0, NX0, gather, 0)

    def keep(x, carry):
        top, tail = to_q0(res, XH + x)
        res_q[x, 0:64, :] = top
        res_q[x, 64:72, :] = tail
        return carry

    lax.fori_loop(0, NX0, keep, 0)

    lane40 = lanes_of((R1, 128))
    halo = jnp.zeros((R1, 128), F32)
    for i in range(4):
        r1, c1 = fold(res, i), coef1[i]
        both = jnp.where(lane40 < 64, r1, turn(c1, 64, 1))
        for msg in (msg2, msg_up, msg_down):
            msg[i * R1 : i * R1 + R1, :] = both
        for a, v in ((0, r1), (1, c1)):
            base = (a * 4 + i) * 8
            halo = jnp.where((lane40 >= base) & (lane40 < base + 4), turn(v, base - 64, 1), halo)
            halo = jnp.where((lane40 >= base + 4) & (lane40 < base + 8), turn(v, base + 4 - 124, 1), halo)
    msg2[160:200, :] = halo
    lane72 = lanes_of((Q0, 128))
    for msg, first in ((msg_up, NX0 - XH), (msg_down, 0)):
        side = jnp.zeros((Q0, 128), F32)
        for i in range(XH):
            msg[160 + i * Q0 : 160 + i * Q0 + Q0, :] = res_q[first + i, :, 0:128]
            v = res_q[first + i, :, 128:256]
            base = 64 + 6 * i
            side = jnp.where((lane72 >= base) & (lane72 < base + 3), turn(v, base, 1), side)
            side = jnp.where((lane72 >= base + 3) & (lane72 < base + 6), turn(v, base + 3 - 125, 1), side)
        at = 160 + XH * Q0
        msg[at : at + R1, :] = jnp.where(lane40 < 64, halo, side[0:R1])
        msg[at + R1 : at + Q0, :] = side[R1:Q0]


def line_sweep(src, dst, res, diag, inverse, planes, scale, pair, sol, ahead=0):
    def body(x, carry):
        d = src[x + 1]
        near = beside(d) + (src[x] + src[x + 2])
        r = res[x] - (diag[x] * d - scale * near)
        res[x] = r
        if pair is not None:
            step = pair[0] * d + (pair[1] * inverse[x]) * r
            dst[x + 1] = step
            sol[x + ahead] += step
        return carry

    lax.fori_loop(0, planes, body, 0, unroll=True)


def middle_before(own, low, high, far, res, sol, coef, low_res, low_coef, up, down, diag, inv, da, db):
    gx = lax.axis_index("gx")
    size = lax.axis_size("gx")
    lane40 = lanes_of((R1, 128))
    for msg, shift, side_at in ((own, 0, 160), (low, 3, 160 + XH * Q0), (high, 1, 160 + XH * Q0), (far, 2, 160)):
        place = lax.rem(gx + shift, size) * 4
        side = msg[side_at : side_at + R1, :]
        for i in range(4):
            both = msg[i * R1 : i * R1 + R1, :]
            for a, ref in ((0, res), (1, coef)):
                base = (a * 4 + i) * 8
                v = both if a == 0 else turn(both, 64, 1)
                v = jnp.where(lane40 < 64, v, turn(side, 64 - base, 1))
                v = jnp.where(lane40 < 68, v, 0.0)
                v = jnp.where(lane40 < 124, v, turn(side, 124 - base - 4, 1))
                ref[place + i] = v
    in_yz = inside_yz((R1, 128), 32, 36, 64, 96)
    empty = jnp.zeros((R1, 128), F32)
    for buffer in (da, db):
        buffer[0] = empty
        buffer[17] = empty

    def start(x, carry):
        g = coef[x] + 1.5
        diag[x] = g
        inverse = jnp.where(in_yz, 1.0 / g, 0.0)
        inv[x] = inverse
        d = res[x] * inverse * (1.0 / THETA)
        da[x + 1] = d
        sol[x] = d
        return carry

    lax.fori_loop(0, 16, start, 0)
    pairs = coefficients(SWEEPS)
    buffers = (da, db)
    for k in range(SWEEPS):
        src, dst = buffers[k % 2], buffers[(k + 1) % 2]
        line_sweep(src, dst, res, diag, inv, 16, 0.25, pairs[k] if k < SWEEPS - 1 else None, sol)
    fold_y = jnp.where(lanes_of((16, R1)) // 2 == rows_of((16, R1)), 0.125, 0.0).astype(F32)
    fold_z = jnp.where(
        (rows_of((128, 128)) // 2 == lanes_of((128, 128))) & (lanes_of((128, 128)) < 32), 1.0, 0.0
    ).astype(F32)
    lane8 = lanes_of((8, 128))
    for i in range(8):
        r2 = dot(fold_y, dot(res[2 * i] + res[2 * i + 1], fold_z))
        c2 = dot(fold_y, dot(coef[2 * i] + coef[2 * i + 1], fold_z))
        low_res[i] = r2
        low_coef[i] = c2
        both = r2 + turn(c2, 32, 1)
        up[i * 8 : i * 8 + 8, :] = both[8:16]
        down[i * 8 : i * 8 + 8, :] = both[0:8]
    for x in range(16):
        at = 64 + x * 8
        up[at : at + 8, :] = jnp.where(lane8 < 64, res[x, 24:32, :], turn(sol[x, 24:32, :], 64, 1))
        down[at : at + 8, :] = jnp.where(lane8 < 64, res[x, 0:8, :], turn(sol[x, 0:8, :], 64, 1))


def pack_low_z(low_res, low_coef, res, sol, below, above, res2, coef2, res1, sol1, up, down):
    lane2 = lanes_of((R2, 128))
    lane1 = lanes_of((Q1, 128))
    lane8 = lanes_of((8, 128))
    ups = jnp.zeros((R2, 128), F32)
    downs = jnp.zeros((R2, 128), F32)
    for i in range(8):
        res2[i, 0:16, :] = low_res[i]
        coef2[i, 0:16, :] = low_coef[i]
        for msg, at in ((above, 16), (below, 24)):
            both = msg[i * 8 : i * 8 + 8, :]
            res2[i, at : at + 8, :] = jnp.where(lane8 < 32, both, 0.0)
            coef2[i, at : at + 8, :] = jnp.where(lane8 < 32, turn(both, -32, 1), 0.0)
        for a, ref in ((0, res2), (1, coef2)):
            v = ref[i]
            base = a * 64 + i * 8
            here = (lane2 >= base) & (lane2 < base + 8)
            ups = jnp.where(here, turn(v, base - 24, 1), ups)
            downs = jnp.where(here, turn(v, base, 1), downs)
    up[0:R2, :] = ups
    down[0:R2, :] = downs
    ups = jnp.zeros((Q1, 128), F32)
    downs = jnp.zeros((Q1, 128), F32)
    for x in range(16):
        res1[x, 0:32, :] = jnp.where(lanes_of((32, 128)) < 64, res[x, 0:32, :], 0.0)
        sol1[x, 0:32, :] = jnp.where(lanes_of((32, 128)) < 64, sol[x, 0:32, :], 0.0)
        for msg, at in ((above, 32), (below, 40)):
            both = msg[64 + x * 8 : 72 + x * 8, :]
            res1[x, at : at + 8, :] = jnp.where(lane8 < 64, both, 0.0)
            sol1[x, at : at + 8, :] = jnp.where(lane8 < 64, turn(both, 64, 1), 0.0)
        base = 4 * x
        here = (lane1 >= base) & (lane1 < base + 4)
        ups = jnp.where(here, turn(res1[x], base - 60, 1), ups)
        downs = jnp.where(here, turn(res1[x], base, 1), downs)
        base = 64 + 2 * x
        here = (lane1 >= base) & (lane1 < base + 2)
        ups = jnp.where(here, turn(sol1[x], base - 62, 1), ups)
        downs = jnp.where(here, turn(sol1[x], base, 1), downs)
    up[R2 : R2 + Q1, :] = ups
    down[R2 : R2 + Q1, :] = downs


def bottom(res2_in, coef2_in, left, right, sol2, res2, diag2, inv2, da2, db2):
    lane2 = lanes_of((R2, 128))
    in_yz = inside_yz((R2, 128), 16, 24, 32, 64)
    empty = jnp.zeros((R2, 128), F32)
    for buffer in (da2, db2):
        buffer[0] = empty
        buffer[9] = empty
    from_left, from_right = left[0:R2, :], right[0:R2, :]
    for i in range(8):
        parts = []
        for a, ref in ((0, res2_in), (1, coef2_in)):
            base = a * 64 + i * 8
            v = jnp.where(lane2 < 32, ref[i], turn(from_right, 32 - base, 1))
            v = jnp.where(lane2 < 40, v, 0.0)
            parts.append(jnp.where(lane2 < 120, v, turn(from_left, 120 - base, 1)))
        g = parts[1] + 0.375
        inverse = jnp.where(in_yz, 1.0 / g, 0.0)
        res2[i] = parts[0]
        diag2[i] = g
        inv2[i] = inverse
        d = parts[0] * inverse * (1.0 / THETA)
        da2[i + 1] = d
        sol2[i] = d
    pairs = coefficients(COARSE_SWEEPS)
    buffers = (da2, db2)
    for k in range(COARSE_SWEEPS - 1):
        src, dst = buffers[k % 2], buffers[(k + 1) % 2]
        line_sweep(src, dst, res2, diag2, inv2, 8, 0.0625, pairs[k], sol2)


def middle_after(sol2, res1_in, sol1_in, coef1, left, right, sol1, res1, diag1, inv1, da1, db1):
    lane1 = lanes_of((Q1, 128))
    in_yz1 = inside_yz((Q1, 128), 32, 40, 64, 96)
    empty = jnp.zeros((Q1, 128), F32)
    for buffer in (da1, db1):
        buffer[0] = empty
        buffer[17] = empty
    for x in (0, 1, 18, 19):
        sol1[x] = empty
    from_left, from_right = left[R2 : R2 + Q1, :], right[R2 : R2 + Q1, :]
    row, col = rows_of((Q1, R2)), lanes_of((Q1, R2))
    lift_y = jnp.where(col == row // 2 + jnp.where(row >= 40, 8, 0), 1.0, 0.0).astype(F32)
    row, col = rows_of((128, 128)), lanes_of((128, 128))
    lift_z = jnp.where(row == col // 2 + jnp.where(col >= 96, 64, 0), 1.0, 0.0).astype(F32)
    for i in range(8):
        lifted = dot(lift_y, dot(sol2[i], lift_z))
        for x in (2 * i, 2 * i + 1):
            db1[x + 1] = lifted
            base = 4 * x
            v = jnp.where(lane1 < 64, res1_in[x], turn(from_right, 64 - base, 1))
            v = jnp.where(lane1 < 68, v, 0.0)
            res1[x] = jnp.where(lane1 < 124, v, turn(from_left, 124 - base, 1))
            base = 64 + 2 * x
            v = jnp.where(lane1 < 64, sol1_in[x], turn(from_right, 64 - base, 1))
            v = jnp.where(lane1 < 66, v, 0.0)
            v = jnp.where(lane1 < 126, v, turn(from_left, 126 - base, 1))
            sol1[x + 2] = jnp.where(in_yz1, v, 0.0) + lifted

    def correct1(x, carry):
        g = jnp.concatenate([coef1[x], coef1[x, 32:40, :]], 0) + 1.5
        inverse = jnp.where(in_yz1, 1.0 / g, 0.0)
        diag1[x] = g
        inv1[x] = inverse
        p = db1[x + 1]
        near = beside(p) + (db1[x] + db1[x + 2])
        r = res1[x] - (g * p - 0.25 * near)
        res1[x] = r
        d = r * inverse * (1.0 / THETA)
        da1[x + 1] = d
        sol1[x + 2] += d
        return carry

    lax.fori_loop(0, 16, correct1, 0)
    pairs = coefficients(SWEEPS)
    buffers = (da1, db1)
    for k in range(SWEEPS - 1):
        src, dst = buffers[k % 2], buffers[(k + 1) % 2]
        line_sweep(src, dst, res1, diag1, inv1, 16, 0.25, pairs[k], sol1, 2)


def fine_after(
    sol1, sol0, res_q, diag_q, inv_q, low, high, out_sol, out_res, p0, res0, da0, db0
):
    gx = lax.axis_index("gx")
    row, col = rows_of((Q0, Q1)), lanes_of((Q0, Q1))
    lift_y = jnp.where(col == row // 2 + jnp.where(row >= 68, 12, 0), 1.0, 0.0).astype(F32)
    lift_z = jnp.where(rows_of((128, 256)) == lanes_of((128, 256)) // 2, 1.0, 0.0).astype(F32)
    for i in range(8):
        lifted = dot(lift_y, dot(sol1[gx * 4 + i], lift_z))
        p0[2 * i] = lifted
        p0[2 * i + 1] = lifted
    lane72 = lanes_of((Q0, 128))
    at = 160 + XH * Q0
    for msg, first in ((low, 0), (high, XH + NX0)):
        side = msg[at : at + Q0, :]
        for i in range(XH):
            base = 64 + 6 * i
            v = jnp.where(lane72 < 3, turn(side, -base, 1), 0.0)
            v = jnp.where(lane72 < 125, v, turn(side, 125 - base - 3, 1))
            res0[first + i, :, 0:128] = msg[160 + i * Q0 : 160 + i * Q0 + Q0, :]
            res0[first + i, :, 128:256] = v

    def fetch(x, carry):
        res0[x + XH] = res_q[x]
        return carry

    lax.fori_loop(0, NX0, fetch, 0)

    def correct0(x, carry):
        p = p0[x + 1]
        near = beside(p) + (p0[x] + p0[x + 2])
        r = res0[x] - (diag_q[x] * p - near)
        res0[x] = r
        da0[x] = r * inv_q[x] * (1.0 / THETA)
        return carry

    lax.fori_loop(0, NXE, correct0, 0)

    def begin(x, carry):
        out_sol[x] = sol0[x] + p0[x + XH + 1, 0:64, 0:128]
        return carry

    lax.fori_loop(0, NX0, begin, 0)
    pairs = coefficients(SWEEPS)
    buffers = (da0, db0)
    for k in range(SWEEPS):
        src, dst = buffers[k % 2], buffers[(k + 1) % 2]

        def gather0(x, carry):
            out_sol[x] += src[x + XH, 0:64, 0:128]
            return carry

        lax.fori_loop(0, NX0, gather0, 0)
        fine_sweep(
            src, dst, res0, diag_q, inv_q, k + 1, NXE - 1 - k, pairs[k] if k < SWEEPS - 1 else None,
            lambda x, d: None,
        )

    def put(x, carry):
        out_res[x] = res0[x + XH, 0:64, 0:128]
        return carry

    lax.fori_loop(0, NX0, put, 0)


def per_device(s, c):
    up = jnp.concatenate([s[NX0 - XH :], c[NX0 - XH :]], 0)
    down = jnp.concatenate([s[:XH], c[:XH]], 0)
    low, high = ring(up, "gx", 1), ring(down, "gx", -1)
    up, down = call(pack_y, 4, [(256, 128)] * 2, [], s, c, low, high)
    below, above = ring(up, "gy", 1), ring(down, "gy", -1)
    main, up, down = call(
        pack_z, 8, [(2, NXE, R0, 128), (2, R0, 128), (2, R0, 128)], [], s, c, low, high, below, above
    )
    below, above = ring(up, "gz", 1), ring(down, "gz", -1)
    big = (NXE, R0, 256)
    sol0, res_q, diag_q, inv_q, msg2, msg_up, msg_down = call(
        fine_before,
        16,
        [(NX0, 64, 128), (NX0, Q0, 256), (NXE, Q0, 256), (NXE, Q0, 256), (200, 128), (448, 128), (448, 128)],
        [big] * 5,
        main, below, above,
    )
    low, high, far = ring(msg_up, "gx", 1), ring(msg_down, "gx", -1), ring(msg2, "gx", 2)
    mid = (16, R1, 128)
    res1, sol1, coef1, res2, coef2, up, down = call(
        middle_before,
        8,
        [mid, mid, mid, (8, 16, 128), (8, 16, 128), (192, 128), (192, 128)],
        [mid, mid, (18, R1, 128), (18, R1, 128)],
        msg2, low, high, far,
    )
    below, above = ring(up, "gy", 1), ring(down, "gy", -1)
    bot, mid = (8, R2, 128), (16, Q1, 128)
    res2, coef2, res1, sol1, up, down = call(
        pack_low_z,
        4,
        [bot, bot, mid, mid, (R2 + Q1, 128), (R2 + Q1, 128)],
        [],
        res2, coef2, res1, sol1, below, above,
    )
    left, right = ring(up, "gz", 1), ring(down, "gz", -1)
    big = (NXE, Q0, 256)
    own = (NX0, NY0, NZ0)
    (sol2,) = call(
        bottom, 4, [bot], [bot] * 3 + [(10, R2, 128)] * 2, res2, coef2, left, right
    )
    (sol1,) = call(
        middle_after,
        8,
        [(20, Q1, 128)],
        [mid] * 3 + [(18, Q1, 128)] * 2,
        sol2, res1, sol1, coef1, left, right,
    )
    return tuple(
        call(
            fine_after,
            16,
            [own, own],
            [(16, Q0, 256)] + [big] * 3,
            sol1, sol0, res_q, diag_q, inv_q, low, high,
        )
    )


def solution(mesh):
    return jax.shard_map(
        per_device,
        mesh=mesh,
        in_specs=(P("gx", "gy", "gz"), P("gx", "gy", "gz")),
        out_specs=(P("gx", "gy", "gz"), P("gx", "gy", "gz")),
        check_vma=False,
    )
```

```python
import jax
import jax.numpy as jnp
from jax import lax
from jax.experimental import pallas as pl
from jax.experimental.pallas import tpu as pltpu
from jax.sharding import PartitionSpec as P

SWEEPS = 3
COARSE_SWEEPS = 6
THETA = 1.25
DELTA = 0.75
F32 = jnp.float32
EXACT = lax.Precision.HIGHEST

XH = 3
NX0, NY0, NZ0 = 8, 64, 128
NXE = NX0 + 2 * XH
W = 9
R0 = 88
Q0 = 72
R1 = 40
Q1 = 48
R2 = 32
MIB = 1024 * 1024


def coefficients(count):
    sigma = THETA / DELTA
    rho = 1.0 / sigma
    pairs = []
    for _ in range(count):
        rho_new = 1.0 / (2.0 * sigma - rho)
        pairs.append((rho_new * rho, 2.0 * rho_new / DELTA))
        rho = rho_new
    return pairs


def turn(value, shift, axis):
    return pltpu.roll(value, shift % value.shape[axis], axis)


def beside(value):
    return (turn(value, 1, 0) + turn(value, -1, 0)) + (turn(value, 1, 1) + turn(value, -1, 1))


def rows_of(shape):
    return lax.broadcasted_iota(jnp.int32, shape, 0)


def lanes_of(shape):
    return lax.broadcasted_iota(jnp.int32, shape, 1)


def inside_yz(shape, own_rows, split_row, own_lanes, split_lane):
    gy, gz = lax.axis_index("gy"), lax.axis_index("gz")
    last_y, last_z = lax.axis_size("gy") - 1, lax.axis_size("gz") - 1
    row, lane = rows_of(shape), lanes_of(shape)
    up_y, down_y = (gy < last_y).astype(jnp.int32), (gy > 0).astype(jnp.int32)
    up_z, down_z = (gz < last_z).astype(jnp.int32), (gz > 0).astype(jnp.int32)
    in_y = jnp.where(row < own_rows, 1, jnp.where(row < split_row, up_y, down_y))
    in_z = jnp.where(lane < own_lanes, 1, jnp.where(lane < split_lane, up_z, down_z))
    return (in_y * in_z) > 0


def dot(a, b):
    return jnp.dot(a, b, precision=EXACT, preferred_element_type=F32)


def call(body, limit, outs, scratch, *args):
    vmem = pl.BlockSpec(memory_space=pltpu.VMEM)
    return pl.pallas_call(
        body,
        out_shape=[jax.ShapeDtypeStruct(s, F32) for s in outs],
        in_specs=[vmem] * len(args),
        out_specs=[vmem] * len(outs),
        scratch_shapes=[pltpu.VMEM(s, F32) for s in scratch],
        compiler_params=pltpu.CompilerParams(vmem_limit_bytes=limit * MIB),
    )(*args)


def ring(value, axis, shift):
    size = lax.axis_size(axis)
    return lax.ppermute(value, axis, [(i, (i + shift) % size) for i in range(size)])


def plane_of(own, low, high, which, x):
    if x < XH:
        return low.at[which * XH + x]
    if x < XH + NX0:
        return own[which].at[x - XH]
    return high.at[which * XH + x - XH - NX0]


def pack_y(s, c, low, high, up, down):
    for a in range(2):
        for x in range(NXE):
            src = plane_of((s, c), low, high, a, x)
            at = a * NXE + x
            up[at * 8 : at * 8 + 8, :] = src[56:64, :]
            down[at * 8 : at * 8 + 8, :] = src[0:8, :]
            up[224 + at : 225 + at, :] = src[55:56, :]
            down[224 + at : 225 + at, :] = src[8:9, :]
    up[252:256, :] = jnp.zeros((4, 128), F32)
    down[252:256, :] = jnp.zeros((4, 128), F32)


def pack_z(s, c, low, high, below, above, main, up, down):
    lane = lanes_of((R0, 128))
    for a in range(2):
        ups = jnp.zeros((R0, 128), F32)
        downs = jnp.zeros((R0, 128), F32)
        for x in range(NXE):
            src = plane_of((s, c), low, high, a, x)
            at = a * NXE + x
            main[a, x, 0:64, :] = src[...]
            main[a, x, 64:72, :] = above[at * 8 : at * 8 + 8, :]
            main[a, x, 72:80, :] = jnp.zeros((8, 128), F32)
            main[a, x, 72:73, :] = above[224 + at : 225 + at, :]
            main[a, x, 79:80, :] = below[224 + at : 225 + at, :]
            main[a, x, 80:88, :] = below[at * 8 : at * 8 + 8, :]
            plane = main[a, x]
            here = (lane >= W * x) & (lane < W * x + W)
            ups = jnp.where(here, turn(plane, W * x - (128 - W), 1), ups)
            downs = jnp.where(here, turn(plane, W * x, 1), downs)
        up[a] = ups
        down[a] = downs


def fine_sweep(src, dst, res, diag, inverse, first, stop, pair, also):
    def body(x, carry):
        d = src[x]
        near = beside(d) + (src[x - 1] + src[x + 1])
        r = res[x] - (diag[x] * d - near)
        res[x] = r
        also(x, d)
        if pair is not None:
            dst[x] = pair[0] * d + (pair[1] * inverse[x]) * r
        return carry

    lax.fori_loop(first, stop, body, 0, unroll=True)


def to_q0(ref, x):
    tail = jnp.where(rows_of((8, 256)) < 4, ref[x, 64:72, :], ref[x, 80:88, :])
    return ref[x, 0:64, :], tail


def fine_before(
    main, below, above, sol, res_q, diag_q, inv_q, msg2, msg_up, msg_down, res, diag, inv, da, db
):
    lane = lanes_of((R0, 128))
    for a in range(2):
        left, right = below[a], above[a]
        for x in range(NXE):
            side = jnp.where(lane < W, turn(right, -W * x, 1), 0.0)
            side = jnp.where(lane >= 128 - W, turn(left, 128 - W - W * x, 1), side)
            ref = (res, diag)[a]
            ref[x, :, 0:128] = main[a, x]
            ref[x, :, 128:256] = side
    row40, row88 = rows_of((R1, R0)), lanes_of((R1, R0))
    fold_y = jnp.where(row88 // 2 == jnp.where(row40 < 36, row40, row40 + 4), 0.125, 0.0).astype(F32)
    fold_z = jnp.where(rows_of((256, 128)) // 2 == lanes_of((256, 128)), 1.0, 0.0).astype(F32)

    def fold(ref, i):
        both = ref[XH + 2 * i] + ref[XH + 2 * i + 1]
        return dot(fold_y, dot(both, fold_z))

    coef1 = [fold(diag, i) for i in range(4)]

    gx = lax.axis_index("gx")
    in_yz = inside_yz((R0, 256), 64, 76, 128, 192)
    low_x, high_x = gx > 0, gx < lax.axis_size("gx") - 1

    def start(x, carry):
        g = diag[x] + 6.0
        diag[x] = g
        here = ((x >= XH) | low_x) & ((x < XH + NX0) | high_x)
        inverse = jnp.where(in_yz & here, 1.0 / g, 0.0)
        inv[x] = inverse
        da[x] = res[x] * inverse * (1.0 / THETA)
        top, tail = to_q0(diag, x)
        diag_q[x, 0:64, :] = top
        diag_q[x, 64:72, :] = tail
        top, tail = to_q0(inv, x)
        inv_q[x, 0:64, :] = top
        inv_q[x, 64:72, :] = tail
        return carry

    lax.fori_loop(0, NXE, start, 0, unroll=True)

    pairs = coefficients(SWEEPS)
    buffers = (da, db)
    for k in range(SWEEPS):
        src, dst = buffers[k % 2], buffers[(k + 1) % 2]
        last = k == SWEEPS - 1

        def nothing(x, d):
            return None

        fine_sweep(src, dst, res, diag, inv, k + 1, NXE - 1 - k, None if last else pairs[k], nothing)

        def gather(x, carry):
            own = src[XH + x, 0:64, 0:128]
            sol[x] = own if k == 0 else sol[x] + own
            return carry

        lax.fori_loop(0, NX0, gather, 0, unroll=True)

    def keep(x, carry):
        top, tail = to_q0(res, XH + x)
        res_q[x, 0:64, :] = top
        res_q[x, 64:72, :] = tail
        return carry

    lax.fori_loop(0, NX0, keep, 0, unroll=True)

    lane40 = lanes_of((R1, 128))
    halo = jnp.zeros((R1, 128), F32)
    for i in range(4):
        r1, c1 = fold(res, i), coef1[i]
        both = jnp.where(lane40 < 64, r1, turn(c1, 64, 1))
        for msg in (msg2, msg_up, msg_down):
            msg[i * R1 : i * R1 + R1, :] = both
        for a, v in ((0, r1), (1, c1)):
            base = (a * 4 + i) * 8
            halo = jnp.where((lane40 >= base) & (lane40 < base + 4), turn(v, base - 64, 1), halo)
            halo = jnp.where((lane40 >= base + 4) & (lane40 < base + 8), turn(v, base + 4 - 124, 1), halo)
    msg2[160:200, :] = halo
    lane72 = lanes_of((Q0, 128))
    for msg, first in ((msg_up, NX0 - XH), (msg_down, 0)):
        side = jnp.zeros((Q0, 128), F32)
        for i in range(XH):
            msg[160 + i * Q0 : 160 + i * Q0 + Q0, :] = res_q[first + i, :, 0:128]
            v = res_q[first + i, :, 128:256]
            base = 64 + 6 * i
            side = jnp.where((lane72 >= base) & (lane72 < base + 3), turn(v, base, 1), side)
            side = jnp.where((lane72 >= base + 3) & (lane72 < base + 6), turn(v, base + 3 - 125, 1), side)
        at = 160 + XH * Q0
        msg[at : at + R1, :] = jnp.where(lane40 < 64, halo, side[0:R1])
        msg[at + R1 : at + Q0, :] = side[R1:Q0]


def line_sweep(src, dst, res, diag, inverse, planes, scale, pair, sol, ahead=0):
    def body(x, carry):
        d = src[x + 1]
        near = beside(d) + (src[x] + src[x + 2])
        r = res[x] - (diag[x] * d - scale * near)
        res[x] = r
        if pair is not None:
            step = pair[0] * d + (pair[1] * inverse[x]) * r
            dst[x + 1] = step
            sol[x + ahead] += step
        return carry

    lax.fori_loop(0, planes, body, 0, unroll=True)


def middle_before(own, low, high, far, res, sol, coef, low_res, low_coef, up, down, diag, inv, da, db):
    gx = lax.axis_index("gx")
    size = lax.axis_size("gx")
    lane40 = lanes_of((R1, 128))
    for msg, shift, side_at in ((own, 0, 160), (low, 3, 160 + XH * Q0), (high, 1, 160 + XH * Q0), (far, 2, 160)):
        place = lax.rem(gx + shift, size) * 4
        side = msg[side_at : side_at + R1, :]
        for i in range(4):
            both = msg[i * R1 : i * R1 + R1, :]
            for a, ref in ((0, res), (1, coef)):
                base = (a * 4 + i) * 8
                v = both if a == 0 else turn(both, 64, 1)
                v = jnp.where(lane40 < 64, v, turn(side, 64 - base, 1))
                v = jnp.where(lane40 < 68, v, 0.0)
                v = jnp.where(lane40 < 124, v, turn(side, 124 - base - 4, 1))
                ref[place + i] = v
    in_yz = inside_yz((R1, 128), 32, 36, 64, 96)
    empty = jnp.zeros((R1, 128), F32)
    for buffer in (da, db):
        buffer[0] = empty
        buffer[17] = empty

    def start(x, carry):
        g = coef[x] + 1.5
        diag[x] = g
        inverse = jnp.where(in_yz, 1.0 / g, 0.0)
        inv[x] = inverse
        d = res[x] * inverse * (1.0 / THETA)
        da[x + 1] = d
        sol[x] = d
        return carry

    lax.fori_loop(0, 16, start, 0, unroll=True)
    pairs = coefficients(SWEEPS)
    buffers = (da, db)
    for k in range(SWEEPS):
        src, dst = buffers[k % 2], buffers[(k + 1) % 2]
        line_sweep(src, dst, res, diag, inv, 16, 0.25, pairs[k] if k < SWEEPS - 1 else None, sol)
    fold_y = jnp.where(lanes_of((16, R1)) // 2 == rows_of((16, R1)), 0.125, 0.0).astype(F32)
    fold_z = jnp.where(
        (rows_of((128, 128)) // 2 == lanes_of((128, 128))) & (lanes_of((128, 128)) < 32), 1.0, 0.0
    ).astype(F32)
    lane8 = lanes_of((8, 128))
    for i in range(8):
        r2 = dot(fold_y, dot(res[2 * i] + res[2 * i + 1], fold_z))
        c2 = dot(fold_y, dot(coef[2 * i] + coef[2 * i + 1], fold_z))
        low_res[i] = r2
        low_coef[i] = c2
        both = r2 + turn(c2, 32, 1)
        up[i * 8 : i * 8 + 8, :] = both[8:16]
        down[i * 8 : i * 8 + 8, :] = both[0:8]
    for x in range(16):
        at = 64 + x * 8
        up[at : at + 8, :] = jnp.where(lane8 < 64, res[x, 24:32, :], turn(sol[x, 24:32, :], 64, 1))
        down[at : at + 8, :] = jnp.where(lane8 < 64, res[x, 0:8, :], turn(sol[x, 0:8, :], 64, 1))


def pack_low_z(low_res, low_coef, res, sol, below, above, res2, coef2, res1, sol1, up, down):
    lane2 = lanes_of((R2, 128))
    lane1 = lanes_of((Q1, 128))
    lane8 = lanes_of((8, 128))
    ups = jnp.zeros((R2, 128), F32)
    downs = jnp.zeros((R2, 128), F32)
    for i in range(8):
        res2[i, 0:16, :] = low_res[i]
        coef2[i, 0:16, :] = low_coef[i]
        for msg, at in ((above, 16), (below, 24)):
            both = msg[i * 8 : i * 8 + 8, :]
            res2[i, at : at + 8, :] = jnp.where(lane8 < 32, both, 0.0)
            coef2[i, at : at + 8, :] = jnp.where(lane8 < 32, turn(both, -32, 1), 0.0)
        for a, ref in ((0, res2), (1, coef2)):
            v = ref[i]
            base = a * 64 + i * 8
            here = (lane2 >= base) & (lane2 < base + 8)
            ups = jnp.where(here, turn(v, base - 24, 1), ups)
            downs = jnp.where(here, turn(v, base, 1), downs)
    up[0:R2, :] = ups
    down[0:R2, :] = downs
    ups = jnp.zeros((Q1, 128), F32)
    downs = jnp.zeros((Q1, 128), F32)
    for x in range(16):
        res1[x, 0:32, :] = jnp.where(lanes_of((32, 128)) < 64, res[x, 0:32, :], 0.0)
        sol1[x, 0:32, :] = jnp.where(lanes_of((32, 128)) < 64, sol[x, 0:32, :], 0.0)
        for msg, at in ((above, 32), (below, 40)):
            both = msg[64 + x * 8 : 72 + x * 8, :]
            res1[x, at : at + 8, :] = jnp.where(lane8 < 64, both, 0.0)
            sol1[x, at : at + 8, :] = jnp.where(lane8 < 64, turn(both, 64, 1), 0.0)
        base = 4 * x
        here = (lane1 >= base) & (lane1 < base + 4)
        ups = jnp.where(here, turn(res1[x], base - 60, 1), ups)
        downs = jnp.where(here, turn(res1[x], base, 1), downs)
        base = 64 + 2 * x
        here = (lane1 >= base) & (lane1 < base + 2)
        ups = jnp.where(here, turn(sol1[x], base - 62, 1), ups)
        downs = jnp.where(here, turn(sol1[x], base, 1), downs)
    up[R2 : R2 + Q1, :] = ups
    down[R2 : R2 + Q1, :] = downs


def bottom(res2_in, coef2_in, left, right, sol2, res2, diag2, inv2, da2, db2):
    lane2 = lanes_of((R2, 128))
    in_yz = inside_yz((R2, 128), 16, 24, 32, 64)
    empty = jnp.zeros((R2, 128), F32)
    for buffer in (da2, db2):
        buffer[0] = empty
        buffer[9] = empty
    from_left, from_right = left[0:R2, :], right[0:R2, :]
    for i in range(8):
        parts = []
        for a, ref in ((0, res2_in), (1, coef2_in)):
            base = a * 64 + i * 8
            v = jnp.where(lane2 < 32, ref[i], turn(from_right, 32 - base, 1))
            v = jnp.where(lane2 < 40, v, 0.0)
            parts.append(jnp.where(lane2 < 120, v, turn(from_left, 120 - base, 1)))
        g = parts[1] + 0.375
        inverse = jnp.where(in_yz, 1.0 / g, 0.0)
        res2[i] = parts[0]
        diag2[i] = g
        inv2[i] = inverse
        d = parts[0] * inverse * (1.0 / THETA)
        da2[i + 1] = d
        sol2[i] = d
    pairs = coefficients(COARSE_SWEEPS)
    buffers = (da2, db2)
    for k in range(COARSE_SWEEPS - 1):
        src, dst = buffers[k % 2], buffers[(k + 1) % 2]
        line_sweep(src, dst, res2, diag2, inv2, 8, 0.0625, pairs[k], sol2)


def middle_after(sol2, res1_in, sol1_in, coef1, left, right, sol1, res1, diag1, inv1, da1, db1):
    lane1 = lanes_of((Q1, 128))
    in_yz1 = inside_yz((Q1, 128), 32, 40, 64, 96)
    empty = jnp.zeros((Q1, 128), F32)
    for buffer in (da1, db1):
        buffer[0] = empty
        buffer[17] = empty
    for x in (0, 1, 18, 19):
        sol1[x] = empty
    from_left, from_right = left[R2 : R2 + Q1, :], right[R2 : R2 + Q1, :]
    row, col = rows_of((Q1, R2)), lanes_of((Q1, R2))
    lift_y = jnp.where(col == row // 2 + jnp.where(row >= 40, 8, 0), 1.0, 0.0).astype(F32)
    row, col = rows_of((128, 128)), lanes_of((128, 128))
    lift_z = jnp.where(row == col // 2 + jnp.where(col >= 96, 64, 0), 1.0, 0.0).astype(F32)
    for i in range(8):
        lifted = dot(lift_y, dot(sol2[i], lift_z))
        for x in (2 * i, 2 * i + 1):
            db1[x + 1] = lifted
            base = 4 * x
            v = jnp.where(lane1 < 64, res1_in[x], turn(from_right, 64 - base, 1))
            v = jnp.where(lane1 < 68, v, 0.0)
            res1[x] = jnp.where(lane1 < 124, v, turn(from_left, 124 - base, 1))
            base = 64 + 2 * x
            v = jnp.where(lane1 < 64, sol1_in[x], turn(from_right, 64 - base, 1))
            v = jnp.where(lane1 < 66, v, 0.0)
            v = jnp.where(lane1 < 126, v, turn(from_left, 126 - base, 1))
            sol1[x + 2] = jnp.where(in_yz1, v, 0.0) + lifted

    def correct1(x, carry):
        g = jnp.concatenate([coef1[x], coef1[x, 32:40, :]], 0) + 1.5
        inverse = jnp.where(in_yz1, 1.0 / g, 0.0)
        diag1[x] = g
        inv1[x] = inverse
        p = db1[x + 1]
        near = beside(p) + (db1[x] + db1[x + 2])
        r = res1[x] - (g * p - 0.25 * near)
        res1[x] = r
        d = r * inverse * (1.0 / THETA)
        da1[x + 1] = d
        sol1[x + 2] += d
        return carry

    lax.fori_loop(0, 16, correct1, 0, unroll=True)
    pairs = coefficients(SWEEPS)
    buffers = (da1, db1)
    for k in range(SWEEPS - 1):
        src, dst = buffers[k % 2], buffers[(k + 1) % 2]
        line_sweep(src, dst, res1, diag1, inv1, 16, 0.25, pairs[k], sol1, 2)


def fine_after(
    sol1, sol0, res_q, diag_q, inv_q, low, high, out_sol, out_res, p0, res0, da0, db0
):
    gx = lax.axis_index("gx")
    row, col = rows_of((Q0, Q1)), lanes_of((Q0, Q1))
    lift_y = jnp.where(col == row // 2 + jnp.where(row >= 68, 12, 0), 1.0, 0.0).astype(F32)
    lift_z = jnp.where(rows_of((128, 256)) == lanes_of((128, 256)) // 2, 1.0, 0.0).astype(F32)
    for i in range(8):
        lifted = dot(lift_y, dot(sol1[gx * 4 + i], lift_z))
        p0[2 * i] = lifted
        p0[2 * i + 1] = lifted
    lane72 = lanes_of((Q0, 128))
    at = 160 + XH * Q0
    for msg, first in ((low, 0), (high, XH + NX0)):
        side = msg[at : at + Q0, :]
        for i in range(XH):
            base = 64 + 6 * i
            v = jnp.where(lane72 < 3, turn(side, -base, 1), 0.0)
            v = jnp.where(lane72 < 125, v, turn(side, 125 - base - 3, 1))
            res0[first + i, :, 0:128] = msg[160 + i * Q0 : 160 + i * Q0 + Q0, :]
            res0[first + i, :, 128:256] = v

    def fetch(x, carry):
        res0[x + XH] = res_q[x]
        return carry

    lax.fori_loop(0, NX0, fetch, 0, unroll=True)

    def correct0(x, carry):
        p = p0[x + 1]
        near = beside(p) + (p0[x] + p0[x + 2])
        r = res0[x] - (diag_q[x] * p - near)
        res0[x] = r
        da0[x] = r * inv_q[x] * (1.0 / THETA)
        return carry

    lax.fori_loop(0, NXE, correct0, 0, unroll=True)

    def begin(x, carry):
        out_sol[x] = sol0[x] + p0[x + XH + 1, 0:64, 0:128]
        return carry

    lax.fori_loop(0, NX0, begin, 0, unroll=True)
    pairs = coefficients(SWEEPS)
    buffers = (da0, db0)
    for k in range(SWEEPS):
        src, dst = buffers[k % 2], buffers[(k + 1) % 2]

        def gather0(x, carry):
            out_sol[x] += src[x + XH, 0:64, 0:128]
            return carry

        lax.fori_loop(0, NX0, gather0, 0, unroll=True)
        fine_sweep(
            src, dst, res0, diag_q, inv_q, k + 1, NXE - 1 - k, pairs[k] if k < SWEEPS - 1 else None,
            lambda x, d: None,
        )

    def put(x, carry):
        out_res[x] = res0[x + XH, 0:64, 0:128]
        return carry

    lax.fori_loop(0, NX0, put, 0, unroll=True)


def per_device(s, c):
    up = jnp.concatenate([s[NX0 - XH :], c[NX0 - XH :]], 0)
    down = jnp.concatenate([s[:XH], c[:XH]], 0)
    low, high = ring(up, "gx", 1), ring(down, "gx", -1)
    up, down = call(pack_y, 4, [(256, 128)] * 2, [], s, c, low, high)
    below, above = ring(up, "gy", 1), ring(down, "gy", -1)
    main, up, down = call(
        pack_z, 8, [(2, NXE, R0, 128), (2, R0, 128), (2, R0, 128)], [], s, c, low, high, below, above
    )
    below, above = ring(up, "gz", 1), ring(down, "gz", -1)
    big = (NXE, R0, 256)
    sol0, res_q, diag_q, inv_q, msg2, msg_up, msg_down = call(
        fine_before,
        16,
        [(NX0, 64, 128), (NX0, Q0, 256), (NXE, Q0, 256), (NXE, Q0, 256), (200, 128), (448, 128), (448, 128)],
        [big] * 5,
        main, below, above,
    )
    low, high, far = ring(msg_up, "gx", 1), ring(msg_down, "gx", -1), ring(msg2, "gx", 2)
    mid = (16, R1, 128)
    res1, sol1, coef1, res2, coef2, up, down = call(
        middle_before,
        8,
        [mid, mid, mid, (8, 16, 128), (8, 16, 128), (192, 128), (192, 128)],
        [mid, mid, (18, R1, 128), (18, R1, 128)],
        msg2, low, high, far,
    )
    below, above = ring(up, "gy", 1), ring(down, "gy", -1)
    bot, mid = (8, R2, 128), (16, Q1, 128)
    res2, coef2, res1, sol1, up, down = call(
        pack_low_z,
        4,
        [bot, bot, mid, mid, (R2 + Q1, 128), (R2 + Q1, 128)],
        [],
        res2, coef2, res1, sol1, below, above,
    )
    left, right = ring(up, "gz", 1), ring(down, "gz", -1)
    big = (NXE, Q0, 256)
    own = (NX0, NY0, NZ0)
    (sol2,) = call(
        bottom, 4, [bot], [bot] * 3 + [(10, R2, 128)] * 2, res2, coef2, left, right
    )
    (sol1,) = call(
        middle_after,
        8,
        [(20, Q1, 128)],
        [mid] * 3 + [(18, Q1, 128)] * 2,
        sol2, res1, sol1, coef1, left, right,
    )
    return tuple(
        call(
            fine_after,
            16,
            [own, own],
            [(16, Q0, 256)] + [big] * 3,
            sol1, sol0, res_q, diag_q, inv_q, low, high,
        )
    )


def solution(mesh):
    return jax.shard_map(
        per_device,
        mesh=mesh,
        in_specs=(P("gx", "gy", "gz"), P("gx", "gy", "gz")),
        out_specs=(P("gx", "gy", "gz"), P("gx", "gy", "gz")),
        check_vma=False,
    )
```

```python
import jax
import jax.numpy as jnp
from jax import lax
from jax.experimental import pallas as pl
from jax.experimental.pallas import tpu as pltpu
from jax.sharding import PartitionSpec as P

SWEEPS = 3
COARSE_SWEEPS = 6
THETA = 1.25
DELTA = 0.75
F32 = jnp.float32

XH = 3
NX0, NY0, NZ0 = 8, 64, 128
NXE = NX0 + 2 * XH
W = 9
R0 = 88
Q0 = 72
R1 = 40
Q1 = 48
R2 = 32
MIB = 1024 * 1024


def coefficients(count):
    sigma = THETA / DELTA
    rho = 1.0 / sigma
    pairs = []
    for _ in range(count):
        rho_new = 1.0 / (2.0 * sigma - rho)
        pairs.append((rho_new * rho, 2.0 * rho_new / DELTA))
        rho = rho_new
    return pairs


def turn(value, shift, axis):
    return pltpu.roll(value, shift % value.shape[axis], axis)


def beside(value):
    return (turn(value, 1, 0) + turn(value, -1, 0)) + (turn(value, 1, 1) + turn(value, -1, 1))


def rows_of(shape):
    return lax.broadcasted_iota(jnp.int32, shape, 0)


def lanes_of(shape):
    return lax.broadcasted_iota(jnp.int32, shape, 1)


def inside_yz(shape, own_rows, split_row, own_lanes, split_lane):
    gy, gz = lax.axis_index("gy"), lax.axis_index("gz")
    last_y, last_z = lax.axis_size("gy") - 1, lax.axis_size("gz") - 1
    row, lane = rows_of(shape), lanes_of(shape)
    up_y, down_y = (gy < last_y).astype(jnp.int32), (gy > 0).astype(jnp.int32)
    up_z, down_z = (gz < last_z).astype(jnp.int32), (gz > 0).astype(jnp.int32)
    in_y = jnp.where(row < own_rows, 1, jnp.where(row < split_row, up_y, down_y))
    in_z = jnp.where(lane < own_lanes, 1, jnp.where(lane < split_lane, up_z, down_z))
    return (in_y * in_z) > 0


def pick(value, lane):
    return jnp.take_along_axis(value, lane, axis=1, mode="promise_in_bounds")


def pairs_of_lanes(value):
    lane = lanes_of(value.shape)
    return pick(value + turn(value, -1, 1), 2 * lane - jnp.where(lane < 64, 0, 128))


def call(body, limit, outs, scratch, *args, micros=1.0):
    vmem = pl.BlockSpec(memory_space=pltpu.VMEM)
    return pl.pallas_call(
        body,
        out_shape=[jax.ShapeDtypeStruct(s, F32) for s in outs],
        in_specs=[vmem] * len(args),
        out_specs=[vmem] * len(outs),
        scratch_shapes=[pltpu.VMEM(s, F32) for s in scratch],
        compiler_params=pltpu.CompilerParams(vmem_limit_bytes=limit * MIB),
        cost_estimate=pl.CostEstimate(flops=0, bytes_accessed=int(micros * 3690000), transcendentals=0),
    )(*args)


def ring(value, axis, shift):
    size = lax.axis_size(axis)
    return lax.ppermute(value, axis, [(i, (i + shift) % size) for i in range(size)])


def plane_of(own, low, high, which, x):
    if x < XH:
        return low.at[which * XH + x]
    if x < XH + NX0:
        return own[which].at[x - XH]
    return high.at[which * XH + x - XH - NX0]


def pack_y(s, c, low, high, up, down):
    for a in range(2):
        for x in range(NXE):
            src = plane_of((s, c), low, high, a, x)
            at = a * NXE + x
            up[at * 8 : at * 8 + 8, :] = src[56:64, :]
            down[at * 8 : at * 8 + 8, :] = src[0:8, :]
            up[224 + at : 225 + at, :] = src[55:56, :]
            down[224 + at : 225 + at, :] = src[8:9, :]
    up[252:256, :] = jnp.zeros((4, 128), F32)
    down[252:256, :] = jnp.zeros((4, 128), F32)


def pack_wide(up, down, row, count, plane):
    lane = lanes_of((count, 128))
    for a in range(2):
        ups = jnp.zeros((count, 128), F32)
        downs = jnp.zeros((count, 128), F32)
        for x in range(NXE):
            v = plane(a, x)
            here = (lane >= W * x) & (lane < W * x + W)
            ups = jnp.where(here, turn(v, W * x - (128 - W), 1), ups)
            downs = jnp.where(here, turn(v, W * x, 1), downs)
        up[a, row : row + count, :] = ups
        down[a, row : row + count, :] = downs


def halo_rows(below, above, a, x):
    at = a * NXE + x
    row = rows_of((8, 128))
    middle = jnp.where(row == 0, above[224 + at : 225 + at, :], 0.0)
    middle = jnp.where(row == 7, below[224 + at : 225 + at, :], middle)
    return jnp.concatenate([above[at * 8 : at * 8 + 8, :], middle, below[at * 8 : at * 8 + 8, :]], 0)


def pack_z_own(s, c, low, high, up, down):
    pack_wide(up, down, 0, 64, lambda a, x: plane_of((s, c), low, high, a, x)[...])


def pack_z_halo(own_up, own_down, below, above, up, down):
    up[:, 0:64, :] = own_up[...]
    down[:, 0:64, :] = own_down[...]
    pack_wide(up, down, 64, 24, lambda a, x: halo_rows(below, above, a, x))


def fine_sweep(src, dst, res, diag, inverse, first, stop, pair, also):
    def body(x, carry):
        d = src[x]
        near = beside(d) + (src[x - 1] + src[x + 1])
        r = res[x] - (diag[x] * d - near)
        res[x] = r
        also(x, d)
        if pair is not None:
            dst[x] = pair[0] * d + (pair[1] * inverse[x]) * r
        return carry

    lax.fori_loop(first, stop, body, 0, unroll=True)


def to_q0(ref, x):
    tail = jnp.where(rows_of((8, 256)) < 4, ref[x, 64:72, :], ref[x, 80:88, :])
    return ref[x, 0:64, :], tail


def fine_before(
    s, c, low, high, below_y, above_y, below, above, sol, res, diag, inv, msg, da, db, rows
):
    lane = lanes_of((R0, 128))
    for a in range(2):
        left, right = below[a], above[a]
        for x in range(NXE):
            side = jnp.where(lane < W, turn(right, -W * x, 1), 0.0)
            side = jnp.where(lane >= 128 - W, turn(left, 128 - W - W * x, 1), side)
            ref = (res, diag)[a]
            ref[x, 0:64, 0:128] = plane_of((s, c), low, high, a, x)[...]
            ref[x, 64:88, 0:128] = halo_rows(below_y, above_y, a, x)
            ref[x, :, 128:256] = side
    lane40 = lanes_of((R1, 128))

    def fold(ref, i, at):
        both = ref[XH + 2 * i] + ref[XH + 2 * i + 1]
        sides = []
        for side in range(2):
            part = both[:, 128 * side : 128 * side + 128]
            rows[at, side, 0:72, :] = part[0:72]
            rows[at, side, 72:80, :] = part[80:88]
            sides.append(rows.at[at, side][pl.ds(0, R1, stride=2), :] + rows.at[at, side][pl.ds(1, R1, stride=2), :])
        return 0.125 * jnp.where(lane40 < 64, pairs_of_lanes(sides[0]), pairs_of_lanes(sides[1]))

    coef1 = [fold(diag, i, i) for i in range(4)]

    gx = lax.axis_index("gx")
    in_yz = inside_yz((R0, 256), 64, 76, 128, 192)
    low_x, high_x = gx > 0, gx < lax.axis_size("gx") - 1

    def start(x, carry):
        g = diag[x] + 6.0
        diag[x] = g
        here = ((x >= XH) | low_x) & ((x < XH + NX0) | high_x)
        inverse = jnp.where(in_yz & here, 1.0 / g, 0.0)
        inv[x] = inverse
        da[x] = res[x] * inverse * (1.0 / THETA)
        return carry

    lax.fori_loop(0, NXE, start, 0, unroll=True)

    pairs = coefficients(SWEEPS)
    buffers = (da, db)
    for k in range(SWEEPS):
        src, dst = buffers[k % 2], buffers[(k + 1) % 2]
        last = k == SWEEPS - 1

        def nothing(x, d):
            return None

        fine_sweep(src, dst, res, diag, inv, k + 1, NXE - 1 - k, None if last else pairs[k], nothing)

        def gather(x, carry):
            own = src[XH + x, 0:64, 0:128]
            sol[x] = own if k == 0 else sol[x] + own
            return carry

        lax.fori_loop(0, NX0, gather, 0, unroll=True)

    halo = jnp.zeros((R1, 128), F32)
    for i in range(4):
        r1, c1 = fold(res, i, 4 + i), coef1[i]
        both = jnp.where(lane40 < 64, r1, turn(c1, 64, 1))
        msg[i * R1 : i * R1 + R1, :] = both
        for a, v in ((0, r1), (1, c1)):
            base = (a * 4 + i) * 8
            halo = jnp.where((lane40 >= base) & (lane40 < base + 4), turn(v, base - 64, 1), halo)
            halo = jnp.where((lane40 >= base + 4) & (lane40 < base + 8), turn(v, base + 4 - 124, 1), halo)
    msg[160:200, :] = halo


def line_sweep(src, dst, res, diag, inverse, planes, scale, pair, sol, ahead=0):
    def body(x, carry):
        d = src[x + 1]
        near = beside(d) + (src[x] + src[x + 2])
        r = res[x] - (diag[x] * d - scale * near)
        res[x] = r
        if pair is not None:
            step = pair[0] * d + (pair[1] * inverse[x]) * r
            dst[x + 1] = step
            sol[x + ahead] += step
        return carry

    lax.fori_loop(0, planes, body, 0, unroll=True)


def middle_before(own, low, high, far, res, sol, coef, low_res, low_coef, up, down, diag, inv, da, db, rows):
    gx = lax.axis_index("gx")
    size = lax.axis_size("gx")
    lane40 = lanes_of((R1, 128))
    for msg, shift in ((own, 0), (low, 3), (high, 1), (far, 2)):
        place = lax.rem(gx + shift, size) * 4
        side = msg[160:200, :]
        for i in range(4):
            both = msg[i * R1 : i * R1 + R1, :]
            for a, ref in ((0, res), (1, coef)):
                base = (a * 4 + i) * 8
                v = both if a == 0 else turn(both, 64, 1)
                v = jnp.where(lane40 < 64, v, turn(side, 64 - base, 1))
                v = jnp.where(lane40 < 68, v, 0.0)
                v = jnp.where(lane40 < 124, v, turn(side, 124 - base - 4, 1))
                ref[place + i] = v
    in_yz = inside_yz((R1, 128), 32, 36, 64, 96)
    empty = jnp.zeros((R1, 128), F32)
    for buffer in (da, db):
        buffer[0] = empty
        buffer[17] = empty

    def start(x, carry):
        g = coef[x] + 1.5
        diag[x] = g
        inverse = jnp.where(in_yz, 1.0 / g, 0.0)
        inv[x] = inverse
        d = res[x] * inverse * (1.0 / THETA)
        da[x + 1] = d
        sol[x] = d
        return carry

    lax.fori_loop(0, 16, start, 0, unroll=True)
    pairs = coefficients(SWEEPS)
    buffers = (da, db)
    for k in range(SWEEPS):
        src, dst = buffers[k % 2], buffers[(k + 1) % 2]
        line_sweep(src, dst, res, diag, inv, 16, 0.25, pairs[k] if k < SWEEPS - 1 else None, sol)
    lane8, row8 = lanes_of((8, 128)), rows_of((8, 128))

    def fold(ref, i, at):
        rows[at] = ref[2 * i, 0:32, :] + ref[2 * i + 1, 0:32, :]
        part = rows.at[at]
        return 0.125 * pairs_of_lanes(part[pl.ds(0, 16, stride=2), :] + part[pl.ds(1, 16, stride=2), :])

    lows = []
    for i in range(8):
        r2, c2 = fold(res, i, i), fold(coef, i, 8 + i)
        low_res[i] = r2
        low_coef[i] = c2
        lows.append(jnp.where(lanes_of((16, 128)) < 32, r2, turn(c2, 32, 1)))
    for i in range(4):
        both = jnp.where(lanes_of((16, 128)) < 64, lows[i], turn(lows[i + 4], 64, 1))
        up[i * 8 : i * 8 + 8, :] = both[8:16]
        down[i * 8 : i * 8 + 8, :] = both[0:8]
    for i in range(8):
        at = 32 + i * 8
        tiles = []
        for first in (24, 0):
            a, b = [
                jnp.where(lane8 < 64, res[x, first : first + 8, :], turn(sol[x, first : first + 8, :], 64, 1))
                for x in (2 * i, 2 * i + 1)
            ]
            tiles.append((a, b))
        up[at : at + 8, :] = jnp.where(row8 < 4, turn(tiles[0][0], 4, 0), tiles[0][1])
        down[at : at + 8, :] = jnp.where(row8 < 4, tiles[1][0], turn(tiles[1][1], 4, 0))


def low_halo(msg, i, which):
    tile = msg[(i % 4) * 8 : (i % 4) * 8 + 8, :]
    return turn(tile, -(64 * (i // 4) + 32 * which), 1)


def middle_halo(msg, x, which, below):
    tile = msg[32 + (x // 2) * 8 : 40 + (x // 2) * 8, :]
    tile = turn(tile, 64, 1) if which else tile
    return turn(tile, 4, 0) if (x % 2 == 0) == below else tile


def pack_lanes(up, down, row, count, planes, width, base, top):
    lane = lanes_of((count, 128))
    ups, downs = up[row : row + count, :], down[row : row + count, :]
    for i, v in enumerate(planes):
        at = base + width * i
        here = (lane >= at) & (lane < at + width)
        ups = jnp.where(here, turn(v, at - (top - width), 1), ups)
        downs = jnp.where(here, turn(v, at, 1), downs)
    up[row : row + count, :] = ups
    down[row : row + count, :] = downs


def pack_low_own(low_res, low_coef, res, sol, up, down):
    up[...] = jnp.zeros((48, 128), F32)
    down[...] = jnp.zeros((48, 128), F32)
    pack_lanes(up, down, 0, 16, [low_res[i] for i in range(8)], 8, 0, 32)
    pack_lanes(up, down, 0, 16, [low_coef[i] for i in range(8)], 8, 64, 32)
    pack_lanes(up, down, 16, 32, [res[x, 0:32, :] for x in range(16)], 4, 0, 64)
    pack_lanes(up, down, 16, 32, [sol[x, 0:32, :] for x in range(16)], 2, 64, 64)


def keep_fine(after, res0, diag0, inv0, res_q, diag_q, inv_q, r0_up, r0_down):
    for ref, kept, skip in ((res0, res_q, XH), (diag0, diag_q, 0), (inv0, inv_q, 0)):
        for x in range(kept.shape[0]):
            top, tail = to_q0(ref, x + skip)
            kept[x, 0:64, :] = top
            kept[x, 64:72, :] = tail
    lane = lanes_of((Q0, 128))
    for msg, first in ((r0_up, NX0 - XH), (r0_down, 0)):
        side = jnp.zeros((Q0, 128), F32)
        for i in range(XH):
            msg[i * Q0 : i * Q0 + Q0, :] = res_q[first + i, :, 0:128]
            v = res_q[first + i, :, 128:256]
            base = 6 * i
            side = jnp.where((lane >= base) & (lane < base + 3), turn(v, base, 1), side)
            side = jnp.where((lane >= base + 3) & (lane < base + 6), turn(v, base + 3 - 125, 1), side)
        msg[XH * Q0 : XH * Q0 + Q0, :] = side


def pack_low_halo(own_up, own_down, below, above, up, down):
    for msg, own in ((up, own_up), (down, own_down)):
        msg[0:16, :] = own[0:16, :]
        msg[16:32, :] = jnp.zeros((16, 128), F32)
        msg[32:64, :] = own[16:48, :]
        msg[64:80, :] = jnp.zeros((16, 128), F32)
    for at, src, is_below in ((0, above, False), (8, below, True)):
        pack_lanes(up, down, 16 + at, 8, [low_halo(src, i, 0) for i in range(8)], 8, 0, 32)
        pack_lanes(up, down, 16 + at, 8, [low_halo(src, i, 1) for i in range(8)], 8, 64, 32)
        pack_lanes(up, down, 64 + at, 8, [middle_halo(src, x, 0, is_below) for x in range(16)], 4, 0, 64)
        pack_lanes(up, down, 64 + at, 8, [middle_halo(src, x, 1, is_below) for x in range(16)], 2, 64, 64)


def with_sides(own, left, right, base, width, own_lanes):
    lane = lanes_of(own.shape)
    v = jnp.where(lane < own_lanes, own, turn(right, own_lanes - base, 1))
    v = jnp.where(lane < own_lanes + width, v, 0.0)
    return jnp.where(lane < 128 - width, v, turn(left, 128 - width - base, 1))


def bottom(low_res, low_coef, below, above, left, right, sol2, res2, diag2, inv2, da2, db2):
    in_yz = inside_yz((R2, 128), 16, 24, 32, 64)
    empty = jnp.zeros((R2, 128), F32)
    for buffer in (da2, db2):
        buffer[0] = empty
        buffer[9] = empty
    from_left, from_right = left[0:R2, :], right[0:R2, :]
    for i in range(8):
        parts = []
        for a, ref in ((0, low_res), (1, low_coef)):
            own = jnp.concatenate([ref[i], low_halo(above, i, a), low_halo(below, i, a)], 0)
            parts.append(with_sides(own, from_left, from_right, a * 64 + i * 8, 8, 32))
        g = parts[1] + 0.375
        inverse = jnp.where(in_yz, 1.0 / g, 0.0)
        res2[i] = parts[0]
        diag2[i] = g
        inv2[i] = inverse
        d = parts[0] * inverse * (1.0 / THETA)
        da2[i + 1] = d
        sol2[i] = d
    pairs = coefficients(COARSE_SWEEPS)
    buffers = (da2, db2)
    for k in range(COARSE_SWEEPS - 1):
        src, dst = buffers[k % 2], buffers[(k + 1) % 2]
        line_sweep(src, dst, res2, diag2, inv2, 8, 0.0625, pairs[k], sol2)


def middle_after(
    sol2, res, sol, coef1, below, above, left, right, sol1, res1, diag1, inv1, da1, db1
):
    in_yz1 = inside_yz((Q1, 128), 32, 40, 64, 96)
    empty = jnp.zeros((Q1, 128), F32)
    for buffer in (da1, db1):
        buffer[0] = empty
        buffer[17] = empty
    for x in (0, 1, 18, 19):
        sol1[x] = empty
    from_left, from_right = left[R2 : R2 + Q1, :], right[R2 : R2 + Q1, :]
    lane = lanes_of((24, 128))
    half = lane // 2 + jnp.where(lane >= 96, 64, 0)
    first = rows_of((8, 128)) < 4
    for i in range(8):
        tail = jnp.where(first, sol2[i, 16:24, :], sol2[i, 24:32, :])
        lifted = pick(jnp.concatenate([sol2[i, 0:16, :], tail], 0), half)
        for x in (2 * i, 2 * i + 1):
            db1.at[x + 1][pl.ds(0, 24, stride=2), :] = lifted
            db1.at[x + 1][pl.ds(1, 24, stride=2), :] = lifted
            parts = []
            for a, ref in ((0, res), (1, sol)):
                own = jnp.concatenate(
                    [ref[x, 0:32, :], middle_halo(above, x, a, False), middle_halo(below, x, a, True)], 0
                )
                width = (4, 2)[a]
                parts.append(with_sides(own, from_left, from_right, a * 64 + width * x, width, 64))
            res1[x] = parts[0]
            sol1[x + 2] = jnp.where(in_yz1, parts[1], 0.0)

    def correct1(x, carry):
        g = jnp.concatenate([coef1[x], coef1[x, 32:40, :]], 0) + 1.5
        inverse = jnp.where(in_yz1, 1.0 / g, 0.0)
        diag1[x] = g
        inv1[x] = inverse
        p = db1[x + 1]
        near = beside(p) + (db1[x] + db1[x + 2])
        r = res1[x] - (g * p - 0.25 * near)
        res1[x] = r
        d = r * inverse * (1.0 / THETA)
        da1[x + 1] = d
        sol1[x + 2] += p + d
        return carry

    lax.fori_loop(0, 16, correct1, 0, unroll=True)
    pairs = coefficients(SWEEPS)
    buffers = (da1, db1)
    for k in range(SWEEPS - 1):
        src, dst = buffers[k % 2], buffers[(k + 1) % 2]
        line_sweep(src, dst, res1, diag1, inv1, 16, 0.25, pairs[k], sol1, 2)


def fine_after(
    sol1, sol0, res_q, diag_q, inv_q, low, high, out_sol, out_res, p0, res0, da0, db0
):
    gx = lax.axis_index("gx")
    half = lanes_of((R1, 128)) // 2
    first2 = rows_of((8, 128)) < 2
    for i in range(8):
        v = sol1[gx * 4 + i]
        v = jnp.concatenate([v[0:32], jnp.where(first2, v[32:40], turn(v[40:48], 4, 0))], 0)
        for side in range(2):
            lifted = pick(v, half + 64 * side)
            for x in (2 * i, 2 * i + 1):
                p0.at[x, side][pl.ds(0, R1, stride=2), :] = lifted
                p0.at[x, side][pl.ds(1, R1, stride=2), :] = lifted

    def lift(x):
        return jnp.concatenate([p0[x, 0, 0:Q0, :], p0[x, 1, 0:Q0, :]], 1)

    lane72 = lanes_of((Q0, 128))
    for msg, first in ((low, 0), (high, XH + NX0)):
        side = msg[XH * Q0 : XH * Q0 + Q0, :]
        for i in range(XH):
            base = 6 * i
            v = jnp.where(lane72 < 3, turn(side, -base, 1), 0.0)
            v = jnp.where(lane72 < 125, v, turn(side, 125 - base - 3, 1))
            res0[first + i, :, 0:128] = msg[i * Q0 : i * Q0 + Q0, :]
            res0[first + i, :, 128:256] = v

    def fetch(x, carry):
        res0[x + XH] = res_q[x]
        return carry

    lax.fori_loop(0, NX0, fetch, 0, unroll=True)

    def correct0(x, carry):
        p = lift(x + 1)
        near = beside(p) + (lift(x) + lift(x + 2))
        r = res0[x] - (diag_q[x] * p - near)
        res0[x] = r
        da0[x] = r * inv_q[x] * (1.0 / THETA)
        return carry

    lax.fori_loop(0, NXE, correct0, 0, unroll=True)

    def begin(x, carry):
        out_sol[x] = sol0[x] + p0[x + XH + 1, 0, 0:64, :]
        return carry

    lax.fori_loop(0, NX0, begin, 0, unroll=True)
    pairs = coefficients(SWEEPS)
    buffers = (da0, db0)
    for k in range(SWEEPS):
        src, dst = buffers[k % 2], buffers[(k + 1) % 2]

        def gather0(x, carry):
            out_sol[x] += src[x + XH, 0:64, 0:128]
            return carry

        lax.fori_loop(0, NX0, gather0, 0, unroll=True)
        fine_sweep(
            src, dst, res0, diag_q, inv_q, k + 1, NXE - 1 - k, pairs[k] if k < SWEEPS - 1 else None,
            lambda x, d: None,
        )

    def put(x, carry):
        out_res[x] = res0[x + XH, 0:64, 0:128]
        return carry

    lax.fori_loop(0, NX0, put, 0, unroll=True)


def per_device(s, c):
    up = jnp.concatenate([s[NX0 - XH :], c[NX0 - XH :]], 0)
    down = jnp.concatenate([s[:XH], c[:XH]], 0)
    low, high = ring(up, "gx", 1), ring(down, "gx", -1)
    up, down = call(pack_y, 4, [(256, 128)] * 2, [], s, c, low, high)
    below_y, above_y = ring(up, "gy", 1), ring(down, "gy", -1)
    own_up, own_down = call(pack_z_own, 4, [(2, 64, 128)] * 2, [], s, c, low, high)
    up, down = call(pack_z_halo, 4, [(2, R0, 128)] * 2, [], own_up, own_down, below_y, above_y)
    below, above = ring(up, "gz", 1), ring(down, "gz", -1)
    big = (NXE, R0, 256)
    sol0, res0, diag0, inv0, msg = call(
        fine_before,
        16,
        [(NX0, 64, 128), big, big, big, (200, 128)],
        [big, big, (8, 2, 80, 128)],
        s, c, low, high, below_y, above_y, below, above,
        micros=4.0,
    )
    low, high, far = ring(msg, "gx", 1), ring(msg, "gx", -1), ring(msg, "gx", 2)
    big = (NXE, Q0, 256)
    res_q, diag_q, inv_q, r0_up, r0_down = call(
        keep_fine,
        8,
        [(NX0, Q0, 256), big, big, (4 * Q0, 128), (4 * Q0, 128)],
        [],
        low, res0, diag0, inv0,
        micros=2.0,
    )
    r0_low, r0_high = ring(r0_up, "gx", 1), ring(r0_down, "gx", -1)
    mid = (16, R1, 128)
    res1, sol1, coef1, res2, coef2, up, down = call(
        middle_before,
        8,
        [mid, mid, mid, (8, 16, 128), (8, 16, 128), (96, 128), (96, 128)],
        [mid, mid, (18, R1, 128), (18, R1, 128), (16, 32, 128)],
        msg, low, high, far,
        micros=2.0,
    )
    below, above = ring(up, "gy", 1), ring(down, "gy", -1)
    own_up, own_down = call(pack_low_own, 4, [(48, 128)] * 2, [], res2, coef2, res1, sol1, micros=2.0)
    up, down = call(pack_low_halo, 4, [(R2 + Q1, 128)] * 2, [], own_up, own_down, below, above)
    left, right = ring(up, "gz", 1), ring(down, "gz", -1)
    bot, mid = (8, R2, 128), (16, Q1, 128)
    big = (NXE, Q0, 256)
    own = (NX0, NY0, NZ0)
    (sol2,) = call(
        bottom, 4, [bot], [bot] * 3 + [(10, R2, 128)] * 2, res2, coef2, below, above, left, right
    )
    (sol1,) = call(
        middle_after,
        8,
        [(20, Q1, 128)],
        [mid] * 3 + [(18, Q1, 128)] * 2,
        sol2, res1, sol1, coef1, below, above, left, right,
        micros=2.0,
    )
    return tuple(
        call(
            fine_after,
            16,
            [own, own],
            [(16, 2, 80, 128)] + [big] * 3,
            sol1, sol0, res_q, diag_q, inv_q, r0_low, r0_high,
        )
    )


def solution(mesh):
    return jax.shard_map(
        per_device,
        mesh=mesh,
        in_specs=(P("gx", "gy", "gz"), P("gx", "gy", "gz")),
        out_specs=(P("gx", "gy", "gz"), P("gx", "gy", "gz")),
        check_vma=False,
    )
```

```python
import jax
import jax.numpy as jnp
from jax import lax
from jax.experimental import pallas as pl
from jax.experimental.pallas import tpu as pltpu
from jax.sharding import PartitionSpec as P

SWEEPS = 3
COARSE_SWEEPS = 6
THETA = 1.25
DELTA = 0.75
F32 = jnp.float32

XH = 3
NX0, NY0, NZ0 = 8, 64, 128
NXE = NX0 + 2 * XH
W = 9
R0 = 88
Q0 = 72
R1 = 40
Q1 = 48
R2 = 32
MIB = 1024 * 1024


def coefficients(count):
    sigma = THETA / DELTA
    rho = 1.0 / sigma
    pairs = []
    for _ in range(count):
        rho_new = 1.0 / (2.0 * sigma - rho)
        pairs.append((rho_new * rho, 2.0 * rho_new / DELTA))
        rho = rho_new
    return pairs


def turn(value, shift, axis):
    return pltpu.roll(value, shift % value.shape[axis], axis)


def beside(value):
    return (turn(value, 1, 0) + turn(value, -1, 0)) + (turn(value, 1, 1) + turn(value, -1, 1))


def rows_of(shape):
    return lax.broadcasted_iota(jnp.int32, shape, 0)


def lanes_of(shape):
    return lax.broadcasted_iota(jnp.int32, shape, 1)


def inside_yz(shape, own_rows, split_row, own_lanes, split_lane):
    gy, gz = lax.axis_index("gy"), lax.axis_index("gz")
    last_y, last_z = lax.axis_size("gy") - 1, lax.axis_size("gz") - 1
    row, lane = rows_of(shape), lanes_of(shape)
    up_y, down_y = (gy < last_y).astype(jnp.int32), (gy > 0).astype(jnp.int32)
    up_z, down_z = (gz < last_z).astype(jnp.int32), (gz > 0).astype(jnp.int32)
    in_y = jnp.where(row < own_rows, 1, jnp.where(row < split_row, up_y, down_y))
    in_z = jnp.where(lane < own_lanes, 1, jnp.where(lane < split_lane, up_z, down_z))
    return (in_y * in_z) > 0


def pick(value, lane):
    return jnp.take_along_axis(value, lane, axis=1, mode="promise_in_bounds")


def pairs_of_lanes(value):
    lane = lanes_of(value.shape)
    return pick(value + turn(value, -1, 1), 2 * lane - jnp.where(lane < 64, 0, 128))


def call(body, limit, outs, scratch, *args, micros=1.0):
    vmem = pl.BlockSpec(memory_space=pltpu.VMEM)
    return pl.pallas_call(
        body,
        out_shape=[jax.ShapeDtypeStruct(s, F32) for s in outs],
        in_specs=[vmem] * len(args),
        out_specs=[vmem] * len(outs),
        scratch_shapes=[pltpu.VMEM(s, F32) for s in scratch],
        compiler_params=pltpu.CompilerParams(vmem_limit_bytes=limit * MIB),
        cost_estimate=pl.CostEstimate(flops=0, bytes_accessed=int(micros * 3690000), transcendentals=0),
    )(*args)


def ring(value, axis, shift):
    size = lax.axis_size(axis)
    return lax.ppermute(value, axis, [(i, (i + shift) % size) for i in range(size)])


def plane_of(own, low, high, which, x):
    if x < XH:
        return low.at[which * XH + x]
    if x < XH + NX0:
        return own[which].at[x - XH]
    return high.at[which * XH + x - XH - NX0]


def pack_y(s, c, high, low, up, down):
    for a in range(2):
        for x in range(NXE):
            src = plane_of((s, c), low, high, a, x)
            at = a * NXE + x
            up[at * 8 : at * 8 + 8, :] = src[56:64, :]
            down[at * 8 : at * 8 + 8, :] = src[0:8, :]
            up[224 + at : 225 + at, :] = src[55:56, :]
            down[224 + at : 225 + at, :] = src[8:9, :]
    up[252:256, :] = jnp.zeros((4, 128), F32)
    down[252:256, :] = jnp.zeros((4, 128), F32)


def pack_wide(up, down, row, count, plane):
    lane = lanes_of((count, 128))
    for a in range(2):
        ups = jnp.zeros((count, 128), F32)
        downs = jnp.zeros((count, 128), F32)
        for x in range(NXE):
            v = plane(a, x)
            here = (lane >= W * x) & (lane < W * x + W)
            ups = jnp.where(here, turn(v, W * x - (128 - W), 1), ups)
            downs = jnp.where(here, turn(v, W * x, 1), downs)
        up[a, row : row + count, :] = ups
        down[a, row : row + count, :] = downs


def halo_rows(below, above, a, x):
    at = a * NXE + x
    row = rows_of((8, 128))
    middle = jnp.where(row == 0, above[224 + at : 225 + at, :], 0.0)
    middle = jnp.where(row == 7, below[224 + at : 225 + at, :], middle)
    return jnp.concatenate([above[at * 8 : at * 8 + 8, :], middle, below[at * 8 : at * 8 + 8, :]], 0)


def pack_z_own(s, c, high, low, up, down):
    pack_wide(up, down, 0, 64, lambda a, x: plane_of((s, c), low, high, a, x)[...])


def pack_z_halo(own_up, own_down, below, above, up, down):
    up[:, 0:64, :] = own_up[...]
    down[:, 0:64, :] = own_down[...]
    pack_wide(up, down, 64, 24, lambda a, x: halo_rows(below, above, a, x))


def fine_sweep(src, dst, res, diag, inverse, first, stop, pair, also):
    def body(x, carry):
        d = src[x]
        near = beside(d) + (src[x - 1] + src[x + 1])
        r = res[x] - (diag[x] * d - near)
        res[x] = r
        also(x, d)
        if pair is not None:
            dst[x] = pair[0] * d + (pair[1] * inverse[x]) * r
        return carry

    lax.fori_loop(first, stop, body, 0, unroll=True)


def to_q0(ref, x):
    tail = jnp.where(rows_of((8, 256)) < 4, ref[x, 64:72, :], ref[x, 80:88, :])
    return ref[x, 0:64, :], tail


def fine_before(
    s, c, high, low, below_y, above_y, below, above, sol, res, diag, inv, msg, da, db, rows
):
    lane = lanes_of((R0, 128))
    for a in range(2):
        left, right = below[a], above[a]
        for x in range(NXE):
            side = jnp.where(lane < W, turn(right, -W * x, 1), 0.0)
            side = jnp.where(lane >= 128 - W, turn(left, 128 - W - W * x, 1), side)
            ref = (res, diag)[a]
            ref[x, 0:64, 0:128] = plane_of((s, c), low, high, a, x)[...]
            ref[x, 64:88, 0:128] = halo_rows(below_y, above_y, a, x)
            ref[x, :, 128:256] = side
    lane40 = lanes_of((R1, 128))

    def fold(ref, i, at):
        both = ref[XH + 2 * i] + ref[XH + 2 * i + 1]
        sides = []
        for side in range(2):
            part = both[:, 128 * side : 128 * side + 128]
            rows[at, side, 0:72, :] = part[0:72]
            rows[at, side, 72:80, :] = part[80:88]
            sides.append(rows.at[at, side][pl.ds(0, R1, stride=2), :] + rows.at[at, side][pl.ds(1, R1, stride=2), :])
        return 0.125 * jnp.where(lane40 < 64, pairs_of_lanes(sides[0]), pairs_of_lanes(sides[1]))

    coef1 = [fold(diag, i, i) for i in range(4)]

    gx = lax.axis_index("gx")
    in_yz = inside_yz((R0, 256), 64, 76, 128, 192)
    low_x, high_x = gx > 0, gx < lax.axis_size("gx") - 1

    def start(x, carry):
        g = diag[x] + 6.0
        diag[x] = g
        here = ((x >= XH) | low_x) & ((x < XH + NX0) | high_x)
        inverse = jnp.where(in_yz & here, 1.0 / g, 0.0)
        inv[x] = inverse
        da[x] = res[x] * inverse * (1.0 / THETA)
        return carry

    lax.fori_loop(0, NXE, start, 0, unroll=True)

    pairs = coefficients(SWEEPS)
    buffers = (da, db)
    for k in range(SWEEPS):
        src, dst = buffers[k % 2], buffers[(k + 1) % 2]
        last = k == SWEEPS - 1

        def nothing(x, d):
            return None

        fine_sweep(src, dst, res, diag, inv, k + 1, NXE - 1 - k, None if last else pairs[k], nothing)

        def gather(x, carry):
            own = src[XH + x, 0:64, 0:128]
            sol[x] = own if k == 0 else sol[x] + own
            return carry

        lax.fori_loop(0, NX0, gather, 0, unroll=True)

    halo = jnp.zeros((R1, 128), F32)
    for i in range(4):
        r1, c1 = fold(res, i, 4 + i), coef1[i]
        both = jnp.where(lane40 < 64, r1, turn(c1, 64, 1))
        msg[i * R1 : i * R1 + R1, :] = both
        for a, v in ((0, r1), (1, c1)):
            base = (a * 4 + i) * 8
            halo = jnp.where((lane40 >= base) & (lane40 < base + 4), turn(v, base - 64, 1), halo)
            halo = jnp.where((lane40 >= base + 4) & (lane40 < base + 8), turn(v, base + 4 - 124, 1), halo)
    msg[160:200, :] = halo


def line_sweep(src, dst, res, diag, inverse, planes, scale, pair, sol, ahead=0):
    def body(x, carry):
        d = src[x + 1]
        near = beside(d) + (src[x] + src[x + 2])
        r = res[x] - (diag[x] * d - scale * near)
        res[x] = r
        if pair is not None:
            step = pair[0] * d + (pair[1] * inverse[x]) * r
            dst[x + 1] = step
            sol[x + ahead] += step
        return carry

    lax.fori_loop(0, planes, body, 0, unroll=True)


def middle_before(own, low, high, far, res, sol, coef, low_res, low_coef, up, down, diag, inv, da, db, rows):
    gx = lax.axis_index("gx")
    size = lax.axis_size("gx")
    lane40 = lanes_of((R1, 128))
    for msg, shift in ((own, 0), (low, 3), (high, 1), (far, 2)):
        place = lax.rem(gx + shift, size) * 4
        side = msg[160:200, :]
        for i in range(4):
            both = msg[i * R1 : i * R1 + R1, :]
            for a, ref in ((0, res), (1, coef)):
                base = (a * 4 + i) * 8
                v = both if a == 0 else turn(both, 64, 1)
                v = jnp.where(lane40 < 64, v, turn(side, 64 - base, 1))
                v = jnp.where(lane40 < 68, v, 0.0)
                v = jnp.where(lane40 < 124, v, turn(side, 124 - base - 4, 1))
                ref[place + i] = v
    in_yz = inside_yz((R1, 128), 32, 36, 64, 96)
    empty = jnp.zeros((R1, 128), F32)
    for buffer in (da, db):
        buffer[0] = empty
        buffer[17] = empty

    def start(x, carry):
        g = coef[x] + 1.5
        diag[x] = g
        inverse = jnp.where(in_yz, 1.0 / g, 0.0)
        inv[x] = inverse
        d = res[x] * inverse * (1.0 / THETA)
        da[x + 1] = d
        sol[x] = d
        return carry

    lax.fori_loop(0, 16, start, 0, unroll=True)
    pairs = coefficients(SWEEPS)
    buffers = (da, db)
    for k in range(SWEEPS):
        src, dst = buffers[k % 2], buffers[(k + 1) % 2]
        line_sweep(src, dst, res, diag, inv, 16, 0.25, pairs[k] if k < SWEEPS - 1 else None, sol)
    lane8, row8 = lanes_of((8, 128)), rows_of((8, 128))

    def fold(ref, i, at):
        rows[at] = ref[2 * i, 0:32, :] + ref[2 * i + 1, 0:32, :]
        part = rows.at[at]
        return 0.125 * pairs_of_lanes(part[pl.ds(0, 16, stride=2), :] + part[pl.ds(1, 16, stride=2), :])

    lows = []
    for i in range(8):
        r2, c2 = fold(res, i, i), fold(coef, i, 8 + i)
        low_res[i] = r2
        low_coef[i] = c2
        lows.append(jnp.where(lanes_of((16, 128)) < 32, r2, turn(c2, 32, 1)))
    for i in range(4):
        both = jnp.where(lanes_of((16, 128)) < 64, lows[i], turn(lows[i + 4], 64, 1))
        up[i * 8 : i * 8 + 8, :] = both[8:16]
        down[i * 8 : i * 8 + 8, :] = both[0:8]
    for i in range(8):
        at = 32 + i * 8
        tiles = []
        for first in (24, 0):
            a, b = [
                jnp.where(lane8 < 64, res[x, first : first + 8, :], turn(sol[x, first : first + 8, :], 64, 1))
                for x in (2 * i, 2 * i + 1)
            ]
            tiles.append((a, b))
        up[at : at + 8, :] = jnp.where(row8 < 4, turn(tiles[0][0], 4, 0), tiles[0][1])
        down[at : at + 8, :] = jnp.where(row8 < 4, tiles[1][0], turn(tiles[1][1], 4, 0))


def low_halo(msg, i, which):
    tile = msg[(i % 4) * 8 : (i % 4) * 8 + 8, :]
    return turn(tile, -(64 * (i // 4) + 32 * which), 1)


def middle_halo(msg, x, which, below):
    tile = msg[32 + (x // 2) * 8 : 40 + (x // 2) * 8, :]
    tile = turn(tile, 64, 1) if which else tile
    return turn(tile, 4, 0) if (x % 2 == 0) == below else tile


def pack_lanes(up, down, row, count, planes, width, base, top):
    lane = lanes_of((count, 128))
    ups, downs = up[row : row + count, :], down[row : row + count, :]
    for i, v in enumerate(planes):
        at = base + width * i
        here = (lane >= at) & (lane < at + width)
        ups = jnp.where(here, turn(v, at - (top - width), 1), ups)
        downs = jnp.where(here, turn(v, at, 1), downs)
    up[row : row + count, :] = ups
    down[row : row + count, :] = downs


def pack_low_own(low_res, low_coef, res, sol, up, down):
    up[...] = jnp.zeros((48, 128), F32)
    down[...] = jnp.zeros((48, 128), F32)
    pack_lanes(up, down, 0, 16, [low_res[i] for i in range(8)], 8, 0, 32)
    pack_lanes(up, down, 0, 16, [low_coef[i] for i in range(8)], 8, 64, 32)
    pack_lanes(up, down, 16, 32, [res[x, 0:32, :] for x in range(16)], 4, 0, 64)
    pack_lanes(up, down, 16, 32, [sol[x, 0:32, :] for x in range(16)], 2, 64, 64)


def keep_fine(after, res0, diag0, inv0, res_q, diag_q, inv_q, r0_up, r0_down):
    for ref, kept, skip in ((res0, res_q, XH), (diag0, diag_q, 0), (inv0, inv_q, 0)):
        for x in range(kept.shape[0]):
            top, tail = to_q0(ref, x + skip)
            kept[x, 0:64, :] = top
            kept[x, 64:72, :] = tail
    lane = lanes_of((Q0, 128))
    for msg, first in ((r0_up, NX0 - XH), (r0_down, 0)):
        side = jnp.zeros((Q0, 128), F32)
        for i in range(XH):
            msg[i * Q0 : i * Q0 + Q0, :] = res_q[first + i, :, 0:128]
            v = res_q[first + i, :, 128:256]
            base = 6 * i
            side = jnp.where((lane >= base) & (lane < base + 3), turn(v, base, 1), side)
            side = jnp.where((lane >= base + 3) & (lane < base + 6), turn(v, base + 3 - 125, 1), side)
        msg[XH * Q0 : XH * Q0 + Q0, :] = side


def pack_low_halo(own_up, own_down, above, below, up, down):
    for msg, own in ((up, own_up), (down, own_down)):
        msg[0:16, :] = own[0:16, :]
        msg[16:32, :] = jnp.zeros((16, 128), F32)
        msg[32:64, :] = own[16:48, :]
        msg[64:80, :] = jnp.zeros((16, 128), F32)
    for at, src, is_below in ((0, above, False), (8, below, True)):
        pack_lanes(up, down, 16 + at, 8, [low_halo(src, i, 0) for i in range(8)], 8, 0, 32)
        pack_lanes(up, down, 16 + at, 8, [low_halo(src, i, 1) for i in range(8)], 8, 64, 32)
        pack_lanes(up, down, 64 + at, 8, [middle_halo(src, x, 0, is_below) for x in range(16)], 4, 0, 64)
        pack_lanes(up, down, 64 + at, 8, [middle_halo(src, x, 1, is_below) for x in range(16)], 2, 64, 64)


def with_sides(own, left, right, base, width, own_lanes):
    lane = lanes_of(own.shape)
    v = jnp.where(lane < own_lanes, own, turn(right, own_lanes - base, 1))
    v = jnp.where(lane < own_lanes + width, v, 0.0)
    return jnp.where(lane < 128 - width, v, turn(left, 128 - width - base, 1))


def bottom(low_res, low_coef, above, below, left, right, sol2, res2, diag2, inv2, da2, db2):
    in_yz = inside_yz((R2, 128), 16, 24, 32, 64)
    empty = jnp.zeros((R2, 128), F32)
    for buffer in (da2, db2):
        buffer[0] = empty
        buffer[9] = empty
    from_left, from_right = left[0:R2, :], right[0:R2, :]
    for i in range(8):
        parts = []
        for a, ref in ((0, low_res), (1, low_coef)):
            own = jnp.concatenate([ref[i], low_halo(above, i, a), low_halo(below, i, a)], 0)
            parts.append(with_sides(own, from_left, from_right, a * 64 + i * 8, 8, 32))
        g = parts[1] + 0.375
        inverse = jnp.where(in_yz, 1.0 / g, 0.0)
        res2[i] = parts[0]
        diag2[i] = g
        inv2[i] = inverse
        d = parts[0] * inverse * (1.0 / THETA)
        da2[i + 1] = d
        sol2[i] = d
    pairs = coefficients(COARSE_SWEEPS)
    buffers = (da2, db2)
    for k in range(COARSE_SWEEPS - 1):
        src, dst = buffers[k % 2], buffers[(k + 1) % 2]
        line_sweep(src, dst, res2, diag2, inv2, 8, 0.0625, pairs[k], sol2)


def middle_after(
    sol2, res, sol, coef1, above, below, left, right, sol1, res1, diag1, inv1, da1, db1
):
    in_yz1 = inside_yz((Q1, 128), 32, 40, 64, 96)
    empty = jnp.zeros((Q1, 128), F32)
    for buffer in (da1, db1):
        buffer[0] = empty
        buffer[17] = empty
    for x in (0, 1, 18, 19):
        sol1[x] = empty
    from_left, from_right = left[R2 : R2 + Q1, :], right[R2 : R2 + Q1, :]
    lane = lanes_of((24, 128))
    half = lane // 2 + jnp.where(lane >= 96, 64, 0)
    first = rows_of((8, 128)) < 4
    for i in range(8):
        tail = jnp.where(first, sol2[i, 16:24, :], sol2[i, 24:32, :])
        lifted = pick(jnp.concatenate([sol2[i, 0:16, :], tail], 0), half)
        for x in (2 * i, 2 * i + 1):
            db1.at[x + 1][pl.ds(0, 24, stride=2), :] = lifted
            db1.at[x + 1][pl.ds(1, 24, stride=2), :] = lifted
            parts = []
            for a, ref in ((0, res), (1, sol)):
                own = jnp.concatenate(
                    [ref[x, 0:32, :], middle_halo(above, x, a, False), middle_halo(below, x, a, True)], 0
                )
                width = (4, 2)[a]
                parts.append(with_sides(own, from_left, from_right, a * 64 + width * x, width, 64))
            res1[x] = parts[0]
            sol1[x + 2] = jnp.where(in_yz1, parts[1], 0.0)

    def correct1(x, carry):
        g = jnp.concatenate([coef1[x], coef1[x, 32:40, :]], 0) + 1.5
        inverse = jnp.where(in_yz1, 1.0 / g, 0.0)
        diag1[x] = g
        inv1[x] = inverse
        p = db1[x + 1]
        near = beside(p) + (db1[x] + db1[x + 2])
        r = res1[x] - (g * p - 0.25 * near)
        res1[x] = r
        d = r * inverse * (1.0 / THETA)
        da1[x + 1] = d
        sol1[x + 2] += p + d
        return carry

    lax.fori_loop(0, 16, correct1, 0, unroll=True)
    pairs = coefficients(SWEEPS)
    buffers = (da1, db1)
    for k in range(SWEEPS - 1):
        src, dst = buffers[k % 2], buffers[(k + 1) % 2]
        line_sweep(src, dst, res1, diag1, inv1, 16, 0.25, pairs[k], sol1, 2)


def fine_after(
    sol1, sol0, res_q, diag_q, inv_q, low, high, out_sol, out_res, p0, res0, da0, db0
):
    gx = lax.axis_index("gx")
    half = lanes_of((R1, 128)) // 2
    first2 = rows_of((8, 128)) < 2
    for i in range(8):
        v = sol1[gx * 4 + i]
        v = jnp.concatenate([v[0:32], jnp.where(first2, v[32:40], turn(v[40:48], 4, 0))], 0)
        for side in range(2):
            lifted = pick(v, half + 64 * side)
            for x in (2 * i, 2 * i + 1):
                p0.at[x, side][pl.ds(0, R1, stride=2), :] = lifted
                p0.at[x, side][pl.ds(1, R1, stride=2), :] = lifted

    def lift(x):
        return jnp.concatenate([p0[x, 0, 0:Q0, :], p0[x, 1, 0:Q0, :]], 1)

    lane72 = lanes_of((Q0, 128))
    for msg, first in ((low, 0), (high, XH + NX0)):
        side = msg[XH * Q0 : XH * Q0 + Q0, :]
        for i in range(XH):
            base = 6 * i
            v = jnp.where(lane72 < 3, turn(side, -base, 1), 0.0)
            v = jnp.where(lane72 < 125, v, turn(side, 125 - base - 3, 1))
            res0[first + i, :, 0:128] = msg[i * Q0 : i * Q0 + Q0, :]
            res0[first + i, :, 128:256] = v

    def fetch(x, carry):
        res0[x + XH] = res_q[x]
        return carry

    lax.fori_loop(0, NX0, fetch, 0, unroll=True)

    def correct0(x, carry):
        p = lift(x + 1)
        near = beside(p) + (lift(x) + lift(x + 2))
        r = res0[x] - (diag_q[x] * p - near)
        res0[x] = r
        da0[x] = r * inv_q[x] * (1.0 / THETA)
        return carry

    lax.fori_loop(0, NXE, correct0, 0, unroll=True)

    def begin(x, carry):
        out_sol[x] = sol0[x] + p0[x + XH + 1, 0, 0:64, :]
        return carry

    lax.fori_loop(0, NX0, begin, 0, unroll=True)
    pairs = coefficients(SWEEPS)
    buffers = (da0, db0)
    for k in range(SWEEPS):
        src, dst = buffers[k % 2], buffers[(k + 1) % 2]

        def gather0(x, carry):
            out_sol[x] += src[x + XH, 0:64, 0:128]
            return carry

        lax.fori_loop(0, NX0, gather0, 0, unroll=True)
        fine_sweep(
            src, dst, res0, diag_q, inv_q, k + 1, NXE - 1 - k, pairs[k] if k < SWEEPS - 1 else None,
            lambda x, d: None,
        )

    def put(x, carry):
        out_res[x] = res0[x + XH, 0:64, 0:128]
        return carry

    lax.fori_loop(0, NX0, put, 0, unroll=True)


def per_device(s, c):
    up = jnp.concatenate([s[NX0 - XH :], c[NX0 - XH :]], 0)
    down = jnp.concatenate([s[:XH], c[:XH]], 0)
    low, high = ring(up, "gx", 1), ring(down, "gx", -1)
    up, down = call(pack_y, 4, [(256, 128)] * 2, [], s, c, high, low)
    below_y, above_y = ring(up, "gy", 1), ring(down, "gy", -1)
    own_up, own_down = call(pack_z_own, 4, [(2, 64, 128)] * 2, [], s, c, high, low)
    up, down = call(pack_z_halo, 4, [(2, R0, 128)] * 2, [], own_up, own_down, below_y, above_y)
    below, above = ring(up, "gz", 1), ring(down, "gz", -1)
    big = (NXE, R0, 256)
    sol0, res0, diag0, inv0, msg = call(
        fine_before,
        16,
        [(NX0, 64, 128), big, big, big, (200, 128)],
        [big, big, (8, 2, 80, 128)],
        s, c, high, low, below_y, above_y, below, above,
        micros=4.0,
    )
    low, high, far = ring(msg, "gx", 1), ring(msg, "gx", -1), ring(msg, "gx", 2)
    big = (NXE, Q0, 256)
    res_q, diag_q, inv_q, r0_up, r0_down = call(
        keep_fine,
        8,
        [(NX0, Q0, 256), big, big, (4 * Q0, 128), (4 * Q0, 128)],
        [],
        low, res0, diag0, inv0,
        micros=2.0,
    )
    r0_low, r0_high = ring(r0_up, "gx", 1), ring(r0_down, "gx", -1)
    mid = (16, R1, 128)
    res1, sol1, coef1, res2, coef2, up, down = call(
        middle_before,
        8,
        [mid, mid, mid, (8, 16, 128), (8, 16, 128), (96, 128), (96, 128)],
        [mid, mid, (18, R1, 128), (18, R1, 128), (16, 32, 128)],
        msg, low, high, far,
        micros=2.0,
    )
    below, above = ring(up, "gy", 1), ring(down, "gy", -1)
    own_up, own_down = call(pack_low_own, 4, [(48, 128)] * 2, [], res2, coef2, res1, sol1, micros=2.0)
    up, down = call(pack_low_halo, 4, [(R2 + Q1, 128)] * 2, [], own_up, own_down, above, below)
    left, right = ring(up, "gz", 1), ring(down, "gz", -1)
    bot, mid = (8, R2, 128), (16, Q1, 128)
    big = (NXE, Q0, 256)
    own = (NX0, NY0, NZ0)
    (sol2,) = call(
        bottom, 4, [bot], [bot] * 3 + [(10, R2, 128)] * 2, res2, coef2, above, below, left, right
    )
    (sol1,) = call(
        middle_after,
        8,
        [(20, Q1, 128)],
        [mid] * 3 + [(18, Q1, 128)] * 2,
        sol2, res1, sol1, coef1, above, below, left, right,
        micros=2.0,
    )
    return tuple(
        call(
            fine_after,
            16,
            [own, own],
            [(16, 2, 80, 128)] + [big] * 3,
            sol1, sol0, res_q, diag_q, inv_q, r0_low, r0_high,
        )
    )


def solution(mesh):
    return jax.shard_map(
        per_device,
        mesh=mesh,
        in_specs=(P("gx", "gy", "gz"), P("gx", "gy", "gz")),
        out_specs=(P("gx", "gy", "gz"), P("gx", "gy", "gz")),
        check_vma=False,
    )
```

```python
import jax
import jax.numpy as jnp
from jax import lax
from jax.experimental import pallas as pl
from jax.experimental.pallas import tpu as pltpu
from jax.sharding import PartitionSpec as P

SWEEPS = 3
COARSE_SWEEPS = 6
THETA = 1.25
DELTA = 0.75
F32 = jnp.float32

XH = 3
NX0, NY0, NZ0 = 8, 64, 128
NXE = NX0 + 2 * XH
W = 9
R0 = 88
Q0 = 72
R1 = 40
Q1 = 48
R2 = 32
MIB = 1024 * 1024


def coefficients(count):
    sigma = THETA / DELTA
    rho = 1.0 / sigma
    pairs = []
    for _ in range(count):
        rho_new = 1.0 / (2.0 * sigma - rho)
        pairs.append((rho_new * rho, 2.0 * rho_new / DELTA))
        rho = rho_new
    return pairs


def turn(value, shift, axis):
    return pltpu.roll(value, shift % value.shape[axis], axis)


def beside(value):
    return (turn(value, 1, 0) + turn(value, -1, 0)) + (turn(value, 1, 1) + turn(value, -1, 1))


def rows_of(shape):
    return lax.broadcasted_iota(jnp.int32, shape, 0)


def lanes_of(shape):
    return lax.broadcasted_iota(jnp.int32, shape, 1)


def inside_yz(shape, own_rows, split_row, own_lanes, split_lane):
    gy, gz = lax.axis_index("gy"), lax.axis_index("gz")
    last_y, last_z = lax.axis_size("gy") - 1, lax.axis_size("gz") - 1
    row, lane = rows_of(shape), lanes_of(shape)
    up_y, down_y = (gy < last_y).astype(jnp.int32), (gy > 0).astype(jnp.int32)
    up_z, down_z = (gz < last_z).astype(jnp.int32), (gz > 0).astype(jnp.int32)
    in_y = jnp.where(row < own_rows, 1, jnp.where(row < split_row, up_y, down_y))
    in_z = jnp.where(lane < own_lanes, 1, jnp.where(lane < split_lane, up_z, down_z))
    return (in_y * in_z) > 0


def pick(value, lane):
    return jnp.take_along_axis(value, lane, axis=1, mode="promise_in_bounds")


def pairs_of_lanes(value):
    lane = lanes_of(value.shape)
    return pick(value + turn(value, -1, 1), 2 * lane - jnp.where(lane < 64, 0, 128))


def call(body, limit, outs, scratch, *args, micros=1.0):
    vmem = pl.BlockSpec(memory_space=pltpu.VMEM)
    return pl.pallas_call(
        body,
        out_shape=[jax.ShapeDtypeStruct(s, F32) for s in outs],
        in_specs=[vmem] * len(args),
        out_specs=[vmem] * len(outs),
        scratch_shapes=[pltpu.VMEM(s, F32) for s in scratch],
        compiler_params=pltpu.CompilerParams(vmem_limit_bytes=limit * MIB),
        cost_estimate=pl.CostEstimate(flops=0, bytes_accessed=int(micros * 3690000), transcendentals=0),
    )(*args)


def ring(value, axis, shift):
    size = lax.axis_size(axis)
    return lax.ppermute(value, axis, [(i, (i + shift) % size) for i in range(size)])


SLABS = [(0, x) for x in range(NXE)] + [(1, x) for x in range(1, NXE - 1)]
SLAB = {slab: at for at, slab in enumerate(SLABS)}
YROWS = 240


def plane_of(own, low, high, which, x):
    if x < XH:
        return low.at[x if which == 0 else XH + x - 1]
    if x < XH + NX0:
        return own[which].at[x - XH]
    return high.at[x - XH - NX0 + (0 if which == 0 else XH)]


def pack_x(s, c, up, down, work, done):
    copies = []

    def fetch(src, dst):
        copies.append(pltpu.make_async_copy(src, dst, done.at[len(copies)]))
        copies[-1].start()

    fetch(s.at[pl.ds(NX0 - XH, XH)], up.at[pl.ds(0, XH)])
    fetch(c.at[pl.ds(NX0 - XH, 1)], work.at[pl.ds(0, 1)])
    fetch(s.at[pl.ds(0, XH)], down.at[pl.ds(0, XH)])
    fetch(c.at[pl.ds(XH - 1, 1)], work.at[pl.ds(1, 1)])
    fetch(c.at[pl.ds(NX0 - XH + 1, XH - 1)], up.at[pl.ds(XH, XH - 1)])
    fetch(c.at[pl.ds(0, XH - 1)], down.at[pl.ds(XH, XH - 1)])
    for copy in copies:
        copy.wait()
    up[0] = up[0] * (1.0 / (work[0] + 6.0)) * (1.0 / THETA)
    down[XH - 1] = down[XH - 1] * (1.0 / (work[1] + 6.0)) * (1.0 / THETA)


def fetch_own(after, s, c, s_out, c_out, done):
    copies = [pltpu.make_async_copy(s, s_out, done.at[0]), pltpu.make_async_copy(c, c_out, done.at[1])]
    for copy in copies:
        copy.start()
    for copy in copies:
        copy.wait()


def pack_y(s, c, high, low, up, down):
    for (a, x), at in SLAB.items():
        src = plane_of((s, c), low, high, a, x)
        up[at * 8 : at * 8 + 8, :] = src[56:64, :]
        down[at * 8 : at * 8 + 8, :] = src[0:8, :]
        up[208 + at : 209 + at, :] = src[55:56, :]
        down[208 + at : 209 + at, :] = src[8:9, :]
    up[234:YROWS, :] = jnp.zeros((YROWS - 234, 128), F32)
    down[234:YROWS, :] = jnp.zeros((YROWS - 234, 128), F32)


def pack_wide(up, down, row, count, plane):
    lane = lanes_of((count, 128))
    for a in range(2):
        ups = jnp.zeros((count, 128), F32)
        downs = jnp.zeros((count, 128), F32)
        for x in range(a, NXE - a):
            v = plane(a, x)
            here = (lane >= W * x) & (lane < W * x + W)
            ups = jnp.where(here, turn(v, W * x - (128 - W), 1), ups)
            downs = jnp.where(here, turn(v, W * x, 1), downs)
        up[a, row : row + count, :] = ups
        down[a, row : row + count, :] = downs


def halo_rows(below, above, a, x):
    at = SLAB[a, x]
    row = rows_of((8, 128))
    middle = jnp.where(row == 0, above[208 + at : 209 + at, :], 0.0)
    middle = jnp.where(row == 7, below[208 + at : 209 + at, :], middle)
    return jnp.concatenate([above[at * 8 : at * 8 + 8, :], middle, below[at * 8 : at * 8 + 8, :]], 0)


def pack_z_own(s, c, high, low, up, down):
    pack_wide(up, down, 0, 64, lambda a, x: plane_of((s, c), low, high, a, x)[...])


def pack_z_halo(own_up, own_down, below, above, up, down):
    up[:, 0:64, :] = own_up[...]
    down[:, 0:64, :] = own_down[...]
    pack_wide(up, down, 64, 24, lambda a, x: halo_rows(below, above, a, x))


def fine_sweep(src, dst, res, diag, inverse, first, stop, pair):
    for x in range(first, stop):
        d = src[x]
        near = beside(d) + (src[x - 1] + src[x + 1])
        r = res[x] - (diag[x] * d - near)
        res[x] = r
        if pair is not None:
            dst[x] = pair[0] * d + (pair[1] * inverse[x]) * r


def to_q0(ref, x):
    tail = jnp.where(rows_of((8, 256)) < 4, ref[x, 64:72, :], ref[x, 80:88, :])
    return ref[x, 0:64, :], tail


def fine_before(
    s, c, high, low, below_y, above_y, below, above, sol, res, diag, inv, msg, da, db, dc, rows
):
    lane = lanes_of((R0, 128))
    for a in range(2):
        left, right = below[a], above[a]
        for x in range(a, NXE - a):
            side = jnp.where(lane < W, turn(right, -W * x, 1), 0.0)
            side = jnp.where(lane >= 128 - W, turn(left, 128 - W - W * x, 1), side)
            ref = (res, diag)[a]
            ref[x, 0:64, 0:128] = plane_of((s, c), low, high, a, x)[...]
            ref[x, 64:88, 0:128] = halo_rows(below_y, above_y, a, x)
            ref[x, :, 128:256] = side
    lane40 = lanes_of((R1, 128))

    def fold(ref, i, at):
        both = ref[XH + 2 * i] + ref[XH + 2 * i + 1]
        sides = []
        for side in range(2):
            part = both[:, 128 * side : 128 * side + 128]
            rows[at, side, 0:72, :] = part[0:72]
            rows[at, side, 72:80, :] = part[80:88]
            sides.append(rows.at[at, side][pl.ds(0, R1, stride=2), :] + rows.at[at, side][pl.ds(1, R1, stride=2), :])
        return 0.125 * jnp.where(lane40 < 64, pairs_of_lanes(sides[0]), pairs_of_lanes(sides[1]))

    coef1 = [fold(diag, i, i) for i in range(4)]

    gx = lax.axis_index("gx")
    in_yz = inside_yz((R0, 256), 64, 76, 128, 192)
    low_x, high_x = gx > 0, gx < lax.axis_size("gx") - 1

    for x in range(NXE):
        here = in_yz & (low_x if x < XH else high_x) if x < XH or x >= XH + NX0 else in_yz
        if x in (0, NXE - 1):
            da[x] = jnp.where(here, res[x], 0.0)
            continue
        g = diag[x] + 6.0
        diag[x] = g
        inverse = jnp.where(here, 1.0 / g, 0.0)
        inv[x] = inverse
        da[x] = res[x] * inverse * (1.0 / THETA)
    pairs = coefficients(SWEEPS)
    steps = (da, db, dc)
    for k in range(SWEEPS):
        last = k == SWEEPS - 1
        fine_sweep(
            steps[k], None if last else steps[k + 1], res, diag, inv, k + 1, NXE - 1 - k, None if last else pairs[k]
        )
    for x in range(NX0):
        sol[x] = sum(d[XH + x, 0:64, 0:128] for d in steps)

    halo = jnp.zeros((R1, 128), F32)
    for i in range(4):
        r1, c1 = fold(res, i, 4 + i), coef1[i]
        both = jnp.where(lane40 < 64, r1, turn(c1, 64, 1))
        msg[i * R1 : i * R1 + R1, :] = both
        for a, v in ((0, r1), (1, c1)):
            base = (a * 4 + i) * 8
            halo = jnp.where((lane40 >= base) & (lane40 < base + 4), turn(v, base - 64, 1), halo)
            halo = jnp.where((lane40 >= base + 4) & (lane40 < base + 8), turn(v, base + 4 - 124, 1), halo)
    msg[160:200, :] = halo


def line_sweep(src, dst, res, diag, inverse, planes, scale, pair, sol, ahead=0):
    def body(x, carry):
        d = src[x + 1]
        near = beside(d) + (src[x] + src[x + 2])
        r = res[x] - (diag[x] * d - scale * near)
        res[x] = r
        if pair is not None:
            step = pair[0] * d + (pair[1] * inverse[x]) * r
            dst[x + 1] = step
            sol[x + ahead] += step
        return carry

    lax.fori_loop(0, planes, body, 0, unroll=True)


def middle_before(own, low, high, far, res, sol, coef, low_res, low_coef, up, down, diag, inv, da, db, rows):
    gx = lax.axis_index("gx")
    size = lax.axis_size("gx")
    lane40 = lanes_of((R1, 128))
    for msg, shift in ((own, 0), (low, 3), (high, 1), (far, 2)):
        place = lax.rem(gx + shift, size) * 4
        side = msg[160:200, :]
        for i in range(4):
            both = msg[i * R1 : i * R1 + R1, :]
            for a, ref in ((0, res), (1, coef)):
                base = (a * 4 + i) * 8
                v = both if a == 0 else turn(both, 64, 1)
                v = jnp.where(lane40 < 64, v, turn(side, 64 - base, 1))
                v = jnp.where(lane40 < 68, v, 0.0)
                v = jnp.where(lane40 < 124, v, turn(side, 124 - base - 4, 1))
                ref[place + i] = v
    in_yz = inside_yz((R1, 128), 32, 36, 64, 96)
    empty = jnp.zeros((R1, 128), F32)
    for buffer in (da, db):
        buffer[0] = empty
        buffer[17] = empty

    def start(x, carry):
        g = coef[x] + 1.5
        diag[x] = g
        inverse = jnp.where(in_yz, 1.0 / g, 0.0)
        inv[x] = inverse
        d = res[x] * inverse * (1.0 / THETA)
        da[x + 1] = d
        sol[x] = d
        return carry

    lax.fori_loop(0, 16, start, 0, unroll=True)
    pairs = coefficients(SWEEPS)
    buffers = (da, db)
    for k in range(SWEEPS):
        src, dst = buffers[k % 2], buffers[(k + 1) % 2]
        line_sweep(src, dst, res, diag, inv, 16, 0.25, pairs[k] if k < SWEEPS - 1 else None, sol)
    lane8, row8 = lanes_of((8, 128)), rows_of((8, 128))

    def fold(ref, i, at):
        rows[at] = ref[2 * i, 0:32, :] + ref[2 * i + 1, 0:32, :]
        part = rows.at[at]
        return 0.125 * pairs_of_lanes(part[pl.ds(0, 16, stride=2), :] + part[pl.ds(1, 16, stride=2), :])

    lows = []
    for i in range(8):
        r2, c2 = fold(res, i, i), fold(coef, i, 8 + i)
        low_res[i] = r2
        low_coef[i] = c2
        lows.append(jnp.where(lanes_of((16, 128)) < 32, r2, turn(c2, 32, 1)))
    for i in range(4):
        both = jnp.where(lanes_of((16, 128)) < 64, lows[i], turn(lows[i + 4], 64, 1))
        up[i * 8 : i * 8 + 8, :] = both[8:16]
        down[i * 8 : i * 8 + 8, :] = both[0:8]
    for i in range(8):
        at = 32 + i * 8
        tiles = []
        for first in (24, 0):
            a, b = [
                jnp.where(lane8 < 64, res[x, first : first + 8, :], turn(sol[x, first : first + 8, :], 64, 1))
                for x in (2 * i, 2 * i + 1)
            ]
            tiles.append((a, b))
        up[at : at + 8, :] = jnp.where(row8 < 4, turn(tiles[0][0], 4, 0), tiles[0][1])
        down[at : at + 8, :] = jnp.where(row8 < 4, tiles[1][0], turn(tiles[1][1], 4, 0))


def low_halo(msg, i, which):
    tile = msg[(i % 4) * 8 : (i % 4) * 8 + 8, :]
    return turn(tile, -(64 * (i // 4) + 32 * which), 1)


def middle_halo(msg, x, which, below):
    tile = msg[32 + (x // 2) * 8 : 40 + (x // 2) * 8, :]
    tile = turn(tile, 64, 1) if which else tile
    return turn(tile, 4, 0) if (x % 2 == 0) == below else tile


def pack_lanes(up, down, row, count, planes, width, base, top):
    lane = lanes_of((count, 128))
    ups, downs = up[row : row + count, :], down[row : row + count, :]
    for i, v in enumerate(planes):
        at = base + width * i
        here = (lane >= at) & (lane < at + width)
        ups = jnp.where(here, turn(v, at - (top - width), 1), ups)
        downs = jnp.where(here, turn(v, at, 1), downs)
    up[row : row + count, :] = ups
    down[row : row + count, :] = downs


def pack_low_own(low_res, low_coef, res, sol, up, down):
    up[...] = jnp.zeros((48, 128), F32)
    down[...] = jnp.zeros((48, 128), F32)
    pack_lanes(up, down, 0, 16, [low_res[i] for i in range(8)], 8, 0, 32)
    pack_lanes(up, down, 0, 16, [low_coef[i] for i in range(8)], 8, 64, 32)
    pack_lanes(up, down, 16, 32, [res[x, 0:32, :] for x in range(16)], 4, 0, 64)
    pack_lanes(up, down, 16, 32, [sol[x, 0:32, :] for x in range(16)], 2, 64, 64)


def keep_fine(after, res0, diag0, inv0, res_q, diag_q, inv_q, r0_up, r0_down):
    for ref, kept, skip in ((res0, res_q, XH), (diag0, diag_q, 0), (inv0, inv_q, 0)):
        for x in range(NX0) if skip else range(1, NXE - 1):
            top, tail = to_q0(ref, x + skip)
            kept[x, 0:64, :] = top
            kept[x, 64:72, :] = tail
    lane = lanes_of((Q0, 128))
    for msg, first in ((r0_up, NX0 - XH), (r0_down, 0)):
        side = jnp.zeros((Q0, 128), F32)
        for i in range(XH):
            msg[i * Q0 : i * Q0 + Q0, :] = res_q[first + i, :, 0:128]
            v = res_q[first + i, :, 128:256]
            base = 6 * i
            side = jnp.where((lane >= base) & (lane < base + 3), turn(v, base, 1), side)
            side = jnp.where((lane >= base + 3) & (lane < base + 6), turn(v, base + 3 - 125, 1), side)
        far = 2 * XH + NX0 - 6 if first else 2 * XH - 1
        msg[4 * Q0 : 5 * Q0, :] = diag_q[far, :, 0:128]
        v = diag_q[far, :, 128:256]
        side = jnp.where((lane >= 18) & (lane < 21), turn(v, 18, 1), side)
        side = jnp.where((lane >= 21) & (lane < 24), turn(v, 21 - 125, 1), side)
        msg[XH * Q0 : XH * Q0 + Q0, :] = side


def pack_low_halo(own_up, own_down, above, below, up, down):
    for msg, own in ((up, own_up), (down, own_down)):
        msg[0:16, :] = own[0:16, :]
        msg[16:32, :] = jnp.zeros((16, 128), F32)
        msg[32:64, :] = own[16:48, :]
        msg[64:80, :] = jnp.zeros((16, 128), F32)
    for at, src, is_below in ((0, above, False), (8, below, True)):
        pack_lanes(up, down, 16 + at, 8, [low_halo(src, i, 0) for i in range(8)], 8, 0, 32)
        pack_lanes(up, down, 16 + at, 8, [low_halo(src, i, 1) for i in range(8)], 8, 64, 32)
        pack_lanes(up, down, 64 + at, 8, [middle_halo(src, x, 0, is_below) for x in range(16)], 4, 0, 64)
        pack_lanes(up, down, 64 + at, 8, [middle_halo(src, x, 1, is_below) for x in range(16)], 2, 64, 64)


def with_sides(own, left, right, base, width, own_lanes):
    lane = lanes_of(own.shape)
    v = jnp.where(lane < own_lanes, own, turn(right, own_lanes - base, 1))
    v = jnp.where(lane < own_lanes + width, v, 0.0)
    return jnp.where(lane < 128 - width, v, turn(left, 128 - width - base, 1))


def bottom(low_res, low_coef, above, below, left, right, sol2, res2, diag2, inv2, da2, db2):
    in_yz = inside_yz((R2, 128), 16, 24, 32, 64)
    empty = jnp.zeros((R2, 128), F32)
    for buffer in (da2, db2):
        buffer[0] = empty
        buffer[9] = empty
    from_left, from_right = left[0:R2, :], right[0:R2, :]
    for i in range(8):
        parts = []
        for a, ref in ((0, low_res), (1, low_coef)):
            own = jnp.concatenate([ref[i], low_halo(above, i, a), low_halo(below, i, a)], 0)
            parts.append(with_sides(own, from_left, from_right, a * 64 + i * 8, 8, 32))
        g = parts[1] + 0.375
        inverse = jnp.where(in_yz, 1.0 / g, 0.0)
        res2[i] = parts[0]
        diag2[i] = g
        inv2[i] = inverse
        d = parts[0] * inverse * (1.0 / THETA)
        da2[i + 1] = d
        sol2[i] = d
    pairs = coefficients(COARSE_SWEEPS)
    buffers = (da2, db2)
    for k in range(COARSE_SWEEPS - 1):
        src, dst = buffers[k % 2], buffers[(k + 1) % 2]
        line_sweep(src, dst, res2, diag2, inv2, 8, 0.0625, pairs[k], sol2)


def middle_after(
    sol2, res, sol, coef1, above, below, left, right, sol1, res1, diag1, inv1, da1, db1
):
    in_yz1 = inside_yz((Q1, 128), 32, 40, 64, 96)
    empty = jnp.zeros((Q1, 128), F32)
    for buffer in (da1, db1):
        buffer[0] = empty
        buffer[17] = empty
    for x in (0, 1, 18, 19):
        sol1[x] = empty
    from_left, from_right = left[R2 : R2 + Q1, :], right[R2 : R2 + Q1, :]
    lane = lanes_of((24, 128))
    half = lane // 2 + jnp.where(lane >= 96, 64, 0)
    first = rows_of((8, 128)) < 4
    for i in range(8):
        tail = jnp.where(first, sol2[i, 16:24, :], sol2[i, 24:32, :])
        lifted = pick(jnp.concatenate([sol2[i, 0:16, :], tail], 0), half)
        for x in (2 * i, 2 * i + 1):
            db1.at[x + 1][pl.ds(0, 24, stride=2), :] = lifted
            db1.at[x + 1][pl.ds(1, 24, stride=2), :] = lifted
            parts = []
            for a, ref in ((0, res), (1, sol)):
                own = jnp.concatenate(
                    [ref[x, 0:32, :], middle_halo(above, x, a, False), middle_halo(below, x, a, True)], 0
                )
                width = (4, 2)[a]
                parts.append(with_sides(own, from_left, from_right, a * 64 + width * x, width, 64))
            res1[x] = parts[0]
            sol1[x + 2] = jnp.where(in_yz1, parts[1], 0.0)

    def correct1(x, carry):
        g = jnp.concatenate([coef1[x], coef1[x, 32:40, :]], 0) + 1.5
        inverse = jnp.where(in_yz1, 1.0 / g, 0.0)
        diag1[x] = g
        inv1[x] = inverse
        p = db1[x + 1]
        near = beside(p) + (db1[x] + db1[x + 2])
        r = res1[x] - (g * p - 0.25 * near)
        res1[x] = r
        d = r * inverse * (1.0 / THETA)
        da1[x + 1] = d
        sol1[x + 2] += p + d
        return carry

    lax.fori_loop(0, 16, correct1, 0, unroll=True)
    pairs = coefficients(SWEEPS)
    buffers = (da1, db1)
    for k in range(SWEEPS - 1):
        src, dst = buffers[k % 2], buffers[(k + 1) % 2]
        line_sweep(src, dst, res1, diag1, inv1, 16, 0.25, pairs[k], sol1, 2)


def fine_after(
    sol1, sol0, res_q, diag_q, inv_q, low, high, out_sol, out_res, p0, res0, da0, db0, dc0
):
    gx = lax.axis_index("gx")
    half = lanes_of((R1, 128)) // 2
    first2 = rows_of((8, 128)) < 2
    for i in range(8):
        v = sol1[gx * 4 + i]
        v = jnp.concatenate([v[0:32], jnp.where(first2, v[32:40], turn(v[40:48], 4, 0))], 0)
        for side in range(2):
            lifted = pick(v, half + 64 * side)
            for x in (2 * i, 2 * i + 1):
                p0.at[x, side][pl.ds(0, R1, stride=2), :] = lifted
                p0.at[x, side][pl.ds(1, R1, stride=2), :] = lifted

    def lift(x):
        return jnp.concatenate([p0[x, 0, 0:Q0, :], p0[x, 1, 0:Q0, :]], 1)

    lane72 = lanes_of((Q0, 128))

    def with_lanes(main, side, base):
        v = jnp.where(lane72 < 3, turn(side, -base, 1), 0.0)
        v = jnp.where(lane72 < 125, v, turn(side, 125 - base - 3, 1))
        return jnp.concatenate([main, v], 1)

    outer = {}
    for msg, first, far in ((low, 0, 0), (high, XH + NX0, NXE - 1)):
        side = msg[XH * Q0 : XH * Q0 + Q0, :]
        for i in range(XH):
            outer[first + i] = with_lanes(msg[i * Q0 : i * Q0 + Q0, :], side, 6 * i)
        outer["diag", far] = with_lanes(msg[4 * Q0 : 5 * Q0, :], side, 18)
    in_yz = inside_yz((Q0, 256), 64, 68, 128, 192)
    low_x, high_x = gx > 0, gx < lax.axis_size("gx") - 1
    for x in range(NXE):
        p = lift(x + 1)
        near = beside(p) + (lift(x) + lift(x + 2))
        if x in (0, NXE - 1):
            g = outer["diag", x]
            inverse = jnp.where(in_yz & (low_x if x == 0 else high_x), 1.0 / g, 0.0)
        else:
            g, inverse = diag_q[x], inv_q[x]
        r = (outer[x] if x in outer else res_q[x - XH]) - (g * p - near)
        res0[x] = r
        da0[x] = r * inverse * (1.0 / THETA)
    pairs = coefficients(SWEEPS)
    steps = (da0, db0, dc0)
    for k in range(SWEEPS - 1):
        fine_sweep(steps[k], steps[k + 1], res0, diag_q, inv_q, k + 1, NXE - 1 - k, pairs[k])
    for x in range(NX0):
        at = x + XH
        d = dc0[at]
        near = beside(d)[0:64, 0:128] + (dc0[at - 1, 0:64, 0:128] + dc0[at + 1, 0:64, 0:128])
        d = d[0:64, 0:128]
        out_res[x] = res0[at, 0:64, 0:128] - (diag_q[at, 0:64, 0:128] * d - near)
        own = da0[at, 0:64, 0:128] + db0[at, 0:64, 0:128] + d
        out_sol[x] = sol0[x] + p0[at + 1, 0, 0:64, :] + own


def per_device(s, c):
    s, c = (pltpu.with_memory_space_constraint(v, pltpu.HBM) for v in (s, c))
    face = jax.ShapeDtypeStruct((2 * XH - 1, NY0, NZ0), F32)
    up, down = pl.pallas_call(
        pack_x,
        out_shape=[face] * 2,
        in_specs=[pl.BlockSpec(memory_space=pl.ANY)] * 2,
        out_specs=[pl.BlockSpec(memory_space=pltpu.VMEM)] * 2,
        scratch_shapes=[pltpu.VMEM((2, NY0, NZ0), F32), pltpu.SemaphoreType.DMA((6,))],
        compiler_params=pltpu.CompilerParams(vmem_limit_bytes=4 * MIB),
    )(s, c)
    s, c = pl.pallas_call(
        fetch_own,
        out_shape=[jax.ShapeDtypeStruct((NX0, NY0, NZ0), F32)] * 2,
        in_specs=[pl.BlockSpec(memory_space=pl.ANY)] * 3,
        out_specs=[pl.BlockSpec(memory_space=pltpu.VMEM)] * 2,
        scratch_shapes=[pltpu.SemaphoreType.DMA((2,))],
        compiler_params=pltpu.CompilerParams(vmem_limit_bytes=4 * MIB),
        cost_estimate=pl.CostEstimate(flops=0, bytes_accessed=3690000, transcendentals=0),
    )(up, s, c)
    low, high = ring(up, "gx", 1), ring(down, "gx", -1)
    up, down = call(pack_y, 4, [(YROWS, 128)] * 2, [], s, c, high, low)
    below_y, above_y = ring(up, "gy", 1), ring(down, "gy", -1)
    own_up, own_down = call(pack_z_own, 4, [(2, 64, 128)] * 2, [], s, c, high, low)
    up, down = call(pack_z_halo, 4, [(2, R0, 128)] * 2, [], own_up, own_down, below_y, above_y)
    below, above = ring(up, "gz", 1), ring(down, "gz", -1)
    big = (NXE, R0, 256)
    sol0, res0, diag0, inv0, msg = call(
        fine_before,
        16,
        [(NX0, 64, 128), big, big, big, (200, 128)],
        [big, big, big, (8, 2, 80, 128)],
        s, c, high, low, below_y, above_y, below, above,
        micros=4.0,
    )
    low, high, far = ring(msg, "gx", 1), ring(msg, "gx", -1), ring(msg, "gx", 2)
    big = (NXE, Q0, 256)
    res_q, diag_q, inv_q, r0_up, r0_down = call(
        keep_fine,
        8,
        [(NX0, Q0, 256), big, big, (5 * Q0, 128), (5 * Q0, 128)],
        [],
        low, res0, diag0, inv0,
        micros=2.0,
    )
    r0_low, r0_high = ring(r0_up, "gx", 1), ring(r0_down, "gx", -1)
    mid = (16, R1, 128)
    res1, sol1, coef1, res2, coef2, up, down = call(
        middle_before,
        8,
        [mid, mid, mid, (8, 16, 128), (8, 16, 128), (96, 128), (96, 128)],
        [mid, mid, (18, R1, 128), (18, R1, 128), (16, 32, 128)],
        msg, low, high, far,
        micros=2.0,
    )
    below, above = ring(up, "gy", 1), ring(down, "gy", -1)
    own_up, own_down = call(pack_low_own, 4, [(48, 128)] * 2, [], res2, coef2, res1, sol1, micros=2.0)
    up, down = call(pack_low_halo, 4, [(R2 + Q1, 128)] * 2, [], own_up, own_down, above, below)
    left, right = ring(up, "gz", 1), ring(down, "gz", -1)
    bot, mid = (8, R2, 128), (16, Q1, 128)
    big = (NXE, Q0, 256)
    own = (NX0, NY0, NZ0)
    (sol2,) = call(
        bottom, 4, [bot], [bot] * 3 + [(10, R2, 128)] * 2, res2, coef2, above, below, left, right
    )
    (sol1,) = call(
        middle_after,
        8,
        [(20, Q1, 128)],
        [mid] * 3 + [(18, Q1, 128)] * 2,
        sol2, res1, sol1, coef1, above, below, left, right,
        micros=2.0,
    )
    return tuple(
        call(
            fine_after,
            16,
            [own, own],
            [(16, 2, 80, 128)] + [big] * 4,
            sol1, sol0, res_q, diag_q, inv_q, r0_low, r0_high,
        )
    )


def solution(mesh):
    return jax.shard_map(
        per_device,
        mesh=mesh,
        in_specs=(P("gx", "gy", "gz"), P("gx", "gy", "gz")),
        out_specs=(P("gx", "gy", "gz"), P("gx", "gy", "gz")),
        check_vma=False,
    )
```

```python
import jax
import jax.numpy as jnp
from jax import lax
from jax.experimental import pallas as pl
from jax.experimental.pallas import tpu as pltpu
from jax.sharding import PartitionSpec as P

SWEEPS = 3
COARSE_SWEEPS = 6
THETA = 1.25
DELTA = 0.75
F32 = jnp.float32

XH = 3
NX0, NY0, NZ0 = 8, 64, 128
NXE = NX0 + 2 * XH
W = 9
R0 = 88
Q0 = 72
R1 = 40
Q1 = 48
R2 = 32
MIB = 1024 * 1024


def coefficients(count):
    sigma = THETA / DELTA
    rho = 1.0 / sigma
    pairs = []
    for _ in range(count):
        rho_new = 1.0 / (2.0 * sigma - rho)
        pairs.append((rho_new * rho, 2.0 * rho_new / DELTA))
        rho = rho_new
    return pairs


def turn(value, shift, axis):
    return pltpu.roll(value, shift % value.shape[axis], axis)


def beside(value):
    return (turn(value, 1, 0) + turn(value, -1, 0)) + (turn(value, 1, 1) + turn(value, -1, 1))


def rows_of(shape):
    return lax.broadcasted_iota(jnp.int32, shape, 0)


def lanes_of(shape):
    return lax.broadcasted_iota(jnp.int32, shape, 1)


def inside_yz(shape, own_rows, split_row, own_lanes, split_lane):
    gy, gz = lax.axis_index("gy"), lax.axis_index("gz")
    last_y, last_z = lax.axis_size("gy") - 1, lax.axis_size("gz") - 1
    row, lane = rows_of(shape), lanes_of(shape)
    up_y, down_y = (gy < last_y).astype(jnp.int32), (gy > 0).astype(jnp.int32)
    up_z, down_z = (gz < last_z).astype(jnp.int32), (gz > 0).astype(jnp.int32)
    in_y = jnp.where(row < own_rows, 1, jnp.where(row < split_row, up_y, down_y))
    in_z = jnp.where(lane < own_lanes, 1, jnp.where(lane < split_lane, up_z, down_z))
    return (in_y * in_z) > 0


def pick(value, lane):
    return jnp.take_along_axis(value, lane, axis=1, mode="promise_in_bounds")


def pairs_of_lanes(value):
    lane = lanes_of(value.shape)
    return pick(value + turn(value, -1, 1), 2 * lane - jnp.where(lane < 64, 0, 128))


def call(body, limit, outs, scratch, *args, micros=1.0):
    vmem = pl.BlockSpec(memory_space=pltpu.VMEM)
    return pl.pallas_call(
        body,
        out_shape=[jax.ShapeDtypeStruct(s, F32) for s in outs],
        in_specs=[vmem] * len(args),
        out_specs=[vmem] * len(outs),
        scratch_shapes=[pltpu.VMEM(s, F32) for s in scratch],
        compiler_params=pltpu.CompilerParams(vmem_limit_bytes=limit * MIB),
        cost_estimate=pl.CostEstimate(flops=0, bytes_accessed=int(micros * 3690000), transcendentals=0),
    )(*args)


def ring(value, axis, shift):
    size = lax.axis_size(axis)
    return lax.ppermute(value, axis, [(i, (i + shift) % size) for i in range(size)])


OWN_SLABS = [(a, x) for a in range(2) for x in range(XH, XH + NX0)]
SIDE_SLABS = [(a, x) for a in range(2) for x in range(a, NXE - a) if (a, x) not in OWN_SLABS]
SLAB = {slab: (which, at) for which, slabs in enumerate((OWN_SLABS, SIDE_SLABS)) for at, slab in enumerate(slabs)}
EXTRA = (8 * len(OWN_SLABS), 8 * len(SIDE_SLABS))
YROWS = (EXTRA[0] + 16, EXTRA[1] + 16)


def plane_of(own, low, high, which, x):
    if x < XH:
        return low.at[x if which == 0 else XH + x - 1]
    if x < XH + NX0:
        return own[which].at[x - XH]
    return high.at[x - XH - NX0 + (0 if which == 0 else XH)]


def pack_x(s, c, up, down, work, done):
    copies = []

    def fetch(src, dst):
        copies.append(pltpu.make_async_copy(src, dst, done.at[len(copies)]))
        copies[-1].start()

    fetch(s.at[pl.ds(NX0 - XH, XH)], up.at[pl.ds(0, XH)])
    fetch(c.at[pl.ds(NX0 - XH, 1)], work.at[pl.ds(0, 1)])
    fetch(s.at[pl.ds(0, XH)], down.at[pl.ds(0, XH)])
    fetch(c.at[pl.ds(XH - 1, 1)], work.at[pl.ds(1, 1)])
    fetch(c.at[pl.ds(NX0 - XH + 1, XH - 1)], up.at[pl.ds(XH, XH - 1)])
    fetch(c.at[pl.ds(0, XH - 1)], down.at[pl.ds(XH, XH - 1)])
    for copy in copies:
        copy.wait()
    up[0] = up[0] * (1.0 / (work[0] + 6.0)) * (1.0 / THETA)
    down[XH - 1] = down[XH - 1] * (1.0 / (work[1] + 6.0)) * (1.0 / THETA)


def put_rows(src, slab, up, down):
    which, at = SLAB[slab]
    up[at * 8 : at * 8 + 8, :] = src[56:64, :]
    down[at * 8 : at * 8 + 8, :] = src[0:8, :]
    extra = EXTRA[which] + at
    up[extra : extra + 1, :] = src[55:56, :]
    down[extra : extra + 1, :] = src[8:9, :]


def fetch_own(after, s, c, s_out, c_out, up, down, done):
    copies = [pltpu.make_async_copy(s, s_out, done.at[0]), pltpu.make_async_copy(c, c_out, done.at[1])]
    for copy in copies:
        copy.start()
    for copy in copies:
        copy.wait()
    for a, x in OWN_SLABS:
        put_rows((s_out, c_out)[a].at[x - XH], (a, x), up, down)


def pack_y(high, low, up, down):
    for a, x in SIDE_SLABS:
        put_rows(plane_of(None, low, high, a, x), (a, x), up, down)
    used = EXTRA[1] + len(SIDE_SLABS)
    up[used:, :] = jnp.zeros((YROWS[1] - used, 128), F32)
    down[used:, :] = jnp.zeros((YROWS[1] - used, 128), F32)


def pack_wide(up, down, row, count, plane):
    lane = lanes_of((count, 128))
    for a in range(2):
        ups = jnp.zeros((count, 128), F32)
        downs = jnp.zeros((count, 128), F32)
        for x in range(a, NXE - a):
            v = plane(a, x)
            here = (lane >= W * x) & (lane < W * x + W)
            ups = jnp.where(here, turn(v, W * x - (128 - W), 1), ups)
            downs = jnp.where(here, turn(v, W * x, 1), downs)
        up[a, row : row + count, :] = ups
        down[a, row : row + count, :] = downs


def halo_rows(below, above, a, x):
    which, at = SLAB[a, x]
    below, above = below[which], above[which]
    extra = EXTRA[which] + at
    row = rows_of((8, 128))
    middle = jnp.where(row == 0, above[extra : extra + 1, :], 0.0)
    middle = jnp.where(row == 7, below[extra : extra + 1, :], middle)
    return jnp.concatenate([above[at * 8 : at * 8 + 8, :], middle, below[at * 8 : at * 8 + 8, :]], 0)


def pack_z_own(s, c, high, low, up, down):
    pack_wide(up, down, 0, 64, lambda a, x: plane_of((s, c), low, high, a, x)[...])


def pack_z_halo(own_up, own_down, below0, above0, below1, above1, up, down):
    up[:, 0:64, :] = own_up[...]
    down[:, 0:64, :] = own_down[...]
    pack_wide(up, down, 64, 24, lambda a, x: halo_rows((below0, below1), (above0, above1), a, x))


def fine_sweep(src, dst, res, diag, inverse, first, stop, pair):
    for x in range(first, stop):
        d = src[x]
        near = beside(d) + (src[x - 1] + src[x + 1])
        r = res[x] - (diag[x] * d - near)
        res[x] = r
        if pair is not None:
            dst[x] = pair[0] * d + (pair[1] * inverse[x]) * r


def to_q0(ref, x):
    tail = jnp.where(rows_of((8, 256)) < 4, ref[x, 64:72, :], ref[x, 80:88, :])
    return ref[x, 0:64, :], tail


def fine_before(
    s, c, high, low, below0, above0, below1, above1, below, above, sol, res, diag, inv, msg, da, db, dc, rows
):
    lane = lanes_of((R0, 128))
    for a in range(2):
        left, right = below[a], above[a]
        for x in range(a, NXE - a):
            side = jnp.where(lane < W, turn(right, -W * x, 1), 0.0)
            side = jnp.where(lane >= 128 - W, turn(left, 128 - W - W * x, 1), side)
            ref = (res, diag)[a]
            ref[x, 0:64, 0:128] = plane_of((s, c), low, high, a, x)[...]
            ref[x, 64:88, 0:128] = halo_rows((below0, below1), (above0, above1), a, x)
            ref[x, :, 128:256] = side
    lane40 = lanes_of((R1, 128))

    def fold(ref, i, at):
        both = ref[XH + 2 * i] + ref[XH + 2 * i + 1]
        sides = []
        for side in range(2):
            part = both[:, 128 * side : 128 * side + 128]
            rows[at, side, 0:72, :] = part[0:72]
            rows[at, side, 72:80, :] = part[80:88]
            sides.append(rows.at[at, side][pl.ds(0, R1, stride=2), :] + rows.at[at, side][pl.ds(1, R1, stride=2), :])
        return 0.125 * jnp.where(lane40 < 64, pairs_of_lanes(sides[0]), pairs_of_lanes(sides[1]))

    coef1 = [fold(diag, i, i) for i in range(4)]

    gx = lax.axis_index("gx")
    in_yz = inside_yz((R0, 256), 64, 76, 128, 192)
    low_x, high_x = gx > 0, gx < lax.axis_size("gx") - 1

    for x in range(NXE):
        here = in_yz & (low_x if x < XH else high_x) if x < XH or x >= XH + NX0 else in_yz
        if x in (0, NXE - 1):
            da[x] = jnp.where(here, res[x], 0.0)
            continue
        g = diag[x] + 6.0
        diag[x] = g
        inverse = jnp.where(here, 1.0 / g, 0.0)
        inv[x] = inverse
        da[x] = res[x] * inverse * (1.0 / THETA)
    pairs = coefficients(SWEEPS)
    steps = (da, db, dc)
    for k in range(SWEEPS):
        last = k == SWEEPS - 1
        fine_sweep(
            steps[k], None if last else steps[k + 1], res, diag, inv, k + 1, NXE - 1 - k, None if last else pairs[k]
        )
    for x in range(NX0):
        sol[x] = sum(d[XH + x, 0:64, 0:128] for d in steps)

    halo = jnp.zeros((R1, 128), F32)
    for i in range(4):
        r1, c1 = fold(res, i, 4 + i), coef1[i]
        both = jnp.where(lane40 < 64, r1, turn(c1, 64, 1))
        msg[i * R1 : i * R1 + R1, :] = both
        for a, v in ((0, r1), (1, c1)):
            base = (a * 4 + i) * 8
            halo = jnp.where((lane40 >= base) & (lane40 < base + 4), turn(v, base - 64, 1), halo)
            halo = jnp.where((lane40 >= base + 4) & (lane40 < base + 8), turn(v, base + 4 - 124, 1), halo)
    msg[160:200, :] = halo


def line_sweep(src, dst, res, diag, inverse, planes, scale, pair, sol, ahead=0):
    def body(x, carry):
        d = src[x + 1]
        near = beside(d) + (src[x] + src[x + 2])
        r = res[x] - (diag[x] * d - scale * near)
        res[x] = r
        if pair is not None:
            step = pair[0] * d + (pair[1] * inverse[x]) * r
            dst[x + 1] = step
            sol[x + ahead] += step
        return carry

    lax.fori_loop(0, planes, body, 0, unroll=True)


def middle_before(own, low, far, high, res, sol, coef, low_res, low_coef, up, down, diag, inv, da, db, rows):
    gx = lax.axis_index("gx")
    size = lax.axis_size("gx")
    lane40 = lanes_of((R1, 128))
    for msg, shift in ((own, 0), (low, 3), (high, 1), (far, 2)):
        place = lax.rem(gx + shift, size) * 4
        side = msg[160:200, :]
        for i in range(4):
            both = msg[i * R1 : i * R1 + R1, :]
            for a, ref in ((0, res), (1, coef)):
                base = (a * 4 + i) * 8
                v = both if a == 0 else turn(both, 64, 1)
                v = jnp.where(lane40 < 64, v, turn(side, 64 - base, 1))
                v = jnp.where(lane40 < 68, v, 0.0)
                v = jnp.where(lane40 < 124, v, turn(side, 124 - base - 4, 1))
                ref[place + i] = v
    in_yz = inside_yz((R1, 128), 32, 36, 64, 96)
    empty = jnp.zeros((R1, 128), F32)
    for buffer in (da, db):
        buffer[0] = empty
        buffer[17] = empty

    def start(x, carry):
        g = coef[x] + 1.5
        diag[x] = g
        inverse = jnp.where(in_yz, 1.0 / g, 0.0)
        inv[x] = inverse
        d = res[x] * inverse * (1.0 / THETA)
        da[x + 1] = d
        sol[x] = d
        return carry

    lax.fori_loop(0, 16, start, 0, unroll=True)
    pairs = coefficients(SWEEPS)
    buffers = (da, db)
    for k in range(SWEEPS):
        src, dst = buffers[k % 2], buffers[(k + 1) % 2]
        line_sweep(src, dst, res, diag, inv, 16, 0.25, pairs[k] if k < SWEEPS - 1 else None, sol)
    lane8, row8 = lanes_of((8, 128)), rows_of((8, 128))

    def fold(ref, i, at):
        rows[at] = ref[2 * i, 0:32, :] + ref[2 * i + 1, 0:32, :]
        part = rows.at[at]
        return 0.125 * pairs_of_lanes(part[pl.ds(0, 16, stride=2), :] + part[pl.ds(1, 16, stride=2), :])

    lows = []
    for i in range(8):
        r2, c2 = fold(res, i, i), fold(coef, i, 8 + i)
        low_res[i] = r2
        low_coef[i] = c2
        lows.append(jnp.where(lanes_of((16, 128)) < 32, r2, turn(c2, 32, 1)))
    for i in range(4):
        both = jnp.where(lanes_of((16, 128)) < 64, lows[i], turn(lows[i + 4], 64, 1))
        up[i * 8 : i * 8 + 8, :] = both[8:16]
        down[i * 8 : i * 8 + 8, :] = both[0:8]
    for i in range(8):
        at = 32 + i * 8
        tiles = []
        for first in (24, 0):
            a, b = [
                jnp.where(lane8 < 64, res[x, first : first + 8, :], turn(sol[x, first : first + 8, :], 64, 1))
                for x in (2 * i, 2 * i + 1)
            ]
            tiles.append((a, b))
        up[at : at + 8, :] = jnp.where(row8 < 4, turn(tiles[0][0], 4, 0), tiles[0][1])
        down[at : at + 8, :] = jnp.where(row8 < 4, tiles[1][0], turn(tiles[1][1], 4, 0))


def low_halo(msg, i, which):
    tile = msg[(i % 4) * 8 : (i % 4) * 8 + 8, :]
    return turn(tile, -(64 * (i // 4) + 32 * which), 1)


def middle_halo(msg, x, which, below):
    tile = msg[32 + (x // 2) * 8 : 40 + (x // 2) * 8, :]
    tile = turn(tile, 64, 1) if which else tile
    return turn(tile, 4, 0) if (x % 2 == 0) == below else tile


def pack_lanes(up, down, row, count, planes, width, base, top):
    lane = lanes_of((count, 128))
    ups, downs = up[row : row + count, :], down[row : row + count, :]
    for i, v in enumerate(planes):
        at = base + width * i
        here = (lane >= at) & (lane < at + width)
        ups = jnp.where(here, turn(v, at - (top - width), 1), ups)
        downs = jnp.where(here, turn(v, at, 1), downs)
    up[row : row + count, :] = ups
    down[row : row + count, :] = downs


def pack_low_own(low_res, low_coef, res, sol, up, down):
    up[...] = jnp.zeros((48, 128), F32)
    down[...] = jnp.zeros((48, 128), F32)
    pack_lanes(up, down, 0, 16, [low_res[i] for i in range(8)], 8, 0, 32)
    pack_lanes(up, down, 0, 16, [low_coef[i] for i in range(8)], 8, 64, 32)
    pack_lanes(up, down, 16, 32, [res[x, 0:32, :] for x in range(16)], 4, 0, 64)
    pack_lanes(up, down, 16, 32, [sol[x, 0:32, :] for x in range(16)], 2, 64, 64)


def keep_fine(after, res0, diag0, inv0, res_q, diag_q, inv_q, r0_up, r0_down):
    for ref, kept, skip in ((res0, res_q, XH), (diag0, diag_q, 0), (inv0, inv_q, 0)):
        for x in range(NX0) if skip else range(1, NXE - 1):
            top, tail = to_q0(ref, x + skip)
            kept[x, 0:64, :] = top
            kept[x, 64:72, :] = tail
    lane = lanes_of((Q0, 128))
    for msg, first in ((r0_up, NX0 - XH), (r0_down, 0)):
        side = jnp.zeros((Q0, 128), F32)
        for i in range(XH):
            msg[i * Q0 : i * Q0 + Q0, :] = res_q[first + i, :, 0:128]
            v = res_q[first + i, :, 128:256]
            base = 6 * i
            side = jnp.where((lane >= base) & (lane < base + 3), turn(v, base, 1), side)
            side = jnp.where((lane >= base + 3) & (lane < base + 6), turn(v, base + 3 - 125, 1), side)
        far = 2 * XH + NX0 - 6 if first else 2 * XH - 1
        msg[4 * Q0 : 5 * Q0, :] = diag_q[far, :, 0:128]
        v = diag_q[far, :, 128:256]
        side = jnp.where((lane >= 18) & (lane < 21), turn(v, 18, 1), side)
        side = jnp.where((lane >= 21) & (lane < 24), turn(v, 21 - 125, 1), side)
        msg[XH * Q0 : XH * Q0 + Q0, :] = side


def pack_low_halo(own_up, own_down, above, below, up, down):
    for msg, own in ((up, own_up), (down, own_down)):
        msg[0:16, :] = own[0:16, :]
        msg[16:32, :] = jnp.zeros((16, 128), F32)
        msg[32:64, :] = own[16:48, :]
        msg[64:80, :] = jnp.zeros((16, 128), F32)
    for at, src, is_below in ((0, above, False), (8, below, True)):
        pack_lanes(up, down, 16 + at, 8, [low_halo(src, i, 0) for i in range(8)], 8, 0, 32)
        pack_lanes(up, down, 16 + at, 8, [low_halo(src, i, 1) for i in range(8)], 8, 64, 32)
        pack_lanes(up, down, 64 + at, 8, [middle_halo(src, x, 0, is_below) for x in range(16)], 4, 0, 64)
        pack_lanes(up, down, 64 + at, 8, [middle_halo(src, x, 1, is_below) for x in range(16)], 2, 64, 64)


def with_sides(own, left, right, base, width, own_lanes):
    lane = lanes_of(own.shape)
    v = jnp.where(lane < own_lanes, own, turn(right, own_lanes - base, 1))
    v = jnp.where(lane < own_lanes + width, v, 0.0)
    return jnp.where(lane < 128 - width, v, turn(left, 128 - width - base, 1))


def bottom(low_res, low_coef, below, above, left, right, sol2, res2, diag2, inv2, da2, db2):
    in_yz = inside_yz((R2, 128), 16, 24, 32, 64)
    empty = jnp.zeros((R2, 128), F32)
    for buffer in (da2, db2):
        buffer[0] = empty
        buffer[9] = empty
    from_left, from_right = left[0:R2, :], right[0:R2, :]
    for i in range(8):
        parts = []
        for a, ref in ((0, low_res), (1, low_coef)):
            own = jnp.concatenate([ref[i], low_halo(above, i, a), low_halo(below, i, a)], 0)
            parts.append(with_sides(own, from_left, from_right, a * 64 + i * 8, 8, 32))
        g = parts[1] + 0.375
        inverse = jnp.where(in_yz, 1.0 / g, 0.0)
        res2[i] = parts[0]
        diag2[i] = g
        inv2[i] = inverse
        d = parts[0] * inverse * (1.0 / THETA)
        da2[i + 1] = d
        sol2[i] = d
    pairs = coefficients(COARSE_SWEEPS)
    buffers = (da2, db2)
    for k in range(COARSE_SWEEPS - 1):
        src, dst = buffers[k % 2], buffers[(k + 1) % 2]
        line_sweep(src, dst, res2, diag2, inv2, 8, 0.0625, pairs[k], sol2)


def middle_after(
    sol2, res, sol, coef1, below, above, left, right, sol1, res1, diag1, inv1, da1, db1
):
    in_yz1 = inside_yz((Q1, 128), 32, 40, 64, 96)
    empty = jnp.zeros((Q1, 128), F32)
    for buffer in (da1, db1):
        buffer[0] = empty
        buffer[17] = empty
    for x in (0, 1, 18, 19):
        sol1[x] = empty
    from_left, from_right = left[R2 : R2 + Q1, :], right[R2 : R2 + Q1, :]
    lane = lanes_of((24, 128))
    half = lane // 2 + jnp.where(lane >= 96, 64, 0)
    first = rows_of((8, 128)) < 4
    for i in range(8):
        tail = jnp.where(first, sol2[i, 16:24, :], sol2[i, 24:32, :])
        lifted = pick(jnp.concatenate([sol2[i, 0:16, :], tail], 0), half)
        for x in (2 * i, 2 * i + 1):
            db1.at[x + 1][pl.ds(0, 24, stride=2), :] = lifted
            db1.at[x + 1][pl.ds(1, 24, stride=2), :] = lifted
            parts = []
            for a, ref in ((0, res), (1, sol)):
                own = jnp.concatenate(
                    [ref[x, 0:32, :], middle_halo(above, x, a, False), middle_halo(below, x, a, True)], 0
                )
                width = (4, 2)[a]
                parts.append(with_sides(own, from_left, from_right, a * 64 + width * x, width, 64))
            res1[x] = parts[0]
            sol1[x + 2] = jnp.where(in_yz1, parts[1], 0.0)

    def correct1(x, carry):
        g = jnp.concatenate([coef1[x], coef1[x, 32:40, :]], 0) + 1.5
        inverse = jnp.where(in_yz1, 1.0 / g, 0.0)
        diag1[x] = g
        inv1[x] = inverse
        p = db1[x + 1]
        near = beside(p) + (db1[x] + db1[x + 2])
        r = res1[x] - (g * p - 0.25 * near)
        res1[x] = r
        d = r * inverse * (1.0 / THETA)
        da1[x + 1] = d
        sol1[x + 2] += p + d
        return carry

    lax.fori_loop(0, 16, correct1, 0, unroll=True)
    pairs = coefficients(SWEEPS)
    buffers = (da1, db1)
    for k in range(SWEEPS - 1):
        src, dst = buffers[k % 2], buffers[(k + 1) % 2]
        line_sweep(src, dst, res1, diag1, inv1, 16, 0.25, pairs[k], sol1, 2)


def fine_after(
    sol1, sol0, res_q, diag_q, inv_q, low, high, out_sol, out_res, p0, res0, da0, db0, dc0
):
    gx = lax.axis_index("gx")
    half = lanes_of((R1, 128)) // 2
    first2 = rows_of((8, 128)) < 2
    for i in range(8):
        v = sol1[gx * 4 + i]
        v = jnp.concatenate([v[0:32], jnp.where(first2, v[32:40], turn(v[40:48], 4, 0))], 0)
        for side in range(2):
            lifted = pick(v, half + 64 * side)
            for x in (2 * i, 2 * i + 1):
                p0.at[x, side][pl.ds(0, R1, stride=2), :] = lifted
                p0.at[x, side][pl.ds(1, R1, stride=2), :] = lifted

    def lift(x):
        return jnp.concatenate([p0[x, 0, 0:Q0, :], p0[x, 1, 0:Q0, :]], 1)

    lane72 = lanes_of((Q0, 128))

    def with_lanes(main, side, base):
        v = jnp.where(lane72 < 3, turn(side, -base, 1), 0.0)
        v = jnp.where(lane72 < 125, v, turn(side, 125 - base - 3, 1))
        return jnp.concatenate([main, v], 1)

    outer = {}
    for msg, first, far in ((low, 0, 0), (high, XH + NX0, NXE - 1)):
        side = msg[XH * Q0 : XH * Q0 + Q0, :]
        for i in range(XH):
            outer[first + i] = with_lanes(msg[i * Q0 : i * Q0 + Q0, :], side, 6 * i)
        outer["diag", far] = with_lanes(msg[4 * Q0 : 5 * Q0, :], side, 18)
    in_yz = inside_yz((Q0, 256), 64, 68, 128, 192)
    low_x, high_x = gx > 0, gx < lax.axis_size("gx") - 1
    for x in range(NXE):
        p = lift(x + 1)
        near = beside(p) + (lift(x) + lift(x + 2))
        if x in (0, NXE - 1):
            g = outer["diag", x]
            inverse = jnp.where(in_yz & (low_x if x == 0 else high_x), 1.0 / g, 0.0)
        else:
            g, inverse = diag_q[x], inv_q[x]
        r = (outer[x] if x in outer else res_q[x - XH]) - (g * p - near)
        res0[x] = r
        da0[x] = r * inverse * (1.0 / THETA)
    pairs = coefficients(SWEEPS)
    steps = (da0, db0, dc0)
    for k in range(SWEEPS - 1):
        fine_sweep(steps[k], steps[k + 1], res0, diag_q, inv_q, k + 1, NXE - 1 - k, pairs[k])
    for x in range(NX0):
        at = x + XH
        d = dc0[at]
        near = beside(d)[0:64, 0:128] + (dc0[at - 1, 0:64, 0:128] + dc0[at + 1, 0:64, 0:128])
        d = d[0:64, 0:128]
        out_res[x] = res0[at, 0:64, 0:128] - (diag_q[at, 0:64, 0:128] * d - near)
        own = da0[at, 0:64, 0:128] + db0[at, 0:64, 0:128] + d
        out_sol[x] = sol0[x] + p0[at + 1, 0, 0:64, :] + own


def per_device(s, c):
    s, c = (pltpu.with_memory_space_constraint(v, pltpu.HBM) for v in (s, c))
    face = jax.ShapeDtypeStruct((2 * XH - 1, NY0, NZ0), F32)
    up, down = pl.pallas_call(
        pack_x,
        out_shape=[face] * 2,
        in_specs=[pl.BlockSpec(memory_space=pl.ANY)] * 2,
        out_specs=[pl.BlockSpec(memory_space=pltpu.VMEM)] * 2,
        scratch_shapes=[pltpu.VMEM((2, NY0, NZ0), F32), pltpu.SemaphoreType.DMA((6,))],
        compiler_params=pltpu.CompilerParams(vmem_limit_bytes=4 * MIB),
    )(s, c)
    s, c, own_up, own_down = pl.pallas_call(
        fetch_own,
        out_shape=[jax.ShapeDtypeStruct((NX0, NY0, NZ0), F32)] * 2 + [jax.ShapeDtypeStruct((YROWS[0], 128), F32)] * 2,
        in_specs=[pl.BlockSpec(memory_space=pl.ANY)] * 3,
        out_specs=[pl.BlockSpec(memory_space=pltpu.VMEM)] * 4,
        scratch_shapes=[pltpu.SemaphoreType.DMA((2,))],
        compiler_params=pltpu.CompilerParams(vmem_limit_bytes=4 * MIB),
        cost_estimate=pl.CostEstimate(flops=0, bytes_accessed=3690000, transcendentals=0),
    )(up, s, c)
    low, high = ring(up, "gx", 1), ring(down, "gx", -1)
    below0, above0 = ring(own_up, "gy", 1), ring(own_down, "gy", -1)
    up, down = call(pack_y, 4, [(YROWS[1], 128)] * 2, [], high, low)
    below1, above1 = ring(up, "gy", 1), ring(down, "gy", -1)
    own_up, own_down = call(pack_z_own, 4, [(2, 64, 128)] * 2, [], s, c, high, low)
    up, down = call(pack_z_halo, 4, [(2, R0, 128)] * 2, [], own_up, own_down, below0, above0, below1, above1)
    below, above = ring(up, "gz", 1), ring(down, "gz", -1)
    big = (NXE, R0, 256)
    sol0, res0, diag0, inv0, msg = call(
        fine_before,
        16,
        [(NX0, 64, 128), big, big, big, (200, 128)],
        [big, big, big, (8, 2, 80, 128)],
        s, c, high, low, below0, above0, below1, above1, below, above,
        micros=4.0,
    )
    low, high, far = ring(msg, "gx", 1), ring(msg, "gx", -1), ring(msg, "gx", 2)
    big = (NXE, Q0, 256)
    res_q, diag_q, inv_q, r0_up, r0_down = call(
        keep_fine,
        8,
        [(NX0, Q0, 256), big, big, (5 * Q0, 128), (5 * Q0, 128)],
        [],
        low, res0, diag0, inv0,
        micros=2.0,
    )
    r0_low, r0_high = ring(r0_up, "gx", 1), ring(r0_down, "gx", -1)
    mid = (16, R1, 128)
    res1, sol1, coef1, res2, coef2, up, down = call(
        middle_before,
        8,
        [mid, mid, mid, (8, 16, 128), (8, 16, 128), (96, 128), (96, 128)],
        [mid, mid, (18, R1, 128), (18, R1, 128), (16, 32, 128)],
        msg, low, far, high,
        micros=2.0,
    )
    below, above = ring(up, "gy", 1), ring(down, "gy", -1)
    own_up, own_down = call(pack_low_own, 4, [(48, 128)] * 2, [], res2, coef2, res1, sol1, micros=2.0)
    up, down = call(pack_low_halo, 4, [(R2 + Q1, 128)] * 2, [], own_up, own_down, above, below)
    left, right = ring(up, "gz", 1), ring(down, "gz", -1)
    bot, mid = (8, R2, 128), (16, Q1, 128)
    big = (NXE, Q0, 256)
    own = (NX0, NY0, NZ0)
    (sol2,) = call(
        bottom, 4, [bot], [bot] * 3 + [(10, R2, 128)] * 2, res2, coef2, below, above, left, right
    )
    (sol1,) = call(
        middle_after,
        8,
        [(20, Q1, 128)],
        [mid] * 3 + [(18, Q1, 128)] * 2,
        sol2, res1, sol1, coef1, below, above, left, right,
        micros=2.0,
    )
    return tuple(
        call(
            fine_after,
            16,
            [own, own],
            [(16, 2, 80, 128)] + [big] * 4,
            sol1, sol0, res_q, diag_q, inv_q, r0_low, r0_high,
        )
    )


def solution(mesh):
    return jax.shard_map(
        per_device,
        mesh=mesh,
        in_specs=(P("gx", "gy", "gz"), P("gx", "gy", "gz")),
        out_specs=(P("gx", "gy", "gz"), P("gx", "gy", "gz")),
        check_vma=False,
    )
```

```python
import jax
import jax.numpy as jnp
from jax import lax
from jax.experimental import pallas as pl
from jax.experimental.pallas import tpu as pltpu
from jax.sharding import PartitionSpec as P

SWEEPS = 3
COARSE_SWEEPS = 6
THETA = 1.25
DELTA = 0.75
F32 = jnp.float32

XH = 3
NX0, NY0, NZ0 = 8, 64, 128
NXE = NX0 + 2 * XH
W = 9
R0 = 88
Q0 = 72
R1 = 40
Q1 = 48
R2 = 32
MIB = 1024 * 1024


def coefficients(count):
    sigma = THETA / DELTA
    rho = 1.0 / sigma
    pairs = []
    for _ in range(count):
        rho_new = 1.0 / (2.0 * sigma - rho)
        pairs.append((rho_new * rho, 2.0 * rho_new / DELTA))
        rho = rho_new
    return pairs


def turn(value, shift, axis):
    return pltpu.roll(value, shift % value.shape[axis], axis)


def beside(value):
    return (turn(value, 1, 0) + turn(value, -1, 0)) + (turn(value, 1, 1) + turn(value, -1, 1))


def rows_of(shape):
    return lax.broadcasted_iota(jnp.int32, shape, 0)


def lanes_of(shape):
    return lax.broadcasted_iota(jnp.int32, shape, 1)


def inside_yz(shape, own_rows, split_row, own_lanes, split_lane):
    gy, gz = lax.axis_index("gy"), lax.axis_index("gz")
    last_y, last_z = lax.axis_size("gy") - 1, lax.axis_size("gz") - 1
    row, lane = rows_of(shape), lanes_of(shape)
    up_y, down_y = (gy < last_y).astype(jnp.int32), (gy > 0).astype(jnp.int32)
    up_z, down_z = (gz < last_z).astype(jnp.int32), (gz > 0).astype(jnp.int32)
    in_y = jnp.where(row < own_rows, 1, jnp.where(row < split_row, up_y, down_y))
    in_z = jnp.where(lane < own_lanes, 1, jnp.where(lane < split_lane, up_z, down_z))
    return (in_y * in_z) > 0


def pick(value, lane):
    return jnp.take_along_axis(value, lane, axis=1, mode="promise_in_bounds")


def pairs_of_lanes(value):
    lane = lanes_of(value.shape)
    return pick(value + turn(value, -1, 1), 2 * lane - jnp.where(lane < 64, 0, 128))


def call(body, limit, outs, scratch, *args, micros=1.0):
    vmem = pl.BlockSpec(memory_space=pltpu.VMEM)
    return pl.pallas_call(
        body,
        out_shape=[jax.ShapeDtypeStruct(s, F32) for s in outs],
        in_specs=[vmem] * len(args),
        out_specs=[vmem] * len(outs),
        scratch_shapes=[pltpu.VMEM(s, F32) for s in scratch],
        compiler_params=pltpu.CompilerParams(vmem_limit_bytes=limit * MIB),
        cost_estimate=pl.CostEstimate(flops=0, bytes_accessed=int(micros * 3690000), transcendentals=0),
    )(*args)


def ring(value, axis, shift):
    size = lax.axis_size(axis)
    return lax.ppermute(value, axis, [(i, (i + shift) % size) for i in range(size)])


OWN_SLABS = [(a, x) for a in range(2) for x in range(XH, XH + NX0)]
SIDE_SLABS = [(a, x) for a in range(2) for x in range(a, NXE - a) if (a, x) not in OWN_SLABS]
SLAB = {slab: (which, at) for which, slabs in enumerate((OWN_SLABS, SIDE_SLABS)) for at, slab in enumerate(slabs)}
EXTRA = (8 * len(OWN_SLABS), 8 * len(SIDE_SLABS))
YROWS = (EXTRA[0] + 16, EXTRA[1] + 16)


def plane_of(own, low, high, which, x):
    if x < XH:
        return low.at[x if which == 0 else XH + x - 1]
    if x < XH + NX0:
        return own[which].at[x - XH]
    return high.at[x - XH - NX0 + (0 if which == 0 else XH)]


def pack_x(s, c, up, down, work, done):
    copies = []

    def fetch(src, dst):
        copies.append(pltpu.make_async_copy(src, dst, done.at[len(copies)]))
        copies[-1].start()

    fetch(s.at[pl.ds(NX0 - XH, XH)], up.at[pl.ds(0, XH)])
    fetch(c.at[pl.ds(NX0 - XH, 1)], work.at[pl.ds(0, 1)])
    fetch(s.at[pl.ds(0, XH)], down.at[pl.ds(0, XH)])
    fetch(c.at[pl.ds(XH - 1, 1)], work.at[pl.ds(1, 1)])
    fetch(c.at[pl.ds(NX0 - XH + 1, XH - 1)], up.at[pl.ds(XH, XH - 1)])
    fetch(c.at[pl.ds(0, XH - 1)], down.at[pl.ds(XH, XH - 1)])
    for copy in copies:
        copy.wait()
    up[0] = up[0] * (1.0 / (work[0] + 6.0)) * (1.0 / THETA)
    down[XH - 1] = down[XH - 1] * (1.0 / (work[1] + 6.0)) * (1.0 / THETA)


def put_rows(src, slab, up, down):
    which, at = SLAB[slab]
    up[at * 8 : at * 8 + 8, :] = src[56:64, :]
    down[at * 8 : at * 8 + 8, :] = src[0:8, :]
    extra = EXTRA[which] + at
    up[extra : extra + 1, :] = src[55:56, :]
    down[extra : extra + 1, :] = src[8:9, :]


def fetch_own(after, s, c, s_out, c_out, up, down, done):
    copies = [pltpu.make_async_copy(s, s_out, done.at[0]), pltpu.make_async_copy(c, c_out, done.at[1])]
    for copy in copies:
        copy.start()
    for copy in copies:
        copy.wait()
    for a, x in OWN_SLABS:
        put_rows((s_out, c_out)[a].at[x - XH], (a, x), up, down)


def pack_y(high, low, up, down):
    for a, x in SIDE_SLABS:
        put_rows(plane_of(None, low, high, a, x), (a, x), up, down)
    used = EXTRA[1] + len(SIDE_SLABS)
    up[used:, :] = jnp.zeros((YROWS[1] - used, 128), F32)
    down[used:, :] = jnp.zeros((YROWS[1] - used, 128), F32)


def pack_wide(up, down, row, count, plane):
    lane = lanes_of((count, 128))
    for a in range(2):
        ups = jnp.zeros((count, 128), F32)
        downs = jnp.zeros((count, 128), F32)
        for x in range(a, NXE - a):
            v = plane(a, x)
            here = (lane >= W * x) & (lane < W * x + W)
            ups = jnp.where(here, turn(v, W * x - (128 - W), 1), ups)
            downs = jnp.where(here, turn(v, W * x, 1), downs)
        up[a, row : row + count, :] = ups
        down[a, row : row + count, :] = downs


def halo_rows(below, above, a, x):
    which, at = SLAB[a, x]
    below, above = below[which], above[which]
    extra = EXTRA[which] + at
    row = rows_of((8, 128))
    middle = jnp.where(row == 0, above[extra : extra + 1, :], 0.0)
    middle = jnp.where(row == 7, below[extra : extra + 1, :], middle)
    return jnp.concatenate([above[at * 8 : at * 8 + 8, :], middle, below[at * 8 : at * 8 + 8, :]], 0)


def pack_z_own(s, c, high, low, up, down):
    pack_wide(up, down, 0, 64, lambda a, x: plane_of((s, c), low, high, a, x)[...])


def pack_z_halo(own_up, own_down, below0, above0, below1, above1, up, down):
    up[:, 0:64, :] = own_up[...]
    down[:, 0:64, :] = own_down[...]
    pack_wide(up, down, 64, 24, lambda a, x: halo_rows((below0, below1), (above0, above1), a, x))


def fine_sweep(src, dst, res, diag, inverse, first, stop, pair, parts):
    for x in range(first, stop):
        d = src[x]
        near = beside(d) + (src[x - 1] + src[x + 1])
        for low, high in parts:
            part = d[low:high]
            r = res[x, low:high, :] - (diag[x, low:high, :] * part - near[low:high])
            res[x, low:high, :] = r
            if pair is not None:
                dst[x, low:high, :] = pair[0] * part + (pair[1] * inverse[x, low:high, :]) * r


def to_q0(ref, x):
    tail = jnp.where(rows_of((8, 256)) < 4, ref[x, 64:72, :], ref[x, 80:88, :])
    return ref[x, 0:64, :], tail


def fine_before(
    s, c, high, low, below0, above0, below1, above1, below, above, sol, res, diag, inv, msg, da, db, dc, rows
):
    lane = lanes_of((R0, 128))
    for a in range(2):
        left, right = below[a], above[a]
        for x in range(a, NXE - a):
            side = jnp.where(lane < W, turn(right, -W * x, 1), 0.0)
            side = jnp.where(lane >= 128 - W, turn(left, 128 - W - W * x, 1), side)
            ref = (res, diag)[a]
            ref[x, 0:64, 0:128] = plane_of((s, c), low, high, a, x)[...]
            ref[x, 64:88, 0:128] = halo_rows((below0, below1), (above0, above1), a, x)
            ref[x, :, 128:256] = side
    lane40 = lanes_of((R1, 128))

    def fold(ref, i, at):
        both = ref[XH + 2 * i] + ref[XH + 2 * i + 1]
        sides = []
        for side in range(2):
            part = both[:, 128 * side : 128 * side + 128]
            rows[at, side, 0:72, :] = part[0:72]
            rows[at, side, 72:80, :] = part[80:88]
            sides.append(rows.at[at, side][pl.ds(0, R1, stride=2), :] + rows.at[at, side][pl.ds(1, R1, stride=2), :])
        return 0.125 * jnp.where(lane40 < 64, pairs_of_lanes(sides[0]), pairs_of_lanes(sides[1]))

    coef1 = [fold(diag, i, i) for i in range(4)]

    gx = lax.axis_index("gx")
    in_yz = inside_yz((R0, 256), 64, 76, 128, 192)
    low_x, high_x = gx > 0, gx < lax.axis_size("gx") - 1

    for x in range(NXE):
        here = in_yz & (low_x if x < XH else high_x) if x < XH or x >= XH + NX0 else in_yz
        if x in (0, NXE - 1):
            da[x] = jnp.where(here, res[x], 0.0)
            continue
        g = diag[x] + 6.0
        diag[x] = g
        inverse = jnp.where(here, 1.0 / g, 0.0)
        inv[x] = inverse
        da[x] = res[x] * inverse * (1.0 / THETA)
    pairs = coefficients(SWEEPS)
    steps = (da, db, dc)
    for x in range(NXE):
        db[x, 72:80, :] = jnp.zeros((8, 256), F32)
        dc[x, 72:80, :] = jnp.zeros((8, 256), F32)
    for k in range(SWEEPS):
        last = k == SWEEPS - 1
        fine_sweep(
            steps[k], None if last else steps[k + 1], res, diag, inv, k + 1, NXE - 1 - k,
            None if last else pairs[k], ((0, 72), (80, 88)),
        )
    for x in range(NX0):
        sol[x] = sum(d[XH + x, 0:64, 0:128] for d in steps)

    halo = jnp.zeros((R1, 128), F32)
    for i in range(4):
        r1, c1 = fold(res, i, 4 + i), coef1[i]
        both = jnp.where(lane40 < 64, r1, turn(c1, 64, 1))
        msg[i * R1 : i * R1 + R1, :] = both
        for a, v in ((0, r1), (1, c1)):
            base = (a * 4 + i) * 8
            halo = jnp.where((lane40 >= base) & (lane40 < base + 4), turn(v, base - 64, 1), halo)
            halo = jnp.where((lane40 >= base + 4) & (lane40 < base + 8), turn(v, base + 4 - 124, 1), halo)
    msg[160:200, :] = halo


def line_sweep(src, dst, res, diag, inverse, planes, scale, pair, sol, ahead=0):
    def body(x, carry):
        d = src[x + 1]
        near = beside(d) + (src[x] + src[x + 2])
        r = res[x] - (diag[x] * d - scale * near)
        res[x] = r
        if pair is not None:
            step = pair[0] * d + (pair[1] * inverse[x]) * r
            dst[x + 1] = step
            sol[x + ahead] += step
        return carry

    lax.fori_loop(0, planes, body, 0, unroll=True)


def middle_before(own, low, far, high, res, sol, coef, low_res, low_coef, up, down, diag, inv, da, db, rows):
    gx = lax.axis_index("gx")
    size = lax.axis_size("gx")
    lane40 = lanes_of((R1, 128))
    for msg, shift in ((own, 0), (low, 3), (high, 1), (far, 2)):
        place = lax.rem(gx + shift, size) * 4
        side = msg[160:200, :]
        for i in range(4):
            both = msg[i * R1 : i * R1 + R1, :]
            for a, ref in ((0, res), (1, coef)):
                base = (a * 4 + i) * 8
                v = both if a == 0 else turn(both, 64, 1)
                v = jnp.where(lane40 < 64, v, turn(side, 64 - base, 1))
                v = jnp.where(lane40 < 68, v, 0.0)
                v = jnp.where(lane40 < 124, v, turn(side, 124 - base - 4, 1))
                ref[place + i] = v
    in_yz = inside_yz((R1, 128), 32, 36, 64, 96)
    empty = jnp.zeros((R1, 128), F32)
    for buffer in (da, db):
        buffer[0] = empty
        buffer[17] = empty

    def start(x, carry):
        g = coef[x] + 1.5
        diag[x] = g
        inverse = jnp.where(in_yz, 1.0 / g, 0.0)
        inv[x] = inverse
        d = res[x] * inverse * (1.0 / THETA)
        da[x + 1] = d
        sol[x] = d
        return carry

    lax.fori_loop(0, 16, start, 0, unroll=True)
    pairs = coefficients(SWEEPS)
    buffers = (da, db)
    for k in range(SWEEPS):
        src, dst = buffers[k % 2], buffers[(k + 1) % 2]
        line_sweep(src, dst, res, diag, inv, 16, 0.25, pairs[k] if k < SWEEPS - 1 else None, sol)
    lane8, row8 = lanes_of((8, 128)), rows_of((8, 128))

    def fold(ref, i, at):
        rows[at] = ref[2 * i, 0:32, :] + ref[2 * i + 1, 0:32, :]
        part = rows.at[at]
        return 0.125 * pairs_of_lanes(part[pl.ds(0, 16, stride=2), :] + part[pl.ds(1, 16, stride=2), :])

    lows = []
    for i in range(8):
        r2, c2 = fold(res, i, i), fold(coef, i, 8 + i)
        low_res[i] = r2
        low_coef[i] = c2
        lows.append(jnp.where(lanes_of((16, 128)) < 32, r2, turn(c2, 32, 1)))
    for i in range(4):
        both = jnp.where(lanes_of((16, 128)) < 64, lows[i], turn(lows[i + 4], 64, 1))
        up[i * 8 : i * 8 + 8, :] = both[8:16]
        down[i * 8 : i * 8 + 8, :] = both[0:8]
    for i in range(8):
        at = 32 + i * 8
        tiles = []
        for first in (24, 0):
            a, b = [
                jnp.where(lane8 < 64, res[x, first : first + 8, :], turn(sol[x, first : first + 8, :], 64, 1))
                for x in (2 * i, 2 * i + 1)
            ]
            tiles.append((a, b))
        up[at : at + 8, :] = jnp.where(row8 < 4, turn(tiles[0][0], 4, 0), tiles[0][1])
        down[at : at + 8, :] = jnp.where(row8 < 4, tiles[1][0], turn(tiles[1][1], 4, 0))


def low_halo(msg, i, which):
    tile = msg[(i % 4) * 8 : (i % 4) * 8 + 8, :]
    return turn(tile, -(64 * (i // 4) + 32 * which), 1)


def middle_halo(msg, x, which, below):
    tile = msg[32 + (x // 2) * 8 : 40 + (x // 2) * 8, :]
    tile = turn(tile, 64, 1) if which else tile
    return turn(tile, 4, 0) if (x % 2 == 0) == below else tile


def pack_lanes(up, down, row, count, planes, width, base, top):
    lane = lanes_of((count, 128))
    ups, downs = up[row : row + count, :], down[row : row + count, :]
    for i, v in enumerate(planes):
        at = base + width * i
        here = (lane >= at) & (lane < at + width)
        ups = jnp.where(here, turn(v, at - (top - width), 1), ups)
        downs = jnp.where(here, turn(v, at, 1), downs)
    up[row : row + count, :] = ups
    down[row : row + count, :] = downs


def pack_low_own(low_res, low_coef, res, sol, up, down):
    up[...] = jnp.zeros((48, 128), F32)
    down[...] = jnp.zeros((48, 128), F32)
    pack_lanes(up, down, 0, 16, [low_res[i] for i in range(8)], 8, 0, 32)
    pack_lanes(up, down, 0, 16, [low_coef[i] for i in range(8)], 8, 64, 32)
    pack_lanes(up, down, 16, 32, [res[x, 0:32, :] for x in range(16)], 4, 0, 64)
    pack_lanes(up, down, 16, 32, [sol[x, 0:32, :] for x in range(16)], 2, 64, 64)


def keep_fine(after, res0, diag0, inv0, res_q, diag_q, inv_q, r0_up, r0_down):
    for ref, kept, skip in ((res0, res_q, XH), (diag0, diag_q, 0), (inv0, inv_q, 0)):
        for x in range(NX0) if skip else range(1, NXE - 1):
            top, tail = to_q0(ref, x + skip)
            kept[x, 0:64, :] = top
            kept[x, 64:72, :] = tail
    lane = lanes_of((Q0, 128))
    for msg, first in ((r0_up, NX0 - XH), (r0_down, 0)):
        side = jnp.zeros((Q0, 128), F32)
        for i in range(XH):
            msg[i * Q0 : i * Q0 + Q0, :] = res_q[first + i, :, 0:128]
            v = res_q[first + i, :, 128:256]
            base = 6 * i
            side = jnp.where((lane >= base) & (lane < base + 3), turn(v, base, 1), side)
            side = jnp.where((lane >= base + 3) & (lane < base + 6), turn(v, base + 3 - 125, 1), side)
        far = 2 * XH + NX0 - 6 if first else 2 * XH - 1
        msg[4 * Q0 : 5 * Q0, :] = diag_q[far, :, 0:128]
        v = diag_q[far, :, 128:256]
        side = jnp.where((lane >= 18) & (lane < 21), turn(v, 18, 1), side)
        side = jnp.where((lane >= 21) & (lane < 24), turn(v, 21 - 125, 1), side)
        msg[XH * Q0 : XH * Q0 + Q0, :] = side


def pack_low_halo(own_up, own_down, above, below, up, down):
    for msg, own in ((up, own_up), (down, own_down)):
        msg[0:16, :] = own[0:16, :]
        msg[16:32, :] = jnp.zeros((16, 128), F32)
        msg[32:64, :] = own[16:48, :]
        msg[64:80, :] = jnp.zeros((16, 128), F32)
    for at, src, is_below in ((0, above, False), (8, below, True)):
        pack_lanes(up, down, 16 + at, 8, [low_halo(src, i, 0) for i in range(8)], 8, 0, 32)
        pack_lanes(up, down, 16 + at, 8, [low_halo(src, i, 1) for i in range(8)], 8, 64, 32)
        pack_lanes(up, down, 64 + at, 8, [middle_halo(src, x, 0, is_below) for x in range(16)], 4, 0, 64)
        pack_lanes(up, down, 64 + at, 8, [middle_halo(src, x, 1, is_below) for x in range(16)], 2, 64, 64)


def with_sides(own, left, right, base, width, own_lanes):
    lane = lanes_of(own.shape)
    v = jnp.where(lane < own_lanes, own, turn(right, own_lanes - base, 1))
    v = jnp.where(lane < own_lanes + width, v, 0.0)
    return jnp.where(lane < 128 - width, v, turn(left, 128 - width - base, 1))


def bottom(low_res, low_coef, below, above, left, right, sol2, res2, diag2, inv2, da2, db2):
    in_yz = inside_yz((R2, 128), 16, 24, 32, 64)
    empty = jnp.zeros((R2, 128), F32)
    for buffer in (da2, db2):
        buffer[0] = empty
        buffer[9] = empty
    from_left, from_right = left[0:R2, :], right[0:R2, :]
    for i in range(8):
        parts = []
        for a, ref in ((0, low_res), (1, low_coef)):
            own = jnp.concatenate([ref[i], low_halo(above, i, a), low_halo(below, i, a)], 0)
            parts.append(with_sides(own, from_left, from_right, a * 64 + i * 8, 8, 32))
        g = parts[1] + 0.375
        inverse = jnp.where(in_yz, 1.0 / g, 0.0)
        res2[i] = parts[0]
        diag2[i] = g
        inv2[i] = inverse
        d = parts[0] * inverse * (1.0 / THETA)
        da2[i + 1] = d
        sol2[i] = d
    pairs = coefficients(COARSE_SWEEPS)
    buffers = (da2, db2)
    for k in range(COARSE_SWEEPS - 1):
        src, dst = buffers[k % 2], buffers[(k + 1) % 2]
        line_sweep(src, dst, res2, diag2, inv2, 8, 0.0625, pairs[k], sol2)


def middle_after(
    sol2, res, sol, coef1, below, above, left, right, sol1, res1, diag1, inv1, da1, db1
):
    in_yz1 = inside_yz((Q1, 128), 32, 40, 64, 96)
    empty = jnp.zeros((Q1, 128), F32)
    for buffer in (da1, db1):
        buffer[0] = empty
        buffer[17] = empty
    for x in (0, 1, 18, 19):
        sol1[x] = empty
    from_left, from_right = left[R2 : R2 + Q1, :], right[R2 : R2 + Q1, :]
    lane = lanes_of((24, 128))
    half = lane // 2 + jnp.where(lane >= 96, 64, 0)
    first = rows_of((8, 128)) < 4
    for i in range(8):
        tail = jnp.where(first, sol2[i, 16:24, :], sol2[i, 24:32, :])
        lifted = pick(jnp.concatenate([sol2[i, 0:16, :], tail], 0), half)
        for x in (2 * i, 2 * i + 1):
            db1.at[x + 1][pl.ds(0, 24, stride=2), :] = lifted
            db1.at[x + 1][pl.ds(1, 24, stride=2), :] = lifted
            parts = []
            for a, ref in ((0, res), (1, sol)):
                own = jnp.concatenate(
                    [ref[x, 0:32, :], middle_halo(above, x, a, False), middle_halo(below, x, a, True)], 0
                )
                width = (4, 2)[a]
                parts.append(with_sides(own, from_left, from_right, a * 64 + width * x, width, 64))
            res1[x] = parts[0]
            sol1[x + 2] = jnp.where(in_yz1, parts[1], 0.0)

    def correct1(x, carry):
        g = jnp.concatenate([coef1[x], coef1[x, 32:40, :]], 0) + 1.5
        inverse = jnp.where(in_yz1, 1.0 / g, 0.0)
        diag1[x] = g
        inv1[x] = inverse
        p = db1[x + 1]
        near = beside(p) + (db1[x] + db1[x + 2])
        r = res1[x] - (g * p - 0.25 * near)
        res1[x] = r
        d = r * inverse * (1.0 / THETA)
        da1[x + 1] = d
        sol1[x + 2] += p + d
        return carry

    lax.fori_loop(0, 16, correct1, 0, unroll=True)
    pairs = coefficients(SWEEPS)
    buffers = (da1, db1)
    for k in range(SWEEPS - 1):
        src, dst = buffers[k % 2], buffers[(k + 1) % 2]
        line_sweep(src, dst, res1, diag1, inv1, 16, 0.25, pairs[k], sol1, 2)


def fine_after(
    sol1, sol0, res_q, diag_q, inv_q, low, high, out_sol, out_res, p0, res0, da0, db0, dc0
):
    gx = lax.axis_index("gx")
    half = lanes_of((R1, 128)) // 2
    first2 = rows_of((8, 128)) < 2
    for i in range(8):
        v = sol1[gx * 4 + i]
        v = jnp.concatenate([v[0:32], jnp.where(first2, v[32:40], turn(v[40:48], 4, 0))], 0)
        for side in range(2):
            lifted = pick(v, half + 64 * side)
            for x in (2 * i, 2 * i + 1):
                p0.at[x, side][pl.ds(0, R1, stride=2), :] = lifted
                p0.at[x, side][pl.ds(1, R1, stride=2), :] = lifted

    def lift(x):
        return jnp.concatenate([p0[x, 0, 0:Q0, :], p0[x, 1, 0:Q0, :]], 1)

    lane72 = lanes_of((Q0, 128))

    def with_lanes(main, side, base):
        v = jnp.where(lane72 < 3, turn(side, -base, 1), 0.0)
        v = jnp.where(lane72 < 125, v, turn(side, 125 - base - 3, 1))
        return jnp.concatenate([main, v], 1)

    outer = {}
    for msg, first, far in ((low, 0, 0), (high, XH + NX0, NXE - 1)):
        side = msg[XH * Q0 : XH * Q0 + Q0, :]
        for i in range(XH):
            outer[first + i] = with_lanes(msg[i * Q0 : i * Q0 + Q0, :], side, 6 * i)
        outer["diag", far] = with_lanes(msg[4 * Q0 : 5 * Q0, :], side, 18)
    in_yz = inside_yz((Q0, 256), 64, 68, 128, 192)
    low_x, high_x = gx > 0, gx < lax.axis_size("gx") - 1
    for x in range(NXE):
        p = lift(x + 1)
        near = beside(p) + (lift(x) + lift(x + 2))
        if x in (0, NXE - 1):
            g = outer["diag", x]
            inverse = jnp.where(in_yz & (low_x if x == 0 else high_x), 1.0 / g, 0.0)
        else:
            g, inverse = diag_q[x], inv_q[x]
        r = (outer[x] if x in outer else res_q[x - XH]) - (g * p - near)
        res0[x] = r
        da0[x] = r * inverse * (1.0 / THETA)
    pairs = coefficients(SWEEPS)
    steps = (da0, db0, dc0)
    for k in range(SWEEPS - 1):
        fine_sweep(steps[k], steps[k + 1], res0, diag_q, inv_q, k + 1, NXE - 1 - k, pairs[k], ((0, 72),))
    for x in range(NX0):
        at = x + XH
        d = dc0[at]
        near = beside(d)[0:64, 0:128] + (dc0[at - 1, 0:64, 0:128] + dc0[at + 1, 0:64, 0:128])
        d = d[0:64, 0:128]
        out_res[x] = res0[at, 0:64, 0:128] - (diag_q[at, 0:64, 0:128] * d - near)
        own = da0[at, 0:64, 0:128] + db0[at, 0:64, 0:128] + d
        out_sol[x] = sol0[x] + p0[at + 1, 0, 0:64, :] + own


def per_device(s, c):
    s, c = (pltpu.with_memory_space_constraint(v, pltpu.HBM) for v in (s, c))
    face = jax.ShapeDtypeStruct((2 * XH - 1, NY0, NZ0), F32)
    up, down = pl.pallas_call(
        pack_x,
        out_shape=[face] * 2,
        in_specs=[pl.BlockSpec(memory_space=pl.ANY)] * 2,
        out_specs=[pl.BlockSpec(memory_space=pltpu.VMEM)] * 2,
        scratch_shapes=[pltpu.VMEM((2, NY0, NZ0), F32), pltpu.SemaphoreType.DMA((6,))],
        compiler_params=pltpu.CompilerParams(vmem_limit_bytes=4 * MIB),
    )(s, c)
    s, c, own_up, own_down = pl.pallas_call(
        fetch_own,
        out_shape=[jax.ShapeDtypeStruct((NX0, NY0, NZ0), F32)] * 2 + [jax.ShapeDtypeStruct((YROWS[0], 128), F32)] * 2,
        in_specs=[pl.BlockSpec(memory_space=pl.ANY)] * 3,
        out_specs=[pl.BlockSpec(memory_space=pltpu.VMEM)] * 4,
        scratch_shapes=[pltpu.SemaphoreType.DMA((2,))],
        compiler_params=pltpu.CompilerParams(vmem_limit_bytes=4 * MIB),
        cost_estimate=pl.CostEstimate(flops=0, bytes_accessed=3690000, transcendentals=0),
    )(up, s, c)
    low, high = ring(up, "gx", 1), ring(down, "gx", -1)
    below0, above0 = ring(own_up, "gy", 1), ring(own_down, "gy", -1)
    up, down = call(pack_y, 4, [(YROWS[1], 128)] * 2, [], high, low)
    below1, above1 = ring(up, "gy", 1), ring(down, "gy", -1)
    own_up, own_down = call(pack_z_own, 4, [(2, 64, 128)] * 2, [], s, c, high, low)
    up, down = call(pack_z_halo, 4, [(2, R0, 128)] * 2, [], own_up, own_down, below0, above0, below1, above1)
    below, above = ring(up, "gz", 1), ring(down, "gz", -1)
    big = (NXE, R0, 256)
    sol0, res0, diag0, inv0, msg = call(
        fine_before,
        16,
        [(NX0, 64, 128), big, big, big, (200, 128)],
        [big, big, big, (8, 2, 80, 128)],
        s, c, high, low, below0, above0, below1, above1, below, above,
        micros=4.0,
    )
    low, high, far = ring(msg, "gx", 1), ring(msg, "gx", -1), ring(msg, "gx", 2)
    big = (NXE, Q0, 256)
    res_q, diag_q, inv_q, r0_up, r0_down = call(
        keep_fine,
        8,
        [(NX0, Q0, 256), big, big, (5 * Q0, 128), (5 * Q0, 128)],
        [],
        low, res0, diag0, inv0,
        micros=2.0,
    )
    r0_low, r0_high = ring(r0_up, "gx", 1), ring(r0_down, "gx", -1)
    mid = (16, R1, 128)
    res1, sol1, coef1, res2, coef2, up, down = call(
        middle_before,
        8,
        [mid, mid, mid, (8, 16, 128), (8, 16, 128), (96, 128), (96, 128)],
        [mid, mid, (18, R1, 128), (18, R1, 128), (16, 32, 128)],
        msg, low, far, high,
        micros=2.0,
    )
    below, above = ring(up, "gy", 1), ring(down, "gy", -1)
    own_up, own_down = call(pack_low_own, 4, [(48, 128)] * 2, [], res2, coef2, res1, sol1, micros=2.0)
    up, down = call(pack_low_halo, 4, [(R2 + Q1, 128)] * 2, [], own_up, own_down, above, below)
    left, right = ring(up, "gz", 1), ring(down, "gz", -1)
    bot, mid = (8, R2, 128), (16, Q1, 128)
    big = (NXE, Q0, 256)
    own = (NX0, NY0, NZ0)
    (sol2,) = call(
        bottom, 4, [bot], [bot] * 3 + [(10, R2, 128)] * 2, res2, coef2, below, above, left, right
    )
    (sol1,) = call(
        middle_after,
        8,
        [(20, Q1, 128)],
        [mid] * 3 + [(18, Q1, 128)] * 2,
        sol2, res1, sol1, coef1, below, above, left, right,
        micros=2.0,
    )
    return tuple(
        call(
            fine_after,
            16,
            [own, own],
            [(16, 2, 80, 128)] + [big] * 4,
            sol1, sol0, res_q, diag_q, inv_q, r0_low, r0_high,
        )
    )


def solution(mesh):
    return jax.shard_map(
        per_device,
        mesh=mesh,
        in_specs=(P("gx", "gy", "gz"), P("gx", "gy", "gz")),
        out_specs=(P("gx", "gy", "gz"), P("gx", "gy", "gz")),
        check_vma=False,
    )
```

```python
import jax
import jax.numpy as jnp
from jax import lax
from jax.experimental import pallas as pl
from jax.experimental.pallas import tpu as pltpu
from jax.sharding import PartitionSpec as P

SWEEPS = 3
COARSE_SWEEPS = 6
THETA = 1.25
DELTA = 0.75
F32 = jnp.float32

XH = 3
NX0, NY0, NZ0 = 8, 64, 128
NXE = NX0 + 2 * XH
W = 9
R0 = 88
Q0 = 72
R1 = 40
Q1 = 48
R2 = 32
MIB = 1024 * 1024


def coefficients(count):
    sigma = THETA / DELTA
    rho = 1.0 / sigma
    pairs = []
    for _ in range(count):
        rho_new = 1.0 / (2.0 * sigma - rho)
        pairs.append((rho_new * rho, 2.0 * rho_new / DELTA))
        rho = rho_new
    return pairs


def turn(value, shift, axis):
    return pltpu.roll(value, shift % value.shape[axis], axis)


def beside(value):
    return (turn(value, 1, 0) + turn(value, -1, 0)) + (turn(value, 1, 1) + turn(value, -1, 1))


def rows_of(shape):
    return lax.broadcasted_iota(jnp.int32, shape, 0)


def lanes_of(shape):
    return lax.broadcasted_iota(jnp.int32, shape, 1)


def inside_yz(shape, own_rows, split_row, own_lanes, split_lane):
    gy, gz = lax.axis_index("gy"), lax.axis_index("gz")
    last_y, last_z = lax.axis_size("gy") - 1, lax.axis_size("gz") - 1
    row, lane = rows_of(shape), lanes_of(shape)
    up_y, down_y = (gy < last_y).astype(jnp.int32), (gy > 0).astype(jnp.int32)
    up_z, down_z = (gz < last_z).astype(jnp.int32), (gz > 0).astype(jnp.int32)
    in_y = jnp.where(row < own_rows, 1, jnp.where(row < split_row, up_y, down_y))
    in_z = jnp.where(lane < own_lanes, 1, jnp.where(lane < split_lane, up_z, down_z))
    return (in_y * in_z) > 0


def pick(value, lane):
    return jnp.take_along_axis(value, lane, axis=1, mode="promise_in_bounds")


def pairs_of_lanes(value):
    lane = lanes_of(value.shape)
    return pick(value + turn(value, -1, 1), 2 * lane - jnp.where(lane < 64, 0, 128))


def call(body, limit, outs, scratch, *args, micros=1.0):
    vmem = pl.BlockSpec(memory_space=pltpu.VMEM)
    return pl.pallas_call(
        body,
        out_shape=[jax.ShapeDtypeStruct(s, F32) for s in outs],
        in_specs=[vmem] * len(args),
        out_specs=[vmem] * len(outs),
        scratch_shapes=[pltpu.VMEM(s, F32) for s in scratch],
        compiler_params=pltpu.CompilerParams(vmem_limit_bytes=limit * MIB),
        cost_estimate=pl.CostEstimate(flops=0, bytes_accessed=int(micros * 3690000), transcendentals=0),
    )(*args)


def ring(value, axis, shift):
    size = lax.axis_size(axis)
    return lax.ppermute(value, axis, [(i, (i + shift) % size) for i in range(size)])


OWN_SLABS = [(a, x) for a in range(2) for x in range(XH, XH + NX0)]
SIDE_SLABS = [(a, x) for a in range(2) for x in range(a, NXE - a) if (a, x) not in OWN_SLABS]
SLAB = {slab: (which, at) for which, slabs in enumerate((OWN_SLABS, SIDE_SLABS)) for at, slab in enumerate(slabs)}
EXTRA = (8 * len(OWN_SLABS), 8 * len(SIDE_SLABS))
YROWS = (EXTRA[0] + 16, EXTRA[1] + 16)


def plane_of(own, low, high, which, x):
    if x < XH:
        return low.at[x if which == 0 else XH + x - 1]
    if x < XH + NX0:
        return own[which].at[x - XH]
    return high.at[x - XH - NX0 + (0 if which == 0 else XH)]


def pack_x(s, c, up, down, work, done):
    copies = []

    def fetch(src, dst):
        copies.append(pltpu.make_async_copy(src, dst, done.at[len(copies)]))
        copies[-1].start()

    fetch(s.at[pl.ds(NX0 - XH, XH)], up.at[pl.ds(0, XH)])
    fetch(c.at[pl.ds(NX0 - XH, 1)], work.at[pl.ds(0, 1)])
    fetch(s.at[pl.ds(0, XH)], down.at[pl.ds(0, XH)])
    fetch(c.at[pl.ds(XH - 1, 1)], work.at[pl.ds(1, 1)])
    fetch(c.at[pl.ds(NX0 - XH + 1, XH - 1)], up.at[pl.ds(XH, XH - 1)])
    fetch(c.at[pl.ds(0, XH - 1)], down.at[pl.ds(XH, XH - 1)])
    for copy in copies:
        copy.wait()
    up[0] = up[0] * (1.0 / (work[0] + 6.0)) * (1.0 / THETA)
    down[XH - 1] = down[XH - 1] * (1.0 / (work[1] + 6.0)) * (1.0 / THETA)


def put_rows(src, slab, up, down):
    which, at = SLAB[slab]
    up[at * 8 : at * 8 + 8, :] = src[56:64, :]
    down[at * 8 : at * 8 + 8, :] = src[0:8, :]
    extra = EXTRA[which] + at
    up[extra : extra + 1, :] = src[55:56, :]
    down[extra : extra + 1, :] = src[8:9, :]


def fetch_own(after, s, c, s_out, c_out, up, down, done):
    copies = [pltpu.make_async_copy(s, s_out, done.at[0]), pltpu.make_async_copy(c, c_out, done.at[1])]
    for copy in copies:
        copy.start()
    for copy in copies:
        copy.wait()
    for a, x in OWN_SLABS:
        put_rows((s_out, c_out)[a].at[x - XH], (a, x), up, down)


def pack_y(high, low, up, down):
    for a, x in SIDE_SLABS:
        put_rows(plane_of(None, low, high, a, x), (a, x), up, down)
    used = EXTRA[1] + len(SIDE_SLABS)
    up[used:, :] = jnp.zeros((YROWS[1] - used, 128), F32)
    down[used:, :] = jnp.zeros((YROWS[1] - used, 128), F32)


def pack_wide(up, down, row, count, plane):
    lane = lanes_of((count, 128))
    for a in range(2):
        ups = jnp.zeros((count, 128), F32)
        downs = jnp.zeros((count, 128), F32)
        for x in range(a, NXE - a):
            v = plane(a, x)
            here = (lane >= W * x) & (lane < W * x + W)
            ups = jnp.where(here, turn(v, W * x - (128 - W), 1), ups)
            downs = jnp.where(here, turn(v, W * x, 1), downs)
        up[a, row : row + count, :] = ups
        down[a, row : row + count, :] = downs


def halo_rows(below, above, a, x):
    which, at = SLAB[a, x]
    below, above = below[which], above[which]
    extra = EXTRA[which] + at
    row = rows_of((8, 128))
    middle = jnp.where(row == 0, above[extra : extra + 1, :], 0.0)
    middle = jnp.where(row == 7, below[extra : extra + 1, :], middle)
    return jnp.concatenate([above[at * 8 : at * 8 + 8, :], middle, below[at * 8 : at * 8 + 8, :]], 0)


def pack_z_own(s, c, high, low, up, down):
    pack_wide(up, down, 0, 64, lambda a, x: plane_of((s, c), low, high, a, x)[...])


def pack_z_halo(own_up, own_down, below0, above0, below1, above1, up, down):
    up[:, 0:64, :] = own_up[...]
    down[:, 0:64, :] = own_down[...]
    pack_wide(up, down, 64, 24, lambda a, x: halo_rows((below0, below1), (above0, above1), a, x))


def fine_sweep(src, dst, res, diag, inverse, first, stop, pair, parts):
    for x in range(first, stop):
        d = src[x]
        near = beside(d) + (src[x - 1] + src[x + 1])
        for low, high in parts:
            part = d[low:high]
            r = res[x, low:high, :] - (diag[x, low:high, :] * part - near[low:high])
            res[x, low:high, :] = r
            if pair is not None:
                dst[x, low:high, :] = pair[0] * part + (pair[1] * inverse[x, low:high, :]) * r


def to_q0(ref, x):
    tail = jnp.where(rows_of((8, 256)) < 4, ref[x, 64:72, :], ref[x, 80:88, :])
    return ref[x, 0:64, :], tail


def fine_before(
    s, c, high, low, below0, above0, below1, above1, below, above, sol, res, diag, inv, msg, da, db, dc, rows
):
    lane = lanes_of((R0, 128))
    for a in range(2):
        left, right = below[a], above[a]
        for x in range(a, NXE - a):
            side = jnp.where(lane < W, turn(right, -W * x, 1), 0.0)
            side = jnp.where(lane >= 128 - W, turn(left, 128 - W - W * x, 1), side)
            ref = (res, diag)[a]
            ref[x, 0:64, 0:128] = plane_of((s, c), low, high, a, x)[...]
            ref[x, 64:88, 0:128] = halo_rows((below0, below1), (above0, above1), a, x)
            ref[x, :, 128:256] = side
    lane40 = lanes_of((R1, 128))

    def fold(ref, i, at):
        both = ref[XH + 2 * i] + ref[XH + 2 * i + 1]
        sides = []
        for side in range(2):
            part = both[:, 128 * side : 128 * side + 128]
            rows[at, side, 0:72, :] = part[0:72]
            rows[at, side, 72:80, :] = part[80:88]
            sides.append(rows.at[at, side][pl.ds(0, R1, stride=2), :] + rows.at[at, side][pl.ds(1, R1, stride=2), :])
        return 0.125 * jnp.where(lane40 < 64, pairs_of_lanes(sides[0]), pairs_of_lanes(sides[1]))

    coef1 = [fold(diag, i, i) for i in range(4)]

    gx = lax.axis_index("gx")
    in_yz = inside_yz((R0, 256), 64, 76, 128, 192)
    low_x, high_x = gx > 0, gx < lax.axis_size("gx") - 1

    for x in range(NXE):
        here = in_yz & (low_x if x < XH else high_x) if x < XH or x >= XH + NX0 else in_yz
        if x in (0, NXE - 1):
            da[x] = jnp.where(here, res[x], 0.0)
            continue
        g = diag[x] + 6.0
        diag[x] = g
        inverse = jnp.where(here, 1.0 / g, 0.0)
        inv[x] = inverse
        da[x] = res[x] * inverse * (1.0 / THETA)
    pairs = coefficients(SWEEPS)
    steps = (da, db, dc)
    for x in range(NXE):
        db[x, 72:80, :] = jnp.zeros((8, 256), F32)
        dc[x, 72:80, :] = jnp.zeros((8, 256), F32)
    for k in range(SWEEPS):
        last = k == SWEEPS - 1
        fine_sweep(
            steps[k], None if last else steps[k + 1], res, diag, inv, k + 1, NXE - 1 - k,
            None if last else pairs[k], ((0, 72), (80, 88)),
        )
    for x in range(NX0):
        sol[x] = sum(d[XH + x, 0:64, 0:128] for d in steps)

    halo = jnp.zeros((R1, 128), F32)
    for i in range(4):
        r1, c1 = fold(res, i, 4 + i), coef1[i]
        both = jnp.where(lane40 < 64, r1, turn(c1, 64, 1))
        msg[i * R1 : i * R1 + R1, :] = both
        for a, v in ((0, r1), (1, c1)):
            base = (a * 4 + i) * 8
            halo = jnp.where((lane40 >= base) & (lane40 < base + 4), turn(v, base - 64, 1), halo)
            halo = jnp.where((lane40 >= base + 4) & (lane40 < base + 8), turn(v, base + 4 - 124, 1), halo)
    msg[160:200, :] = halo


def line_sweep(src, dst, res, diag, inverse, planes, scale, pair, sol, ahead=0):
    def body(x, carry):
        d = src[x + 1]
        near = beside(d) + (src[x] + src[x + 2])
        if pair is None:
            own = slice(0, 32)
            res[x, own, :] = res[x, own, :] - (diag[x, own, :] * d[own] - scale * near[own])
            return carry
        r = res[x] - (diag[x] * d - scale * near)
        res[x] = r
        if pair is not None:
            step = pair[0] * d + (pair[1] * inverse[x]) * r
            dst[x + 1] = step
            sol[x + ahead] += step
        return carry

    lax.fori_loop(0, planes, body, 0, unroll=True)


def middle_before(own, low, far, high, res, sol, coef, low_res, low_coef, up, down, diag, inv, da, db, rows):
    gx = lax.axis_index("gx")
    size = lax.axis_size("gx")
    lane40 = lanes_of((R1, 128))
    for msg, shift in ((own, 0), (low, 3), (high, 1), (far, 2)):
        place = lax.rem(gx + shift, size) * 4
        side = msg[160:200, :]
        for i in range(4):
            both = msg[i * R1 : i * R1 + R1, :]
            for a, ref in ((0, res), (1, coef)):
                base = (a * 4 + i) * 8
                v = both if a == 0 else turn(both, 64, 1)
                v = jnp.where(lane40 < 64, v, turn(side, 64 - base, 1))
                v = jnp.where(lane40 < 68, v, 0.0)
                v = jnp.where(lane40 < 124, v, turn(side, 124 - base - 4, 1))
                ref[place + i] = v
    in_yz = inside_yz((R1, 128), 32, 36, 64, 96)
    empty = jnp.zeros((R1, 128), F32)
    for buffer in (da, db):
        buffer[0] = empty
        buffer[17] = empty

    def start(x, carry):
        g = coef[x] + 1.5
        diag[x] = g
        inverse = jnp.where(in_yz, 1.0 / g, 0.0)
        inv[x] = inverse
        d = res[x] * inverse * (1.0 / THETA)
        da[x + 1] = d
        sol[x] = d
        return carry

    lax.fori_loop(0, 16, start, 0, unroll=True)
    pairs = coefficients(SWEEPS)
    buffers = (da, db)
    for k in range(SWEEPS):
        src, dst = buffers[k % 2], buffers[(k + 1) % 2]
        line_sweep(src, dst, res, diag, inv, 16, 0.25, pairs[k] if k < SWEEPS - 1 else None, sol)
    lane8, row8 = lanes_of((8, 128)), rows_of((8, 128))

    def fold(ref, i, at):
        rows[at] = ref[2 * i, 0:32, :] + ref[2 * i + 1, 0:32, :]
        part = rows.at[at]
        return 0.125 * pairs_of_lanes(part[pl.ds(0, 16, stride=2), :] + part[pl.ds(1, 16, stride=2), :])

    lows = []
    for i in range(8):
        r2, c2 = fold(res, i, i), fold(coef, i, 8 + i)
        low_res[i] = r2
        low_coef[i] = c2
        lows.append(jnp.where(lanes_of((16, 128)) < 32, r2, turn(c2, 32, 1)))
    for i in range(4):
        both = jnp.where(lanes_of((16, 128)) < 64, lows[i], turn(lows[i + 4], 64, 1))
        up[i * 8 : i * 8 + 8, :] = both[8:16]
        down[i * 8 : i * 8 + 8, :] = both[0:8]
    for i in range(8):
        at = 32 + i * 8
        tiles = []
        for first in (24, 0):
            a, b = [
                jnp.where(lane8 < 64, res[x, first : first + 8, :], turn(sol[x, first : first + 8, :], 64, 1))
                for x in (2 * i, 2 * i + 1)
            ]
            tiles.append((a, b))
        up[at : at + 8, :] = jnp.where(row8 < 4, turn(tiles[0][0], 4, 0), tiles[0][1])
        down[at : at + 8, :] = jnp.where(row8 < 4, tiles[1][0], turn(tiles[1][1], 4, 0))


def low_halo(msg, i, which):
    tile = msg[(i % 4) * 8 : (i % 4) * 8 + 8, :]
    return turn(tile, -(64 * (i // 4) + 32 * which), 1)


def middle_halo(msg, x, which, below):
    tile = msg[32 + (x // 2) * 8 : 40 + (x // 2) * 8, :]
    tile = turn(tile, 64, 1) if which else tile
    return turn(tile, 4, 0) if (x % 2 == 0) == below else tile


def pack_lanes(up, down, row, count, planes, width, base, top):
    lane = lanes_of((count, 128))
    ups, downs = up[row : row + count, :], down[row : row + count, :]
    for i, v in enumerate(planes):
        at = base + width * i
        here = (lane >= at) & (lane < at + width)
        ups = jnp.where(here, turn(v, at - (top - width), 1), ups)
        downs = jnp.where(here, turn(v, at, 1), downs)
    up[row : row + count, :] = ups
    down[row : row + count, :] = downs


def pack_low_own(low_res, low_coef, res, sol, up, down):
    up[...] = jnp.zeros((48, 128), F32)
    down[...] = jnp.zeros((48, 128), F32)
    pack_lanes(up, down, 0, 16, [low_res[i] for i in range(8)], 8, 0, 32)
    pack_lanes(up, down, 0, 16, [low_coef[i] for i in range(8)], 8, 64, 32)
    pack_lanes(up, down, 16, 32, [res[x, 0:32, :] for x in range(16)], 4, 0, 64)
    pack_lanes(up, down, 16, 32, [sol[x, 0:32, :] for x in range(16)], 2, 64, 64)


def keep_fine(after, res0, diag0, inv0, res_q, diag_q, inv_q, r0_up, r0_down):
    for ref, kept, skip in ((res0, res_q, XH), (diag0, diag_q, 0), (inv0, inv_q, 0)):
        for x in range(NX0) if skip else range(1, NXE - 1):
            top, tail = to_q0(ref, x + skip)
            kept[x, 0:64, :] = top
            kept[x, 64:72, :] = tail
    lane = lanes_of((Q0, 128))
    for msg, first in ((r0_up, NX0 - XH), (r0_down, 0)):
        side = jnp.zeros((Q0, 128), F32)
        for i in range(XH):
            msg[i * Q0 : i * Q0 + Q0, :] = res_q[first + i, :, 0:128]
            v = res_q[first + i, :, 128:256]
            base = 6 * i
            side = jnp.where((lane >= base) & (lane < base + 3), turn(v, base, 1), side)
            side = jnp.where((lane >= base + 3) & (lane < base + 6), turn(v, base + 3 - 125, 1), side)
        far = 2 * XH + NX0 - 6 if first else 2 * XH - 1
        msg[4 * Q0 : 5 * Q0, :] = diag_q[far, :, 0:128]
        v = diag_q[far, :, 128:256]
        side = jnp.where((lane >= 18) & (lane < 21), turn(v, 18, 1), side)
        side = jnp.where((lane >= 21) & (lane < 24), turn(v, 21 - 125, 1), side)
        msg[XH * Q0 : XH * Q0 + Q0, :] = side


def pack_low_halo(own_up, own_down, above, below, up, down):
    for msg, own in ((up, own_up), (down, own_down)):
        msg[0:16, :] = own[0:16, :]
        msg[16:32, :] = jnp.zeros((16, 128), F32)
        msg[32:64, :] = own[16:48, :]
        msg[64:80, :] = jnp.zeros((16, 128), F32)
    for at, src, is_below in ((0, above, False), (8, below, True)):
        pack_lanes(up, down, 16 + at, 8, [low_halo(src, i, 0) for i in range(8)], 8, 0, 32)
        pack_lanes(up, down, 16 + at, 8, [low_halo(src, i, 1) for i in range(8)], 8, 64, 32)
        pack_lanes(up, down, 64 + at, 8, [middle_halo(src, x, 0, is_below) for x in range(16)], 4, 0, 64)
        pack_lanes(up, down, 64 + at, 8, [middle_halo(src, x, 1, is_below) for x in range(16)], 2, 64, 64)


def with_sides(own, left, right, base, width, own_lanes):
    lane = lanes_of(own.shape)
    v = jnp.where(lane < own_lanes, own, turn(right, own_lanes - base, 1))
    v = jnp.where(lane < own_lanes + width, v, 0.0)
    return jnp.where(lane < 128 - width, v, turn(left, 128 - width - base, 1))


def bottom(low_res, low_coef, below, above, left, right, sol2, res2, diag2, inv2, da2, db2):
    in_yz = inside_yz((R2, 128), 16, 24, 32, 64)
    empty = jnp.zeros((R2, 128), F32)
    for buffer in (da2, db2):
        buffer[0] = empty
        buffer[9] = empty
    from_left, from_right = left[0:R2, :], right[0:R2, :]
    for i in range(8):
        parts = []
        for a, ref in ((0, low_res), (1, low_coef)):
            own = jnp.concatenate([ref[i], low_halo(above, i, a), low_halo(below, i, a)], 0)
            parts.append(with_sides(own, from_left, from_right, a * 64 + i * 8, 8, 32))
        g = parts[1] + 0.375
        inverse = jnp.where(in_yz, 1.0 / g, 0.0)
        res2[i] = parts[0]
        diag2[i] = g
        inv2[i] = inverse
        d = parts[0] * inverse * (1.0 / THETA)
        da2[i + 1] = d
        sol2[i] = d
    pairs = coefficients(COARSE_SWEEPS)
    buffers = (da2, db2)
    for k in range(COARSE_SWEEPS - 1):
        src, dst = buffers[k % 2], buffers[(k + 1) % 2]
        line_sweep(src, dst, res2, diag2, inv2, 8, 0.0625, pairs[k], sol2)


def middle_after(
    sol2, res, sol, coef1, below, above, left, right, sol1, res1, diag1, inv1, da1, db1
):
    in_yz1 = inside_yz((Q1, 128), 32, 40, 64, 96)
    empty = jnp.zeros((Q1, 128), F32)
    for buffer in (da1, db1):
        buffer[0] = empty
        buffer[17] = empty
    for x in (0, 1, 18, 19):
        sol1[x] = empty
    from_left, from_right = left[R2 : R2 + Q1, :], right[R2 : R2 + Q1, :]
    lane = lanes_of((24, 128))
    half = lane // 2 + jnp.where(lane >= 96, 64, 0)
    first = rows_of((8, 128)) < 4
    for i in range(8):
        tail = jnp.where(first, sol2[i, 16:24, :], sol2[i, 24:32, :])
        lifted = pick(jnp.concatenate([sol2[i, 0:16, :], tail], 0), half)
        for x in (2 * i, 2 * i + 1):
            db1.at[x + 1][pl.ds(0, 24, stride=2), :] = lifted
            db1.at[x + 1][pl.ds(1, 24, stride=2), :] = lifted
            parts = []
            for a, ref in ((0, res), (1, sol)):
                own = jnp.concatenate(
                    [ref[x, 0:32, :], middle_halo(above, x, a, False), middle_halo(below, x, a, True)], 0
                )
                width = (4, 2)[a]
                parts.append(with_sides(own, from_left, from_right, a * 64 + width * x, width, 64))
            res1[x] = parts[0]
            sol1[x + 2] = jnp.where(in_yz1, parts[1], 0.0)

    def correct1(x, carry):
        g = jnp.concatenate([coef1[x], coef1[x, 32:40, :]], 0) + 1.5
        inverse = jnp.where(in_yz1, 1.0 / g, 0.0)
        diag1[x] = g
        inv1[x] = inverse
        p = db1[x + 1]
        near = beside(p) + (db1[x] + db1[x + 2])
        r = res1[x] - (g * p - 0.25 * near)
        res1[x] = r
        d = r * inverse * (1.0 / THETA)
        da1[x + 1] = d
        sol1[x + 2] += p + d
        return carry

    lax.fori_loop(0, 16, correct1, 0, unroll=True)
    pairs = coefficients(SWEEPS)
    buffers = (da1, db1)
    for k in range(SWEEPS - 1):
        src, dst = buffers[k % 2], buffers[(k + 1) % 2]
        line_sweep(src, dst, res1, diag1, inv1, 16, 0.25, pairs[k], sol1, 2)


def fine_after(
    sol1, sol0, res_q, diag_q, inv_q, low, high, out_sol, out_res, p0, res0, da0, db0, dc0
):
    gx = lax.axis_index("gx")
    half = lanes_of((R1, 128)) // 2
    first2 = rows_of((8, 128)) < 2
    for i in range(8):
        v = sol1[gx * 4 + i]
        v = jnp.concatenate([v[0:32], jnp.where(first2, v[32:40], turn(v[40:48], 4, 0))], 0)
        for side in range(2):
            lifted = pick(v, half + 64 * side)
            for x in (2 * i, 2 * i + 1):
                p0.at[x, side][pl.ds(0, R1, stride=2), :] = lifted
                p0.at[x, side][pl.ds(1, R1, stride=2), :] = lifted

    def lift(x):
        return jnp.concatenate([p0[x, 0, 0:Q0, :], p0[x, 1, 0:Q0, :]], 1)

    lane72 = lanes_of((Q0, 128))

    def with_lanes(main, side, base):
        v = jnp.where(lane72 < 3, turn(side, -base, 1), 0.0)
        v = jnp.where(lane72 < 125, v, turn(side, 125 - base - 3, 1))
        return jnp.concatenate([main, v], 1)

    outer = {}
    for msg, first, far in ((low, 0, 0), (high, XH + NX0, NXE - 1)):
        side = msg[XH * Q0 : XH * Q0 + Q0, :]
        for i in range(XH):
            outer[first + i] = with_lanes(msg[i * Q0 : i * Q0 + Q0, :], side, 6 * i)
        outer["diag", far] = with_lanes(msg[4 * Q0 : 5 * Q0, :], side, 18)
    in_yz = inside_yz((Q0, 256), 64, 68, 128, 192)
    low_x, high_x = gx > 0, gx < lax.axis_size("gx") - 1
    for x in range(NXE):
        p = lift(x + 1)
        near = beside(p) + (lift(x) + lift(x + 2))
        if x in (0, NXE - 1):
            g = outer["diag", x]
            inverse = jnp.where(in_yz & (low_x if x == 0 else high_x), 1.0 / g, 0.0)
        else:
            g, inverse = diag_q[x], inv_q[x]
        r = (outer[x] if x in outer else res_q[x - XH]) - (g * p - near)
        res0[x] = r
        da0[x] = r * inverse * (1.0 / THETA)
    pairs = coefficients(SWEEPS)
    steps = (da0, db0, dc0)
    for k in range(SWEEPS - 1):
        fine_sweep(steps[k], steps[k + 1], res0, diag_q, inv_q, k + 1, NXE - 1 - k, pairs[k], ((0, 72),))
    for x in range(NX0):
        at = x + XH
        d = dc0[at]
        near = beside(d)[0:64, 0:128] + (dc0[at - 1, 0:64, 0:128] + dc0[at + 1, 0:64, 0:128])
        d = d[0:64, 0:128]
        out_res[x] = res0[at, 0:64, 0:128] - (diag_q[at, 0:64, 0:128] * d - near)
        own = da0[at, 0:64, 0:128] + db0[at, 0:64, 0:128] + d
        out_sol[x] = sol0[x] + p0[at + 1, 0, 0:64, :] + own


def per_device(s, c):
    s, c = (pltpu.with_memory_space_constraint(v, pltpu.HBM) for v in (s, c))
    face = jax.ShapeDtypeStruct((2 * XH - 1, NY0, NZ0), F32)
    up, down = pl.pallas_call(
        pack_x,
        out_shape=[face] * 2,
        in_specs=[pl.BlockSpec(memory_space=pl.ANY)] * 2,
        out_specs=[pl.BlockSpec(memory_space=pltpu.VMEM)] * 2,
        scratch_shapes=[pltpu.VMEM((2, NY0, NZ0), F32), pltpu.SemaphoreType.DMA((6,))],
        compiler_params=pltpu.CompilerParams(vmem_limit_bytes=4 * MIB),
    )(s, c)
    s, c, own_up, own_down = pl.pallas_call(
        fetch_own,
        out_shape=[jax.ShapeDtypeStruct((NX0, NY0, NZ0), F32)] * 2 + [jax.ShapeDtypeStruct((YROWS[0], 128), F32)] * 2,
        in_specs=[pl.BlockSpec(memory_space=pl.ANY)] * 3,
        out_specs=[pl.BlockSpec(memory_space=pltpu.VMEM)] * 4,
        scratch_shapes=[pltpu.SemaphoreType.DMA((2,))],
        compiler_params=pltpu.CompilerParams(vmem_limit_bytes=4 * MIB),
        cost_estimate=pl.CostEstimate(flops=0, bytes_accessed=3690000, transcendentals=0),
    )(up, s, c)
    low, high = ring(up, "gx", 1), ring(down, "gx", -1)
    below0, above0 = ring(own_up, "gy", 1), ring(own_down, "gy", -1)
    up, down = call(pack_y, 4, [(YROWS[1], 128)] * 2, [], high, low)
    below1, above1 = ring(up, "gy", 1), ring(down, "gy", -1)
    own_up, own_down = call(pack_z_own, 4, [(2, 64, 128)] * 2, [], s, c, high, low)
    up, down = call(pack_z_halo, 4, [(2, R0, 128)] * 2, [], own_up, own_down, below0, above0, below1, above1)
    below, above = ring(up, "gz", 1), ring(down, "gz", -1)
    big = (NXE, R0, 256)
    sol0, res0, diag0, inv0, msg = call(
        fine_before,
        16,
        [(NX0, 64, 128), big, big, big, (200, 128)],
        [big, big, big, (8, 2, 80, 128)],
        s, c, high, low, below0, above0, below1, above1, below, above,
        micros=4.0,
    )
    low, high, far = ring(msg, "gx", 1), ring(msg, "gx", -1), ring(msg, "gx", 2)
    big = (NXE, Q0, 256)
    res_q, diag_q, inv_q, r0_up, r0_down = call(
        keep_fine,
        8,
        [(NX0, Q0, 256), big, big, (5 * Q0, 128), (5 * Q0, 128)],
        [],
        low, res0, diag0, inv0,
        micros=2.0,
    )
    r0_low, r0_high = ring(r0_up, "gx", 1), ring(r0_down, "gx", -1)
    mid = (16, R1, 128)
    res1, sol1, coef1, res2, coef2, up, down = call(
        middle_before,
        8,
        [mid, mid, mid, (8, 16, 128), (8, 16, 128), (96, 128), (96, 128)],
        [mid, mid, (18, R1, 128), (18, R1, 128), (16, 32, 128)],
        msg, low, far, high,
        micros=2.0,
    )
    below, above = ring(up, "gy", 1), ring(down, "gy", -1)
    own_up, own_down = call(pack_low_own, 4, [(48, 128)] * 2, [], res2, coef2, res1, sol1, micros=2.0)
    up, down = call(pack_low_halo, 4, [(R2 + Q1, 128)] * 2, [], own_up, own_down, above, below)
    left, right = ring(up, "gz", 1), ring(down, "gz", -1)
    bot, mid = (8, R2, 128), (16, Q1, 128)
    big = (NXE, Q0, 256)
    own = (NX0, NY0, NZ0)
    (sol2,) = call(
        bottom, 4, [bot], [bot] * 3 + [(10, R2, 128)] * 2, res2, coef2, below, above, left, right
    )
    (sol1,) = call(
        middle_after,
        8,
        [(20, Q1, 128)],
        [mid] * 3 + [(18, Q1, 128)] * 2,
        sol2, res1, sol1, coef1, below, above, left, right,
        micros=2.0,
    )
    return tuple(
        call(
            fine_after,
            16,
            [own, own],
            [(16, 2, 80, 128)] + [big] * 4,
            sol1, sol0, res_q, diag_q, inv_q, r0_low, r0_high,
        )
    )


def solution(mesh):
    return jax.shard_map(
        per_device,
        mesh=mesh,
        in_specs=(P("gx", "gy", "gz"), P("gx", "gy", "gz")),
        out_specs=(P("gx", "gy", "gz"), P("gx", "gy", "gz")),
        check_vma=False,
    )
```
